32 devices in a mesh: grp: 2 (over y), smp: 4 (over x, core), row: 4 (over z).
Axes of the slice: x: 2, y: 2, z: 4, core: 2. Of those that a mesh axis runs over, the one named last changes fastest.
Arguments:
- positions: float32 [8, 3, 4096], P(('grp', 'smp'), None, 'row'), parts along dimension 0, may hold values from -60 to 60
- noise_draw: float32 [8, 3, 4096], P(('grp', 'smp'), None, 'row'), parts along dimension 0, may hold values from -6 to 6
- noise_level: float32 [8], P(('grp', 'smp')), parts along dimension 0, may hold values from 0.5 to 80
- atom_single: bfloat16 [8192, 128], P(('grp', 'row')), parts along dimension 0, may hold values from -6 to 6
- token_single: bfloat16 [1024, 768], P(('grp', 'row')), parts along dimension 0, may hold values from -6 to 6
- pair_cond: bfloat16 [1024, 512, 128], P(('grp', 'row'), 'smp'), parts along dimension 0, may hold values from -6 to 6
- atom_to_token: int32 [8192], P(('grp', 'row')), parts along dimension 0, may hold values from 0 to 511, as said below
- window_offsets: int32 [256], P(('grp', 'row')), parts along dimension 0, may hold values from -96 to 0
- atom_mask: int32 [8192], P('grp'), parts along dimension 0, may hold values 0 or 1
- token_mask: int32 [1024], P('grp'), parts along dimension 0, may hold values 0 or 1
- coord_in: float32 [3, 128], replicated, may hold values from -3.5 to 3.5
- atom_gain: float32 [2, 128], replicated, may hold values from 0.1 to 1.9
- atom_qkv: bfloat16 [2, 128, 384], replicated, may hold values from -1 to 1
- atom_proj: bfloat16 [2, 128, 128], replicated, may hold values from -0.5 to 0.5
- gather_in: bfloat16 [128, 768], replicated, may hold values from -0.5 to 0.5
- noise_embed: float32 [768], replicated, may hold values from -6 to 6
- pair_gain: float32 [128], replicated, may hold values from 0.1 to 1.9
- pair_heads: bfloat16 [128, 16], replicated, may hold values from -0.5 to 0.5
- token_gain: float32 [2, 768], replicated, may hold values from 0.1 to 1.9
- token_qkv: bfloat16 [768, 2304], replicated, may hold values from -1 to 1
- token_proj: bfloat16 [768, 768], replicated, may hold values from -0.21875 to 0.21875
- ffn_in: bfloat16 [768, 3072], replicated, may hold values from -0.21875 to 0.21875
- ffn_out: bfloat16 [1536, 768], replicated, may hold values from -0.15625 to 0.15625
- scatter_out: bfloat16 [768, 128], replicated, may hold values from -0.21875 to 0.21875
- out_gain: float32 [128], replicated, may hold values from 0.1 to 1.9
- coord_out: bfloat16 [3, 128], replicated, may hold values from -0.5 to 0.5
Outputs:
- token_out: bfloat16 [8, 512, 768], P(('grp', 'smp'), 'row'), parts along dimension 0
- direction: float32 [8, 3, 4096], P(('grp', 'smp'), None, 'row'), parts along dimension 0
The draws below stay inside these ranges and needn't reach their ends.
There are 2 independent parts, one for each index of `grp`. The reference program is written for one: setup_inputs(seed, part) draws one part's arguments, and reference() takes and returns one part's arrays. A program takes and returns all parts, laid end to end along the dimension named above; an argument that names none is the same for every part. Nothing has to cross between parts.
Inputs may be any that keep to these rules, and one draw needn't show every extreme that they name: `atom_to_token`: never falls along the atoms; atoms k * 1024 to (k + 1) * 1024 - 1 belong to tokens k * 128 to (k + 1) * 128 - 1; some tokens have no atom.
All inputs are finite; a program needn't handle non-finite values.
Results may differ from the reference program's by a relative error of at most 0.013.
Values may be sent and summed in bfloat16 or wider, within the bound.
No kernel may reach another device: no remote copies, remote signals or barrier semaphores. Data moves between devices by JAX's collectives and lax.ppermute only.
A program may use at most 128 MiB of HBM per device.

```python
import math
import jax
import jax.numpy as jnp
from jax import lax

D = 768
HEADS = 16
FF = 1536
CP = 128
CA = 128
AHEADS = 4
TOKR = 128
WQ = 32
WK = 128
HALO = 96
ATOMR = 1024
TOK = 512
ATOMS = 4096
SAMPLES = 4


def draw_atom_to_token(key, part):
    block_total = ATOMS // ATOMR
    local_ids = jax.random.randint(jax.random.fold_in(key, 11), (block_total, ATOMR), 0, TOKR)
    empty_ids = jax.random.randint(jax.random.fold_in(key, 12), (block_total, 2), 0, TOKR - 1)
    for column in range(2):
        local_ids = jnp.where(local_ids == empty_ids[:, column:column + 1], local_ids + 1, local_ids)
    local_ids = jnp.minimum(local_ids, TOKR - 1)
    local_ids = jnp.sort(local_ids, axis=1)
    local_ids = local_ids.at[:, 0].set(0).at[:, ATOMR - 1].set(TOKR - 1)
    base_ids = jnp.arange(block_total, dtype=jnp.int32)[:, None] * TOKR
    return (local_ids + base_ids).reshape(ATOMS).astype(jnp.int32)


def draw_window_offsets(key, part):
    block_total = ATOMS // ATOMR
    per_device = ATOMR // WQ
    offsets = jax.random.randint(jax.random.fold_in(key, 21), (block_total, per_device), 0 - HALO, 1)
    offsets = offsets.at[:, 0].set(0 - HALO).at[:, per_device - 1].set(0)
    return offsets.reshape(block_total * per_device).astype(jnp.int32)


def single_features(key, count, width):
    values = jnp.clip(jax.random.normal(jax.random.fold_in(key, 1), (count, width), jnp.float32), -6.0, 6.0)
    return values.astype(jnp.bfloat16)


def draw_token_single(key, part):
    return single_features(key, TOK, D)


def draw_atom_single(key, part):
    return single_features(key, ATOMS, CA)


def weight_values(key, shape, fan_in):
    values = jax.random.truncated_normal(jax.random.fold_in(key, 6), -4.0, 4.0, shape, jnp.float32)
    return values / math.sqrt(fan_in)


def draw_token_qkv(key, part):
    matrix = weight_values(key, (D, 3 * D), D)
    return matrix.astype(jnp.bfloat16)


def draw_atom_qkv(key, part):
    matrix = weight_values(key, (2, CA, 3 * CA), CA)
    return matrix.astype(jnp.bfloat16)


def with_ends(values, own_key, low, high):
    longest = values.shape.index(max(values.shape))
    spots = []
    for shift in (0, 1):
        where = [jax.random.randint(jax.random.fold_in(own_key, axis), (), 0, length) for axis, length in enumerate(values.shape)]
        where[longest] = (where[longest] + shift) % values.shape[longest]
        spots.append(tuple(where))
    return values.at[spots[0]].set(low).at[spots[1]].set(high)


def block_levels(stream_key, dims, shards, smallest, high):
    level, own = 1.0, jax.random.fold_in(stream_key, 6)
    for position, parts in shards:
        draws = jnp.exp(jax.random.uniform(jax.random.fold_in(own, position), (parts,), jnp.float32, smallest / len(shards), high / len(shards)))
        level = level * jnp.repeat(draws, dims[position] // parts).reshape([-1 if axis == position else 1 for axis in range(len(dims))])
    return level


def gaussian(stream_key, extent, spread, bound, split=(), held_as=jnp.bfloat16):
    level = block_levels(stream_key, extent, split, -0.22, 0.18) if split else 1.0
    result = jax.random.normal(stream_key, extent, jnp.float32) * spread * level
    return jnp.minimum(jnp.maximum(result, -bound), bound).astype(held_as)


def setup_inputs(seed: int = 0, part: int = 0) -> dict:
    arg_keys = jax.random.split(jax.random.key(seed), 27)
    part_splits = jax.random.split(jax.random.fold_in(arg_keys[26], part), 27)
    positions = gaussian(part_splits[0], (SAMPLES, 3, ATOMS), 10.0, 60.0, ((0, 4), (2, 4)), jnp.float32)
    noise_draw = gaussian(part_splits[1], (SAMPLES, 3, ATOMS), 1.0, 6.0, ((0, 4), (2, 4)), jnp.float32)
    noise_level = jnp.clip(jnp.exp(math.log(80.0) - 5.075174 * jax.random.uniform(part_splits[2], (SAMPLES,), jnp.float32) ** block_levels(part_splits[2], (SAMPLES,), ((0, 4),), -0.2, 0.2)), 0.5, 80.0)
    atom_single = draw_atom_single(jax.random.fold_in(jax.random.fold_in(arg_keys[26], part), 71), part)
    token_single = draw_token_single(jax.random.fold_in(jax.random.fold_in(arg_keys[26], part), 71), part)
    pair_cond = gaussian(part_splits[5], (TOK, TOK, CP), 1.0, 6.0, ((0, 4), (1, 4)))
    atom_to_token = draw_atom_to_token(jax.random.fold_in(jax.random.fold_in(arg_keys[26], part), 71), part)
    window_offsets = draw_window_offsets(jax.random.fold_in(jax.random.fold_in(arg_keys[26], part), 71), part)
    atom_mask = with_ends((jax.random.randint(part_splits[8], (ATOMS,), 0, 8) < 7).astype(jnp.int32), jax.random.fold_in(part_splits[8], 1), 0, 1)
    token_mask = with_ends((jax.random.randint(part_splits[9], (TOK,), 0, 16) < 15).astype(jnp.int32), jax.random.fold_in(part_splits[9], 1), 0, 1)
    coord_in = gaussian(arg_keys[10], (3, CA), 3 ** -0.5, 3.5, (), jnp.float32)
    atom_gain = jnp.clip(1.0 + 0.18 * jax.random.normal(arg_keys[11], (2, CA), jnp.float32), 0.1, 1.9)
    atom_qkv = draw_atom_qkv(jax.random.fold_in(arg_keys[26], 71), part)
    atom_proj = gaussian(arg_keys[13], (2, CA, CA), CA ** -0.5, 0.5)
    gather_in = gaussian(arg_keys[14], (CA, D), CA ** -0.5, 0.5)
    noise_embed = gaussian(arg_keys[15], (D,), 1.0, 6.0, (), jnp.float32)
    pair_gain = jnp.clip(1.0 + 0.18 * jax.random.normal(arg_keys[16], (CP,), jnp.float32), 0.1, 1.9)
    pair_heads = gaussian(arg_keys[17], (CP, HEADS), CP ** -0.5, 0.5)
    token_gain = jnp.clip(1.0 + 0.18 * jax.random.normal(arg_keys[18], (2, D), jnp.float32), 0.1, 1.9)
    token_qkv = draw_token_qkv(jax.random.fold_in(arg_keys[26], 71), part)
    token_proj = gaussian(arg_keys[20], (D, D), D ** -0.5, 0.21875)
    ffn_in = gaussian(arg_keys[21], (D, 2 * FF), D ** -0.5, 0.21875)
    ffn_out = gaussian(arg_keys[22], (FF, D), FF ** -0.5, 0.15625)
    scatter_out = gaussian(arg_keys[23], (D, CA), D ** -0.5, 0.21875)
    out_gain = jnp.clip(1.0 + 0.18 * jax.random.normal(arg_keys[24], (CA,), jnp.float32), 0.1, 1.9)
    coord_out = gaussian(arg_keys[25], (3, CA), CA ** -0.5, 0.5)
    return dict(positions=positions, noise_draw=noise_draw, noise_level=noise_level, atom_single=atom_single, token_single=token_single, pair_cond=pair_cond, atom_to_token=atom_to_token, window_offsets=window_offsets, atom_mask=atom_mask, token_mask=token_mask, coord_in=coord_in, atom_gain=atom_gain, atom_qkv=atom_qkv, atom_proj=atom_proj, gather_in=gather_in, noise_embed=noise_embed, pair_gain=pair_gain, pair_heads=pair_heads, token_gain=token_gain, token_qkv=token_qkv, token_proj=token_proj, ffn_in=ffn_in, ffn_out=ffn_out, scatter_out=scatter_out, out_gain=out_gain, coord_out=coord_out)


sigma_data = 16.0
gamma_boost = 0.8
norm_eps = 1e-05
masked_score = -1e+30

def layer_norm(values, norm_gain):
    average = lax.optimization_barrier(jnp.mean(values, axis=-1, keepdims=True))
    centred = values - average
    variance = lax.optimization_barrier(jnp.mean(centred * centred, axis=-1, keepdims=True))
    return centred * lax.rsqrt(variance + norm_eps) * norm_gain

def softmax_rows(scores):
    largest = lax.optimization_barrier(jnp.max(scores, axis=-1, keepdims=True))
    exponent = jnp.exp(scores - largest)
    return exponent / lax.optimization_barrier(jnp.sum(exponent, axis=-1, keepdims=True))

def pair_bias_of(pair_tile, pair_gain, pair_heads):
    normed = layer_norm(pair_tile.astype(jnp.float32), pair_gain).astype(jnp.bfloat16)
    normed = lax.optimization_barrier(normed)
    return jnp.einsum('ijc,ch->hij', normed.astype(jnp.float32), pair_heads.astype(jnp.float32)).astype(jnp.bfloat16)

def window_attend(queries, windows, live, w_out):
    block_count = queries.shape[0] // WQ
    head_size = CA // AHEADS
    query_heads = queries.reshape(block_count, WQ, AHEADS, head_size).astype(jnp.float32)
    key_heads = windows[:, :, :CA].reshape(block_count, WK, AHEADS, head_size).astype(jnp.float32)
    value_heads = windows[:, :, CA:].reshape(block_count, WK, AHEADS, head_size).astype(jnp.float32)
    scores = jnp.einsum('bqhd,bkhd->bhqk', query_heads, key_heads) / jnp.sqrt(jnp.float32(head_size))
    scores = jnp.where(live[:, None, None, :], scores, masked_score)
    weights = lax.optimization_barrier(softmax_rows(scores).astype(jnp.bfloat16)).astype(jnp.float32)
    mixed_heads = jnp.einsum('bhqk,bkhd->bqhd', weights, value_heads).astype(jnp.bfloat16)
    return jnp.dot(mixed_heads.reshape(block_count * WQ, CA), w_out, preferred_element_type=jnp.float32)

def atom_block(atom_state, norm_gain, w_qkv, w_out, offsets, valid):
    atom_count = atom_state.shape[0]
    block_count = atom_count // WQ
    normed = layer_norm(atom_state, norm_gain).astype(jnp.bfloat16)
    projected = jnp.dot(normed, w_qkv, preferred_element_type=jnp.float32).astype(jnp.bfloat16)
    padded = jnp.pad(projected[:, CA:], ((HALO, HALO), (0, 0)))
    live_padded = jnp.pad(valid, (HALO, HALO))
    starts = jnp.arange(block_count, dtype=jnp.int32) * WQ + offsets + HALO
    window_index = starts[:, None] + jnp.arange(WK, dtype=jnp.int32)[None, :]
    return atom_state + window_attend(projected[:, :CA], padded[window_index], live_padded[window_index] > 0, w_out)

def reference(positions, noise_draw, noise_level, atom_single, token_single, pair_cond, atom_to_token, window_offsets, atom_mask, token_mask, coord_in, atom_gain, atom_qkv, atom_proj, gather_in, noise_embed, pair_gain, pair_heads, token_gain, token_qkv, token_proj, ffn_in, ffn_out, scatter_out, out_gain, coord_out):
    biases = pair_bias_of(pair_cond, pair_gain, pair_heads).astype(jnp.float32)
    token_ids = jnp.arange(TOK, dtype=jnp.int32)
    member = (atom_to_token[None, :] == token_ids[:, None]) & (atom_mask[None, :] > 0)
    onehot = member.astype(jnp.bfloat16)
    counts = jnp.maximum(lax.optimization_barrier(jnp.sum(member.astype(jnp.float32), axis=1)), 1.0)
    key_live = token_mask > 0
    head_size = D // HEADS

    def one_sample(sample_inputs):
        coords, kicks, level_now = sample_inputs
        level_hat = (1.0 + gamma_boost) * level_now
        noisy = coords + jnp.sqrt(level_hat * level_hat - level_now * level_now) * kicks
        scaled = noisy / jnp.sqrt(level_hat * level_hat + sigma_data * sigma_data)
        atom_state = atom_single.astype(jnp.float32) + jnp.einsum('ka,kc->ac', scaled, coord_in, precision=lax.Precision.HIGHEST)
        atom_state = atom_block(atom_state, atom_gain[0], atom_qkv[0], atom_proj[0], window_offsets, atom_mask)
        lifted = jax.nn.relu(jnp.dot(atom_state.astype(jnp.bfloat16), gather_in, preferred_element_type=jnp.float32)).astype(jnp.bfloat16)
        pooled = jnp.dot(onehot, lifted, preferred_element_type=jnp.float32) / counts[:, None]
        token_state = pooled + token_single.astype(jnp.float32) + jnp.log(level_hat / sigma_data) / 4.0 * noise_embed
        normed = layer_norm(token_state, token_gain[0]).astype(jnp.bfloat16)
        projected = jnp.dot(normed, token_qkv, preferred_element_type=jnp.float32).astype(jnp.bfloat16)
        query_heads = projected[:, :D].reshape(TOK, HEADS, head_size).astype(jnp.float32)
        key_heads = projected[:, D:2 * D].reshape(TOK, HEADS, head_size).astype(jnp.float32)
        value_heads = projected[:, 2 * D:].reshape(TOK, HEADS, head_size).astype(jnp.float32)
        scores = jnp.einsum('ihd,jhd->hij', query_heads, key_heads) / jnp.sqrt(jnp.float32(head_size)) + biases
        scores = jnp.where(key_live[None, None, :], scores, masked_score)
        weights = lax.optimization_barrier(softmax_rows(scores).astype(jnp.bfloat16)).astype(jnp.float32)
        mixed_heads = jnp.einsum('hij,jhd->ihd', weights, value_heads).astype(jnp.bfloat16).reshape(TOK, D)
        token_state = token_state + jnp.dot(mixed_heads, token_proj, preferred_element_type=jnp.float32)
        normed = layer_norm(token_state, token_gain[1]).astype(jnp.bfloat16)
        hidden = jnp.dot(normed, ffn_in, preferred_element_type=jnp.float32)
        active = (jax.nn.silu(hidden[:, :FF]) * hidden[:, FF:]).astype(jnp.bfloat16)
        token_state = token_state + jnp.dot(active, ffn_out, preferred_element_type=jnp.float32)
        token_result = token_state.astype(jnp.bfloat16)
        spread_back = jnp.dot(token_result, scatter_out, preferred_element_type=jnp.float32).astype(jnp.bfloat16)
        atom_state = atom_state + lax.dot_general(onehot, spread_back, (((0,), (0,)), ((), ())), preferred_element_type=jnp.float32)
        atom_state = atom_block(atom_state, atom_gain[1], atom_qkv[1], atom_proj[1], window_offsets, atom_mask)
        normed_out = layer_norm(atom_state, out_gain).astype(jnp.bfloat16)
        update = lax.dot_general(coord_out, normed_out, (((1,), (1,)), ((), ())), preferred_element_type=jnp.float32)
        base_square = sigma_data * sigma_data + level_hat * level_hat
        skip_scale = sigma_data * sigma_data / base_square
        out_scale = level_hat * sigma_data / jnp.sqrt(base_square)
        denoised = skip_scale * noisy + out_scale * update
        return (token_result, (noisy - denoised) / level_hat)
    token_out, direction = lax.map(one_sample, (positions, noise_draw, noise_level))
    return (token_out, direction)
```

```python
import functools
import math

import jax
import jax.numpy as jnp
from jax import lax
from jax.experimental import pallas as pl
from jax.experimental.pallas import tpu as pltpu
from jax.sharding import PartitionSpec as P

HEADS = 16
AHEADS = 4
WQ = 32
WK = 128
HALO = 96
LANES = 128

sigma_data = 16.0
gamma_boost = 0.8
norm_eps = 1e-05
masked_score = -1e30
LOG2E = math.log2(math.e)
F32 = jnp.float32
BF16 = jnp.bfloat16
NT = (((1,), (1,)), ((), ()))
TN = (((0,), (0,)), ((), ()))


def vmem(mib):
    return pltpu.CompilerParams(vmem_limit_bytes=mib * 1024 * 1024)


def whole(count):
    return [pl.BlockSpec(memory_space=pltpu.VMEM)] * count


def dot(a, b, dims=(((1,), (0,)), ((), ()))):
    return lax.dot_general(a, b, dims, preferred_element_type=F32)


def norm_rows(values, gain):
    average = jnp.mean(values, axis=-1, keepdims=True)
    centred = values - average
    variance = jnp.mean(centred * centred, axis=-1, keepdims=True)
    return centred * lax.rsqrt(variance + norm_eps) * gain


def noisy_of(level, coords, kicks):
    level_hat = (1.0 + gamma_boost) * level
    noisy = coords + jnp.sqrt(level_hat * level_hat - level * level) * kicks
    return level_hat, noisy


def column_of(row):
    size = row.shape[1]
    down = lax.broadcasted_iota(jnp.int32, (size, size), 0)
    across = lax.broadcasted_iota(jnp.int32, (size, size), 1)
    spread = jnp.where(down == across, jnp.broadcast_to(row, (size, size)), 0.0)
    return dot(spread.astype(BF16), jnp.ones((size, LANES), BF16))


def prepare_kernel(level_ref, coords_ref, kicks_ref, single_ref, coord_in_ref, gain_ref, state_ref, normed_ref):
    level_hat, noisy = noisy_of(level_ref[...], coords_ref[0], kicks_ref[0])
    scaled = noisy / jnp.sqrt(level_hat * level_hat + sigma_data * sigma_data)
    embedded = lax.dot_general(
        scaled, coord_in_ref[...], TN, precision=lax.Precision.HIGHEST, preferred_element_type=F32
    )
    state = single_ref[...].astype(F32) + embedded
    state_ref[...] = state
    normed_ref[...] = norm_rows(state, gain_ref[0:1]).astype(BF16)


def pair_kernel(tile_ref, gain_ref, heads_ref, bias_ref):
    rows, keys, channels = tile_ref.shape
    head_count = heads_ref.shape[0]
    weights = heads_ref[...].astype(F32) * gain_ref[...]
    high = weights.astype(BF16)
    low = (weights - high.astype(F32)).astype(BF16)
    total = jnp.sum(high.astype(F32) + low.astype(F32), axis=1, keepdims=True)
    ones = jnp.ones((head_count, channels), BF16)
    left = jnp.concatenate([high, low, ones], axis=0)
    tile = tile_ref[...].reshape(rows * keys, channels)
    wide = tile.astype(F32)
    square = wide * wide
    square_high = square.astype(BF16)
    square_low = (square - square_high.astype(F32)).astype(BF16)
    sums = dot(left, tile, NT)
    squares = dot(ones, square_high, NT) + dot(ones, square_low, NT)
    average = sums[2 * head_count :] / channels
    variance = jnp.maximum(squares / channels - average * average, 0.0)
    raw = sums[:head_count] + sums[head_count : 2 * head_count]
    result = (raw - average * total) * lax.rsqrt(variance + norm_eps)
    pieces = [result[:, i * keys : (i + 1) * keys] for i in range(rows)]
    stacked = jnp.stack(pieces, axis=1)
    bias_ref[...] = stacked.astype(BF16)


def window_block(
    first, last, state, low_ref, mid_ref, high_ref, gain_unused, w_qkv, w_out, offsets_ref, mask_ref, first_chunk, scratch
):
    key_scr, value_scr, live_scr, score_scr, prob_scr, out_scr = scratch
    row_count = state.shape[0]
    width = state.shape[1]
    block_count = row_count // WQ
    head_size = width // AHEADS
    low = jnp.where(first, jnp.zeros_like(low_ref[...]), low_ref[...])
    high = jnp.where(last, jnp.zeros_like(high_ref[...]), high_ref[...])
    mid = mid_ref[...]
    w_kv = w_qkv[:, width:]
    for start, part in ((0, low), (HALO, mid), (HALO + row_count, high)):
        projected = dot(part, w_kv).astype(BF16).astype(F32)
        key_scr[start : start + part.shape[0], :] = projected[:, :width]
        value_scr[start : start + part.shape[0], :] = projected[:, width:]
    queries = dot(mid, w_qkv[:, :width]).astype(BF16)

    chunk_count = row_count // LANES
    outside = -1e30
    edge = column_of(mask_ref[pl.ds(jnp.maximum(first_chunk - 1, 0), 1), :].astype(F32))
    edge = jnp.where(first, 0.0, edge)
    live_scr[0:HALO, :] = (edge[LANES - HALO :] - 1.0) * -outside
    for chunk in range(chunk_count):
        column = column_of(mask_ref[pl.ds(first_chunk + chunk, 1), :].astype(F32))
        begin = HALO + chunk * LANES
        live_scr[begin : begin + LANES, :] = (column - 1.0) * -outside
    final = mask_ref.shape[0] - 1
    edge = column_of(mask_ref[pl.ds(jnp.minimum(first_chunk + chunk_count, final), 1), :].astype(F32))
    edge = jnp.where(last, 0.0, edge)
    live_scr[HALO + row_count :, :] = (edge[:HALO] - 1.0) * -outside

    stacked_rows = AHEADS * WQ
    lane = lax.broadcasted_iota(jnp.int32, (stacked_rows, width), 1)
    line = lax.broadcasted_iota(jnp.int32, (stacked_rows, width), 0)
    own_head = lane // head_size == line // WQ
    pick = jnp.where(lane == 0, 1.0, 0.0).astype(BF16)
    ones = jnp.ones((WK, width), BF16)
    begins = []
    for b in range(block_count):
        begin = b * WQ + HALO + offsets_ref[b]
        begins.append(begin)
        keys = key_scr[pl.ds(begin, WK), :].astype(BF16)
        live = live_scr[pl.ds(begin, WK), :].astype(BF16)
        query = queries[b * WQ : (b + 1) * WQ]
        query = jnp.concatenate([query] * AHEADS, axis=0)
        query = jnp.where(own_head, query, jnp.zeros_like(query))
        score_scr[b * stacked_rows : (b + 1) * stacked_rows, :] = dot(
            jnp.concatenate([query, pick], axis=1), jnp.concatenate([keys, live], axis=1), NT
        )
    factor = LOG2E / math.sqrt(head_size)
    step = 4 * stacked_rows
    for begin in range(0, block_count * stacked_rows, step):
        scores = score_scr[begin : begin + step, :]
        largest = jnp.max(scores, axis=-1, keepdims=True)
        prob_scr[begin : begin + step, :] = jnp.exp2((scores - largest) * factor).astype(BF16)
    for b in range(block_count):
        values = value_scr[pl.ds(begins[b], WK), :].astype(BF16)
        probs = prob_scr[b * stacked_rows : (b + 1) * stacked_rows, :]
        both = dot(probs, jnp.concatenate([values, ones], axis=1))
        mixed = jnp.where(own_head, both[:, :width], 0.0)
        weight = jnp.where(own_head, both[:, width:], 0.0)
        mixed = sum(mixed[h * WQ : (h + 1) * WQ] for h in range(AHEADS))
        weight = sum(weight[h * WQ : (h + 1) * WQ] for h in range(AHEADS))
        out_scr[b * WQ : (b + 1) * WQ, :] = (mixed / weight).astype(BF16)
    return state + dot(out_scr[...], w_out)


def window_scratch(row_count, width):
    extended = row_count + 2 * HALO
    scores = row_count * AHEADS
    return [
        pltpu.VMEM((extended, width), F32),
        pltpu.VMEM((extended, width), F32),
        pltpu.VMEM((extended, LANES), F32),
        pltpu.VMEM((scores, WK), F32),
        pltpu.VMEM((scores, WK), BF16),
        pltpu.VMEM((row_count, width), BF16),
    ]


def member_of(token_ref, mask_ref, first_chunk, base, tok_rows):
    chunk_count = token_ref.shape[0]
    tokens = lax.broadcasted_iota(jnp.int32, (tok_rows, LANES), 0)
    pieces = []
    for chunk in range(chunk_count):
        local = token_ref[chunk : chunk + 1, :] - base
        valid = mask_ref[pl.ds(first_chunk + chunk, 1), :]
        local = jnp.where(valid > 0, local, -1)
        pieces.append(jnp.where(local == tokens, 1.0, 0.0).astype(BF16))
    return jnp.concatenate(pieces, axis=1)


def encoder_kernel(
    place_ref, offsets_ref, level_ref, state_ref, low_ref, mid_ref, high_ref, mask_ref, token_ref, w_qkv_ref, w_out_ref,
    lift_ref, single_ref, embed_ref, gain_ref, encoded_ref, token_state_ref, normed_ref, *scratch
):
    row, count = place_ref[0], place_ref[1]
    tok_rows = single_ref.shape[0]
    chunk_count = token_ref.shape[0]
    first_chunk = row * chunk_count
    state = window_block(
        row == 0, row == count - 1, state_ref[...], low_ref, mid_ref, high_ref, None,
        w_qkv_ref[0], w_out_ref[0], offsets_ref, mask_ref, first_chunk, scratch,
    )
    encoded_ref[...] = state
    lifted = jnp.maximum(dot(state.astype(BF16), lift_ref[...]), 0.0).astype(BF16)
    member = member_of(token_ref, mask_ref, first_chunk, row * tok_rows, tok_rows)
    counts = jnp.maximum(dot(member, jnp.ones((member.shape[1], LANES), BF16)), 1.0)
    pooled = dot(member, lifted) / counts[:, 0:1]
    level_hat = (1.0 + gamma_boost) * level_ref[...]
    token_state = (
        pooled + single_ref[...].astype(F32) + jnp.log(level_hat / sigma_data) / 4.0 * embed_ref[...]
    )
    token_state_ref[...] = token_state
    normed_ref[...] = norm_rows(token_state, gain_ref[0:1]).astype(BF16)


def token_kernel(row_count, smp_count, *refs):
    place_ref = refs[0]
    normed_refs = refs[1 : 1 + row_count]
    bias_refs = refs[1 + row_count : 1 + row_count + smp_count]
    (
        state_ref, key_mask_ref, w_qkv_ref, w_proj_ref, gain_ref, ffn_in_ref, ffn_out_ref, spread_ref,
        encoded_ref, mask_ref, token_ref, atom_gain_ref, out_ref, joined_ref, atom_normed_ref, kv_scr, score_scr, mixed_scr,
    ) = refs[1 + row_count + smp_count :]
    row, smp = place_ref[0], place_ref[2]
    tok_rows, width = state_ref.shape
    head_size = width // HEADS
    piece = bias_refs[0].shape[2]
    for d in range(row_count):
        begin = pl.multiple_of((row ^ d) * tok_rows, tok_rows)
        kv_scr[pl.ds(begin, tok_rows), :] = dot(normed_refs[d][...], w_qkv_ref[:, width:]).astype(BF16)
    queries = dot(normed_refs[0][...], w_qkv_ref[:, :width]).astype(BF16)
    scale = 1.0 / math.sqrt(head_size)
    spans = []
    for h in range(HEADS):
        begin = h * head_size // LANES * LANES
        end = -(-(h + 1) * head_size // LANES) * LANES
        spans.append((begin, end))
    order = []
    for d in range(smp_count):
        other = smp ^ d
        order.append(pl.multiple_of(other * piece, piece))
        live = key_mask_ref[pl.ds(other, 1), :] > 0
        for h in range(HEADS):
            begin, end = spans[h]
            lane = lax.broadcasted_iota(jnp.int32, (tok_rows, end - begin), 1) + begin
            query = queries[:, begin:end]
            query = jnp.where((lane >= h * head_size) & (lane < (h + 1) * head_size), query, jnp.zeros_like(query))
            keys = kv_scr[pl.ds(order[d], piece), begin:end]
            scores = dot(query, keys, NT) * scale + bias_refs[d][h].astype(F32)
            score_scr[d, h] = jnp.where(live, scores, masked_score)
    mixed_scr[...] = jnp.zeros_like(mixed_scr)
    for h in range(HEADS):
        begin, end = spans[h]
        scores = [score_scr[d, h] for d in range(smp_count)]
        largest = jnp.max(functools.reduce(jnp.maximum, scores), axis=-1, keepdims=True)
        exponents = [jnp.exp2((part - largest) * LOG2E) for part in scores]
        total = jnp.sum(functools.reduce(jnp.add, exponents), axis=-1, keepdims=True)
        mixed = functools.reduce(
            jnp.add,
            [
                dot(exponents[d].astype(BF16), kv_scr[pl.ds(order[d], piece), width + begin : width + end])
                for d in range(smp_count)
            ],
        )
        lane = lax.broadcasted_iota(jnp.int32, (tok_rows, end - begin), 1) + begin
        inside = (lane >= h * head_size) & (lane < (h + 1) * head_size)
        mixed_scr[:, begin:end] += jnp.where(inside, mixed / total, 0.0)
    state = state_ref[...] + dot(mixed_scr[...].astype(BF16), w_proj_ref[...])
    normed = norm_rows(state, gain_ref[1:2]).astype(BF16)
    hidden = dot(normed, ffn_in_ref[...])
    half = hidden.shape[1] // 2
    gate, up = hidden[:, :half], hidden[:, half:]
    active = (gate / (1.0 + jnp.exp(-gate)) * up).astype(BF16)
    state = state + dot(active, ffn_out_ref[...])
    result = state.astype(BF16)
    out_ref[0] = result
    spread = dot(result, spread_ref[...]).astype(BF16)
    chunk_count = token_ref.shape[0]
    member = member_of(token_ref, mask_ref, row * chunk_count, row * tok_rows, tok_rows)
    joined = encoded_ref[...] + dot(member, spread, TN)
    joined_ref[...] = joined
    atom_normed_ref[...] = norm_rows(joined, atom_gain_ref[1:2]).astype(BF16)


def decoder_kernel(
    place_ref, offsets_ref, level_ref, coords_ref, kicks_ref, state_ref, low_ref, mid_ref, high_ref, mask_ref,
    w_qkv_ref, w_out_ref, gain_ref, coord_out_ref, direction_ref, *scratch
):
    row, count = place_ref[0], place_ref[1]
    chunk_count = state_ref.shape[0] // LANES
    state = window_block(
        row == 0, row == count - 1, state_ref[...], low_ref, mid_ref, high_ref, None,
        w_qkv_ref[1], w_out_ref[1], offsets_ref, mask_ref, row * chunk_count, scratch,
    )
    normed = norm_rows(state, gain_ref[...]).astype(BF16)
    update = dot(coord_out_ref[...], normed, NT)
    level_hat, noisy = noisy_of(level_ref[...], coords_ref[0], kicks_ref[0])
    base_square = sigma_data * sigma_data + level_hat * level_hat
    skip_scale = sigma_data * sigma_data / base_square
    out_scale = level_hat * sigma_data / jnp.sqrt(base_square)
    denoised = skip_scale * noisy + out_scale * update
    direction_ref[0] = (noisy - denoised) / level_hat


def halos_of(normed):
    count = lax.axis_size("row")
    up = [(i, (i + 1) % count) for i in range(count)]
    down = [((i + 1) % count, i) for i in range(count)]
    low = lax.ppermute(normed[normed.shape[0] - HALO :], "row", up)
    high = lax.ppermute(normed[:HALO], "row", down)
    return low, high


def spread_over(block, axis):
    count = lax.axis_size(axis)
    found = [block]
    bits = []
    bit = count // 2
    have = {0: block}
    while bit:
        pairs = [(i, i ^ bit) for i in range(count)]
        for d in list(have):
            have[d | bit] = lax.ppermute(have[d], axis, pairs)
        bit //= 2
    return [have[d] for d in range(count)]


def per_device(
    positions,
    noise_draw,
    noise_level,
    atom_single,
    token_single,
    pair_cond,
    atom_to_token,
    window_offsets,
    atom_mask,
    token_mask,
    coord_in,
    atom_gain,
    atom_qkv,
    atom_proj,
    gather_in,
    noise_embed,
    pair_gain,
    pair_heads,
    token_gain,
    token_qkv,
    token_proj,
    ffn_in,
    ffn_out,
    scatter_out,
    out_gain,
    coord_out,
):
    row_count, smp_count = lax.axis_size("row"), lax.axis_size("smp")
    atoms, width = atom_single.shape
    tok_rows, token_width = token_single.shape
    heads = pair_heads.shape[1]
    keys = pair_cond.shape[1]
    place = jnp.stack(
        [lax.axis_index("row"), jnp.int32(row_count), lax.axis_index("smp")]
    ).astype(jnp.int32)
    level = noise_level.reshape(1, 1)
    mask = atom_mask.reshape(-1, LANES)
    tokens = atom_to_token.reshape(-1, LANES)
    smem = pl.BlockSpec(memory_space=pltpu.SMEM)
    shape = jax.ShapeDtypeStruct

    state, normed = pl.pallas_call(
        prepare_kernel,
        out_shape=(shape((atoms, width), F32), shape((atoms, width), BF16)),
        in_specs=whole(6),
        out_specs=tuple(whole(2)),
        compiler_params=vmem(32),
    )(level, positions, noise_draw, atom_single, coord_in, atom_gain)
    low, high = halos_of(normed)

    pair_rows = 16
    bias = pl.pallas_call(
        pair_kernel,
        grid=(pair_cond.shape[0] // pair_rows,),
        out_shape=shape((heads, pair_cond.shape[0], keys), BF16),
        in_specs=[
            pl.BlockSpec((pair_rows, keys, pair_cond.shape[2]), lambda i: (i, 0, 0)),
            pl.BlockSpec((1, pair_cond.shape[2]), lambda i: (0, 0)),
            pl.BlockSpec((heads, pair_cond.shape[2]), lambda i: (0, 0)),
        ],
        out_specs=pl.BlockSpec((heads, pair_rows, keys), lambda i: (0, i, 0)),
        compiler_params=vmem(32),
    )(pair_cond, pair_gain.reshape(1, -1), pair_heads.T)
    biases = spread_over(bias, "smp")

    encoded, token_state, token_normed = pl.pallas_call(
        encoder_kernel,
        out_shape=(
            shape((atoms, width), F32),
            shape((tok_rows, token_width), F32),
            shape((tok_rows, token_width), BF16),
        ),
        in_specs=[smem, smem] + whole(13),
        out_specs=tuple(whole(3)),
        scratch_shapes=window_scratch(atoms, width),
        compiler_params=vmem(40),
    )(
        place, window_offsets, level, state, low, normed, high, mask, tokens, atom_qkv, atom_proj, gather_in,
        token_single, noise_embed.reshape(1, -1), token_gain,
    )
    gathered = spread_over(token_normed, "row")

    key_mask = token_mask.reshape(-1, keys)
    token_result, joined, atom_normed = pl.pallas_call(
        functools.partial(token_kernel, row_count, smp_count),
        out_shape=(
            shape((1, tok_rows, token_width), BF16),
            shape((atoms, width), F32),
            shape((atoms, width), BF16),
        ),
        in_specs=[smem] + whole(row_count + smp_count + 12),
        out_specs=tuple(whole(3)),
        scratch_shapes=[
            pltpu.VMEM((token_mask.shape[0], 2 * token_width), BF16),
            pltpu.VMEM((smp_count, heads, tok_rows, keys), F32),
            pltpu.VMEM((tok_rows, token_width), F32),
        ],
        compiler_params=vmem(56),
    )(
        place, *gathered, *biases, token_state, key_mask, token_qkv, token_proj, token_gain, ffn_in, ffn_out,
        scatter_out, encoded, mask, tokens, atom_gain,
    )
    low, high = halos_of(atom_normed)

    direction = pl.pallas_call(
        decoder_kernel,
        out_shape=shape((1,) + positions.shape[1:], F32),
        in_specs=[smem, smem] + whole(12),
        out_specs=whole(1)[0],
        scratch_shapes=window_scratch(atoms, width),
        compiler_params=vmem(40),
    )(
        place, window_offsets, level, positions, noise_draw, joined, low, atom_normed, high, mask, atom_qkv, atom_proj,
        out_gain.reshape(1, -1), coord_out,
    )
    return (token_result, direction)


def solution(mesh):
    in_specs = (
        P(("grp", "smp"), None, "row"),
        P(("grp", "smp"), None, "row"),
        P(("grp", "smp")),
        P(("grp", "row"), None),
        P(("grp", "row"), None),
        P(("grp", "row"), "smp", None),
        P(("grp", "row")),
        P(("grp", "row")),
        P("grp"),
        P("grp"),
        P(),
        P(),
        P(),
        P(),
        P(),
        P(),
        P(),
        P(),
        P(),
        P(),
        P(),
        P(),
        P(),
        P(),
        P(),
        P(),
    )
    out_specs = (P(("grp", "smp"), "row", None), P(("grp", "smp"), None, "row"))
    return jax.shard_map(
        per_device, mesh=mesh, in_specs=in_specs, out_specs=out_specs, check_vma=False
    )
```

```python
import functools
import math

import jax
import jax.numpy as jnp
from jax import lax
from jax.experimental import pallas as pl
from jax.experimental.pallas import tpu as pltpu
from jax.sharding import PartitionSpec as P

HEADS = 16
AHEADS = 4
WQ = 32
WK = 128
HALO = 96
LANES = 128
PRIVATE = 62

sigma_data = 16.0
gamma_boost = 0.8
norm_eps = 1e-05
masked_score = -1e30
LOG2E = math.log2(math.e)
F32 = jnp.float32
BF16 = jnp.bfloat16
NT = (((1,), (1,)), ((), ()))
TN = (((0,), (0,)), ((), ()))


def vmem(mib):
    return pltpu.CompilerParams(vmem_limit_bytes=mib * 1024 * 1024)


def cost(micros):
    return pl.CostEstimate(flops=int(micros * 1e9), transcendentals=0, bytes_accessed=int(micros * 3e6))


def hbm(count):
    return [pl.BlockSpec(memory_space=pltpu.HBM)] * count


def fetch(sources, targets, sems):
    copies = [pltpu.make_async_copy(a, b, sems.at[i]) for i, (a, b) in enumerate(zip(sources, targets))]
    for copy in copies:
        copy.start()
    return copies


def whole(count):
    return [pl.BlockSpec(memory_space=pltpu.VMEM)] * count


def dot(a, b, dims=(((1,), (0,)), ((), ()))):
    return lax.dot_general(a, b, dims, preferred_element_type=F32)


def norm_rows(values, gain):
    average = jnp.mean(values, axis=-1, keepdims=True)
    centred = values - average
    variance = jnp.mean(centred * centred, axis=-1, keepdims=True)
    return centred * lax.rsqrt(variance + norm_eps) * gain


def noisy_of(level, coords, kicks):
    level_hat = (1.0 + gamma_boost) * level
    noisy = coords + jnp.sqrt(level_hat * level_hat - level * level) * kicks
    return level_hat, noisy


def column_of(row):
    size = row.shape[1]
    down = lax.broadcasted_iota(jnp.int32, (size, size), 0)
    across = lax.broadcasted_iota(jnp.int32, (size, size), 1)
    spread = jnp.where(down == across, jnp.broadcast_to(row, (size, size)), 0.0)
    return dot(spread.astype(BF16), jnp.ones((size, LANES), BF16))


def rows_of(ref):
    return jnp.concatenate([ref[k] for k in range(ref.shape[0])], axis=0)


def write_edges(normed, low_edge_ref, high_edge_ref):
    low_edge_ref[...] = normed[:HALO]
    high_edge_ref[...] = normed[normed.shape[0] - HALO :]


def prepare_kernel(
    level_ref, coords_hbm, kicks_hbm, single_hbm, coord_in_hbm, gain_hbm, state_ref, normed_ref, low_edge_ref, high_edge_ref,
    coords_ref, kicks_ref, single_ref, coord_in_ref, gain_ref, sems
):
    copies = fetch(
        [coords_hbm, kicks_hbm, single_hbm, coord_in_hbm, gain_hbm],
        [coords_ref, kicks_ref, single_ref, coord_in_ref, gain_ref], sems,
    )
    for copy in copies:
        copy.wait()
    level_hat, noisy = noisy_of(level_ref[...], rows_of(coords_ref), rows_of(kicks_ref))
    scaled = noisy / jnp.sqrt(level_hat * level_hat + sigma_data * sigma_data)
    embedded = lax.dot_general(
        scaled, coord_in_ref[...], TN, precision=lax.Precision.HIGHEST, preferred_element_type=F32
    )
    state = single_ref[...].astype(F32) + embedded
    state_ref[...] = state
    normed = norm_rows(state, gain_ref[0:1]).astype(BF16)
    normed_ref[...] = normed
    write_edges(normed, low_edge_ref, high_edge_ref)


def pair_kernel(step_rows, tile_hbm, gain_hbm, heads_hbm, bias_ref, tile_ref, gain_ref, heads_ref, tile_sems, sems):
    keys, channels = tile_ref.shape[1:]
    head_count = heads_ref.shape[0]
    steps = tile_ref.shape[0] // step_rows
    small = fetch([gain_hbm, heads_hbm], [gain_ref, heads_ref], sems)
    spans = [pl.ds(step * step_rows, step_rows) for step in range(steps)]
    tiles = fetch([tile_hbm.at[span] for span in spans], [tile_ref.at[span] for span in spans], tile_sems)
    for copy in small:
        copy.wait()
    weights = heads_ref[...].astype(F32) * gain_ref[...]
    high = weights.astype(BF16)
    low = (weights - high.astype(F32)).astype(BF16)
    total = jnp.sum(high.astype(F32) + low.astype(F32), axis=1, keepdims=True)
    ones = jnp.ones((head_count, channels), BF16)
    left = jnp.concatenate([high, low, ones], axis=0)
    for step in range(steps):
        tiles[step].wait()
        begin = step * step_rows
        tile = tile_ref[begin : begin + step_rows].reshape(step_rows * keys, channels)
        wide = tile.astype(F32)
        square = wide * wide
        square_high = square.astype(BF16)
        square_low = (square - square_high.astype(F32)).astype(BF16)
        sums = dot(left, tile, NT)
        squares = dot(ones, square_high, NT) + dot(ones, square_low, NT)
        average = sums[2 * head_count :] / channels
        variance = jnp.maximum(squares / channels - average * average, 0.0)
        raw = sums[:head_count] + sums[head_count : 2 * head_count]
        result = (raw - average * total) * lax.rsqrt(variance + norm_eps)
        pieces = [result[:, i * keys : (i + 1) * keys] for i in range(step_rows)]
        bias_ref[:, begin : begin + step_rows, :] = jnp.stack(pieces, axis=1).astype(BF16)


def live_bias(mask_ref, chunk, outside):
    final = mask_ref.shape[0] - 1
    row = mask_ref[pl.ds(jnp.clip(chunk, 0, final), 1), :].astype(F32)
    column = column_of(row)
    column = jnp.where(outside, 0.0, column)
    return (column - 1.0) * -masked_score


def attend(queries, blocks, parts, lives, w_kv, offsets_ref, scratch):
    key_scr, value_scr, live_scr, score_scr, prob_scr, out_scr = scratch
    row_count, width = queries.shape
    block_count = len(blocks)
    head_size = width // AHEADS
    at = 0
    for part in parts:
        projected = dot(part, w_kv).astype(BF16).astype(F32)
        key_scr[at : at + part.shape[0], :] = projected[:, :width]
        value_scr[at : at + part.shape[0], :] = projected[:, width:]
        at += part.shape[0]
    at = 0
    for live in lives:
        live_scr[at : at + live.shape[0], :] = live
        at += live.shape[0]

    stacked_rows = AHEADS * WQ
    lane = lax.broadcasted_iota(jnp.int32, (stacked_rows, width), 1)
    line = lax.broadcasted_iota(jnp.int32, (stacked_rows, width), 0)
    own_head = lane // head_size == line // WQ
    pick = jnp.where(lane == 0, 1.0, 0.0).astype(BF16)
    ones = jnp.ones((WK, width), BF16)
    begins = []
    for b, (block, shift) in enumerate(blocks):
        begin = block * WQ + shift + offsets_ref[block]
        begins.append(begin)
        keys = key_scr[pl.ds(begin, WK), :].astype(BF16)
        live = live_scr[pl.ds(begin, WK), :].astype(BF16)
        query = queries[b * WQ : (b + 1) * WQ]
        query = jnp.concatenate([query] * AHEADS, axis=0)
        query = jnp.where(own_head, query, jnp.zeros_like(query))
        score_scr[b * stacked_rows : (b + 1) * stacked_rows, :] = dot(
            jnp.concatenate([query, pick], axis=1), jnp.concatenate([keys, live], axis=1), NT
        )
    factor = LOG2E / math.sqrt(head_size)
    step = 4 * stacked_rows
    for begin in range(0, block_count * stacked_rows, step):
        scores = score_scr[begin : begin + step, :]
        largest = jnp.max(scores, axis=-1, keepdims=True)
        prob_scr[begin : begin + step, :] = jnp.exp2((scores - largest) * factor).astype(BF16)
    for b in range(block_count):
        values = value_scr[pl.ds(begins[b], WK), :].astype(BF16)
        probs = prob_scr[b * stacked_rows : (b + 1) * stacked_rows, :]
        both = dot(probs, jnp.concatenate([values, ones], axis=1))
        mixed = jnp.where(own_head, both[:, :width], 0.0)
        weight = jnp.where(own_head, both[:, width:], 0.0)
        mixed = sum(mixed[h * WQ : (h + 1) * WQ] for h in range(AHEADS))
        weight = sum(weight[h * WQ : (h + 1) * WQ] for h in range(AHEADS))
        out_scr[b * WQ : (b + 1) * WQ, :] = (mixed / weight).astype(BF16)
    return out_scr[0:row_count, :]


def window_scratch(extended, row_count, width):
    scores = row_count * AHEADS
    return [
        pltpu.VMEM((extended, width), F32),
        pltpu.VMEM((extended, width), F32),
        pltpu.VMEM((extended, LANES), F32),
        pltpu.VMEM((scores, WK), F32),
        pltpu.VMEM((scores, WK), BF16),
        pltpu.VMEM((row_count, width), BF16),
    ]


def member_of(token_ref, mask_ref, first_chunk, base, tok_rows):
    chunk_count = token_ref.shape[0]
    tokens = lax.broadcasted_iota(jnp.int32, (tok_rows, LANES), 0)
    pieces = []
    for chunk in range(chunk_count):
        local = token_ref[chunk : chunk + 1, :] - base
        valid = mask_ref[pl.ds(first_chunk + chunk, 1), :]
        local = jnp.where(valid > 0, local, -1)
        pieces.append(jnp.where(local == tokens, 1.0, 0.0).astype(BF16))
    return jnp.concatenate(pieces, axis=1)


def encoder_kernel(
    place_ref, offsets_ref, level_ref, state_ref, low_ref, mid_ref, high_ref, mask_ref, token_ref, w_qkv_ref, w_out_ref,
    lift_hbm, single_hbm, embed_ref, gain_ref, encoded_ref, token_state_ref, normed_ref, member_ref, lift_ref, single_ref, sems,
    *scratch
):
    late = fetch([lift_hbm, single_hbm], [lift_ref, single_ref], sems)
    row, count = place_ref[0], place_ref[1]
    first, last = row == 0, row == count - 1
    tok_rows = single_ref.shape[0]
    chunks = token_ref.shape[0]
    width = state_ref.shape[1]
    begin = row * chunks
    low = jnp.where(first, jnp.zeros_like(low_ref[...]), low_ref[...])
    high = jnp.where(last, jnp.zeros_like(high_ref[...]), high_ref[...])
    mid = mid_ref[...]
    lives = [live_bias(mask_ref, begin - 1, first)[LANES - HALO :]]
    lives += [live_bias(mask_ref, begin + chunk, False) for chunk in range(chunks)]
    lives += [live_bias(mask_ref, begin + chunks, last)[:HALO]]
    w_qkv = w_qkv_ref[0]
    queries = dot(mid, w_qkv[:, :width]).astype(BF16)
    mixed = attend(
        queries, [(b, HALO) for b in range(mid.shape[0] // WQ)], [low, mid, high], lives, w_qkv[:, width:], offsets_ref, scratch
    )
    state = state_ref[...] + dot(mixed, w_out_ref[0])
    encoded_ref[...] = state
    for copy in late:
        copy.wait()
    lifted = jnp.maximum(dot(state.astype(BF16), lift_ref[...]), 0.0).astype(BF16)
    member = member_of(token_ref, mask_ref, begin, row * tok_rows, tok_rows)
    member_ref[...] = member
    counts = jnp.maximum(dot(member, jnp.ones((member.shape[1], LANES), BF16)), 1.0)
    pooled = dot(member, lifted) / counts[:, 0:1]
    level_hat = (1.0 + gamma_boost) * level_ref[...]
    token_state = (
        pooled + single_ref[...].astype(F32) + jnp.log(level_hat / sigma_data) / 4.0 * embed_ref[...]
    )
    token_state_ref[...] = token_state
    normed_ref[...] = norm_rows(token_state, gain_ref[0:1]).astype(BF16)


def head_spans(head_size):
    spans = []
    for h in range(HEADS):
        begin = h * head_size // LANES * LANES
        end = -(-(h + 1) * head_size // LANES) * LANES
        spans.append((begin, end))
    return spans


def inside_head(h, head_size, shape, begin):
    lane = lax.broadcasted_iota(jnp.int32, shape, 1) + begin
    return (lane >= h * head_size) & (lane < (h + 1) * head_size)


def token_scores(query_of, kv_scr, bias_of, key_mask_ref, row, near, count, per_block, spans, scale, score_scr):
    piece = key_mask_ref.shape[1]

    def one(at):
        other = (row ^ (near + at // per_block)) * per_block + at % per_block
        live = key_mask_ref[pl.ds(other, 1), :] > 0
        rows = pl.ds(at * piece if isinstance(at, int) else pl.multiple_of(at * piece, piece), piece)
        for h in range(HEADS):
            begin, end = spans[h]
            scores = dot(query_of(h), kv_scr[rows, begin:end], NT) * scale
            scores = scores + bias_of(at, other, h).astype(F32)
            score_scr[at, h] = jnp.where(live, scores, masked_score)

    if count <= 4:
        for at in range(count):
            one(at)
    else:
        lax.fori_loop(0, count, lambda at, carry: (one(at), carry)[1], 0)


def attend_first_kernel(near_count, row_count, smp_count, *refs):
    place_ref = refs[0]
    normed_refs = refs[1 : 1 + near_count]
    bias_refs = refs[1 + near_count : 1 + near_count + smp_count]
    (
        key_mask_ref, w_qkv_ref, query_ref, mixed_ref, stat_ref, far_bias_ref, kv_scr, score_scr, bias_scr,
    ) = refs[1 + near_count + smp_count :]
    row, smp = place_ref[0], place_ref[2]
    tok_rows, width = query_ref.shape
    head_size = width // HEADS
    piece = key_mask_ref.shape[1]
    per_block = tok_rows // piece
    for d in range(smp_count):
        bias_scr[smp ^ d] = bias_refs[d][...]
    for d in range(near_count, row_count):
        for e in range(per_block):
            far_bias_ref[(d - near_count) * per_block + e] = bias_scr[(row ^ d) * per_block + e]
    queries = dot(normed_refs[0][...], w_qkv_ref[:, :width]).astype(BF16)
    query_ref[...] = queries
    for d in range(near_count):
        kv_scr[d * tok_rows : (d + 1) * tok_rows, :] = dot(normed_refs[d][...], w_qkv_ref[:, width:]).astype(BF16)
    spans = head_spans(head_size)

    def query_of(h):
        begin, end = spans[h]
        query = queries[:, begin:end]
        return jnp.where(inside_head(h, head_size, query.shape, begin), query, jnp.zeros_like(query))

    count = near_count * per_block
    token_scores(
        query_of, kv_scr, lambda at, other, h: bias_scr[other, h], key_mask_ref, row, 0, count, per_block, spans,
        1.0 / math.sqrt(head_size), score_scr,
    )
    mixed_ref[...] = jnp.zeros_like(mixed_ref)
    lane = lax.broadcasted_iota(jnp.int32, (tok_rows, LANES), 1)
    stats = jnp.zeros((tok_rows, LANES), F32)
    for h in range(HEADS):
        begin, end = spans[h]
        scores = [score_scr[at, h] for at in range(count)]
        largest = jnp.max(functools.reduce(jnp.maximum, scores), axis=-1, keepdims=True)
        exponents = [jnp.exp2((part - largest) * LOG2E) for part in scores]
        total = jnp.sum(functools.reduce(jnp.add, exponents), axis=-1, keepdims=True)
        mixed = functools.reduce(
            jnp.add,
            [
                dot(exponents[at].astype(BF16), kv_scr[at * piece : (at + 1) * piece, width + begin : width + end])
                for at in range(count)
            ],
        )
        mixed_ref[:, begin:end] += jnp.where(inside_head(h, head_size, mixed.shape, begin), mixed, 0.0)
        stats = jnp.where(lane == h, largest, jnp.where(lane == HEADS + h, total, stats))
    stat_ref[...] = stats


def token_kernel(near_count, row_count, *refs):
    far_count = row_count - near_count
    place_ref = refs[0]
    normed_refs = refs[1 : 1 + far_count]
    (
        query_ref, carried_ref, stat_ref, bias_ref, state_ref, key_mask_ref, w_qkv_ref, w_proj_ref, gain_ref, ffn_in_ref,
        ffn_out_ref, spread_ref, encoded_ref, member_ref, atom_gain_ref, out_ref, joined_ref, atom_normed_ref,
        low_edge_ref, high_edge_ref, kv_scr, score_scr, mixed_scr,
    ) = refs[1 + far_count :]
    row = place_ref[0]
    tok_rows, width = state_ref.shape
    head_size = width // HEADS
    piece = key_mask_ref.shape[1]
    per_block = tok_rows // piece
    for d in range(far_count):
        kv_scr[d * tok_rows : (d + 1) * tok_rows, :] = dot(normed_refs[d][...], w_qkv_ref[:, width:]).astype(BF16)
    spans = head_spans(head_size)
    queries = query_ref[...]

    def query_of(h):
        begin, end = spans[h]
        query = queries[:, begin:end]
        return jnp.where(inside_head(h, head_size, query.shape, begin), query, jnp.zeros_like(query))

    count = far_count * per_block
    token_scores(
        query_of, kv_scr, lambda at, other, h: bias_ref[at, h], key_mask_ref, row, near_count, count, per_block, spans,
        1.0 / math.sqrt(head_size), score_scr,
    )
    mixed_scr[...] = jnp.zeros_like(mixed_scr)
    for h in range(HEADS):
        begin, end = spans[h]
        scores = [score_scr[at, h] for at in range(count)]
        before = stat_ref[:, h : h + 1]
        largest = jnp.max(functools.reduce(jnp.maximum, scores), axis=-1, keepdims=True)
        largest = jnp.maximum(largest, before)
        exponents = [jnp.exp2((part - largest) * LOG2E) for part in scores]
        shrink = jnp.exp2((before - largest) * LOG2E)
        total = jnp.sum(functools.reduce(jnp.add, exponents), axis=-1, keepdims=True)
        total = total + shrink * stat_ref[:, HEADS + h : HEADS + h + 1]
        mixed = functools.reduce(
            jnp.add,
            [
                dot(exponents[at].astype(BF16), kv_scr[at * piece : (at + 1) * piece, width + begin : width + end])
                for at in range(count)
            ],
        )
        mixed = (mixed + shrink * carried_ref[:, begin:end]) / total
        mixed_scr[:, begin:end] += jnp.where(inside_head(h, head_size, mixed.shape, begin), mixed, 0.0)
    state = state_ref[...] + dot(mixed_scr[...].astype(BF16), w_proj_ref[...])
    normed = norm_rows(state, gain_ref[1:2]).astype(BF16)
    hidden = dot(normed, ffn_in_ref[...])
    half = hidden.shape[1] // 2
    gate, up = hidden[:, :half], hidden[:, half:]
    active = (gate / (1.0 + jnp.exp(-gate)) * up).astype(BF16)
    state = state + dot(active, ffn_out_ref[...])
    result = state.astype(BF16)
    out_ref[0] = result
    spread = dot(result, spread_ref[...]).astype(BF16)
    joined = encoded_ref[...] + dot(member_ref[...], spread, TN)
    joined_ref[...] = joined
    normed = norm_rows(joined, atom_gain_ref[1:2]).astype(BF16)
    atom_normed_ref[...] = normed
    write_edges(normed, low_edge_ref, high_edge_ref)


def directions(state, level_ref, coords_ref, kicks_ref, gain_ref, coord_out_ref, direction_ref, begin):
    rows = state.shape[0]
    normed = norm_rows(state, gain_ref[...]).astype(BF16)
    update = dot(coord_out_ref[...], normed, NT)
    for k in range(coords_ref.shape[0]):
        level_hat, noisy = noisy_of(
            level_ref[...], coords_ref[k, :, begin : begin + rows], kicks_ref[k, :, begin : begin + rows]
        )
        base_square = sigma_data * sigma_data + level_hat * level_hat
        skip_scale = sigma_data * sigma_data / base_square
        out_scale = level_hat * sigma_data / jnp.sqrt(base_square)
        denoised = skip_scale * noisy + out_scale * update[k : k + 1]
        direction_ref[k, :, begin : begin + rows] = (noisy - denoised) / level_hat


def inner_kernel(
    place_ref, offsets_ref, level_ref, coords_ref, kicks_ref, state_ref, mid_ref, mask_ref, w_qkv_ref, w_out_ref, gain_ref,
    coord_out_ref, direction_ref, *scratch
):
    atoms, width = state_ref.shape
    chunks = atoms // LANES
    begin = place_ref[0] * chunks
    edge = LANES
    skip = edge - HALO
    lives = [live_bias(mask_ref, begin, False)[skip:]]
    lives += [live_bias(mask_ref, begin + chunk, False) for chunk in range(1, chunks)]
    w_qkv = w_qkv_ref[1]
    queries = dot(mid_ref[edge : atoms - edge, :], w_qkv[:, :width]).astype(BF16)
    blocks = [(b, -skip) for b in range(edge // WQ, (atoms - edge) // WQ)]
    mixed = attend(queries, blocks, [mid_ref[skip:, :]], lives, w_qkv[:, width:], offsets_ref, scratch)
    state = state_ref[edge : atoms - edge, :] + dot(mixed, w_out_ref[1])
    for k in range(direction_ref.shape[0]):
        direction_ref[k, :, 0:edge] = jnp.zeros((1, edge), F32)
        direction_ref[k, :, atoms - edge :] = jnp.zeros((1, edge), F32)
    directions(state, level_ref, coords_ref, kicks_ref, gain_ref, coord_out_ref, direction_ref, edge)


def edge_kernel(
    place_ref, offsets_ref, level_ref, coords_ref, kicks_ref, state_ref, low_ref, mid_ref, high_ref, mask_ref, w_qkv_ref,
    w_out_ref, gain_ref, coord_out_ref, inner_ref, direction_ref, *scratch
):
    row, count = place_ref[0], place_ref[1]
    first, last = row == 0, row == count - 1
    atoms, width = state_ref.shape
    chunks = atoms // LANES
    begin = row * chunks
    edge = LANES
    reach = edge + HALO
    w_qkv = w_qkv_ref[1]
    w_out = w_out_ref[1]
    for k in range(direction_ref.shape[0]):
        direction_ref[k, :, edge : atoms - edge] = inner_ref[k, :, edge : atoms - edge]
    low = jnp.where(first, jnp.zeros_like(low_ref[...]), low_ref[...])
    high = jnp.where(last, jnp.zeros_like(high_ref[...]), high_ref[...])
    lives = [
        live_bias(mask_ref, begin - 1, first)[LANES - HALO :],
        live_bias(mask_ref, begin, False),
        live_bias(mask_ref, begin + 1, False)[:HALO],
        live_bias(mask_ref, begin + chunks - 2, False)[LANES - HALO :],
        live_bias(mask_ref, begin + chunks - 1, False),
        live_bias(mask_ref, begin + chunks, last)[:HALO],
    ]
    own = jnp.concatenate([mid_ref[0:edge, :], mid_ref[atoms - edge :, :]], axis=0)
    queries = dot(own, w_qkv[:, :width]).astype(BF16)
    span = edge + 2 * HALO
    blocks = [(b, HALO) for b in range(edge // WQ)]
    blocks += [(b, span + reach - atoms) for b in range((atoms - edge) // WQ, atoms // WQ)]
    mixed = attend(
        queries, blocks, [low, mid_ref[0:reach, :], mid_ref[atoms - reach :, :], high], lives, w_qkv[:, width:], offsets_ref,
        scratch,
    )
    shift = dot(mixed, w_out)
    lower = state_ref[0:edge, :] + shift[:edge]
    upper = state_ref[atoms - edge :, :] + shift[edge:]
    directions(lower, level_ref, coords_ref, kicks_ref, gain_ref, coord_out_ref, direction_ref, 0)
    directions(upper, level_ref, coords_ref, kicks_ref, gain_ref, coord_out_ref, direction_ref, atoms - edge)


def halos_of(low_edge, high_edge):
    count = lax.axis_size("row")
    up = [(i, (i + 1) % count) for i in range(count)]
    down = [((i + 1) % count, i) for i in range(count)]
    low = lax.ppermute(high_edge, "row", up)
    high = lax.ppermute(low_edge, "row", down)
    return low, high


def spread_over(block, axis, after=None):
    count = lax.axis_size(axis)
    have = {0: block}
    bit = count // 2
    while bit:
        pairs = [(i, i ^ bit) for i in range(count)]
        for d in list(have):
            sent = have[d]
            if d and after is not None:
                sent, _ = lax.optimization_barrier((sent, after))
            have[d | bit] = lax.ppermute(sent, axis, pairs)
        bit //= 2
    return [have[d] for d in range(count)]


def per_device(
    positions,
    noise_draw,
    noise_level,
    atom_single,
    token_single,
    pair_cond,
    atom_to_token,
    window_offsets,
    atom_mask,
    token_mask,
    coord_in,
    atom_gain,
    atom_qkv,
    atom_proj,
    gather_in,
    noise_embed,
    pair_gain,
    pair_heads,
    token_gain,
    token_qkv,
    token_proj,
    ffn_in,
    ffn_out,
    scatter_out,
    out_gain,
    coord_out,
):
    row_count, smp_count = lax.axis_size("row"), lax.axis_size("smp")
    atoms, width = atom_single.shape
    tok_rows, token_width = token_single.shape
    heads = pair_heads.shape[1]
    keys = pair_cond.shape[1]
    place = jnp.stack(
        [lax.axis_index("row"), jnp.int32(row_count), lax.axis_index("smp")]
    ).astype(jnp.int32)
    level = noise_level.reshape(1, 1)
    coords = positions.transpose(1, 0, 2)
    kicks = noise_draw.transpose(1, 0, 2)
    mask = atom_mask.reshape(-1, LANES)
    tokens = atom_to_token.reshape(-1, LANES)
    smem = pl.BlockSpec(memory_space=pltpu.SMEM)
    shape = jax.ShapeDtypeStruct
    state_like = shape((atoms, width), F32)
    normed_like = shape((atoms, width), BF16)
    edge_like = shape((HALO, width), BF16)

    state, normed, low_edge, high_edge = pl.pallas_call(
        prepare_kernel,
        out_shape=(state_like, normed_like, edge_like, edge_like),
        in_specs=whole(1) + hbm(5),
        out_specs=tuple(whole(4)),
        scratch_shapes=[pltpu.VMEM(a.shape, a.dtype) for a in (coords, kicks, atom_single, coord_in, atom_gain)]
        + [pltpu.SemaphoreType.DMA((5,))],
        compiler_params=vmem(PRIVATE),
        cost_estimate=cost(1.5),
    )(level, coords, kicks, atom_single, coord_in, atom_gain)
    low, high = halos_of(low_edge, high_edge)

    pair_rows, _, channels = pair_cond.shape
    step_rows = 16
    gain_row, _ = lax.optimization_barrier((pair_gain, low_edge))
    bias = pl.pallas_call(
        functools.partial(pair_kernel, step_rows),
        out_shape=shape((heads, pair_rows, keys), BF16),
        in_specs=hbm(3),
        out_specs=whole(1)[0],
        scratch_shapes=[
            pltpu.VMEM(pair_cond.shape, BF16),
            pltpu.VMEM((1, channels), F32),
            pltpu.VMEM((heads, channels), BF16),
            pltpu.SemaphoreType.DMA((pair_rows // step_rows,)),
            pltpu.SemaphoreType.DMA((2,)),
        ],
        compiler_params=vmem(PRIVATE),
        cost_estimate=cost(5),
    )(pair_cond, gain_row.reshape(1, -1), pair_heads.T)

    encoded, token_state, token_normed, member = pl.pallas_call(
        encoder_kernel,
        out_shape=(
            state_like,
            shape((tok_rows, token_width), F32),
            shape((tok_rows, token_width), BF16),
            shape((tok_rows, atoms), BF16),
        ),
        in_specs=[smem, smem] + whole(9) + hbm(2) + whole(2),
        out_specs=tuple(whole(4)),
        scratch_shapes=[
            pltpu.VMEM(gather_in.shape, BF16),
            pltpu.VMEM(token_single.shape, BF16),
            pltpu.SemaphoreType.DMA((2,)),
        ]
        + window_scratch(atoms + 2 * HALO, atoms, width),
        compiler_params=vmem(16),
        cost_estimate=cost(3.4),
    )(
        place, window_offsets, level, state, low, normed, high, mask, tokens, atom_qkv, atom_proj, gather_in,
        token_single, noise_embed.reshape(1, -1), token_gain,
    )
    gathered = spread_over(token_normed, "row")
    biases = spread_over(bias, "smp", gathered[1 : row_count // 2 + 1])

    key_mask = token_mask.reshape(-1, keys)
    near_count = row_count - row_count // 4
    far_count = row_count - near_count
    pieces = tok_rows // keys

    def need(count):
        tile = tok_rows * max(keys, LANES)
        return (count * (keys * token_width * 4 + heads * tile * 4) + smp_count * heads * tile * 2) // 2**20 + 1

    queries, carried, stats, far_bias = pl.pallas_call(
        functools.partial(attend_first_kernel, near_count, row_count, smp_count),
        out_shape=(
            shape((tok_rows, token_width), BF16),
            shape((tok_rows, token_width), F32),
            shape((tok_rows, LANES), F32),
            shape((far_count * pieces, heads, tok_rows, keys), BF16),
        ),
        in_specs=[smem] + whole(near_count + smp_count + 2),
        out_specs=tuple(whole(4)),
        scratch_shapes=[
            pltpu.VMEM((near_count * tok_rows, 2 * token_width), BF16),
            pltpu.VMEM((near_count * pieces, heads, tok_rows, keys), F32),
            pltpu.VMEM((smp_count, heads, tok_rows, keys), BF16),
        ],
        compiler_params=vmem(8 + 2 * need(near_count * pieces)),
        cost_estimate=cost(4),
    )(place, *gathered[:near_count], *biases, key_mask, token_qkv)
    token_result, joined, atom_normed, low_edge, high_edge = pl.pallas_call(
        functools.partial(token_kernel, near_count, row_count),
        out_shape=(
            shape((1, tok_rows, token_width), BF16),
            state_like,
            normed_like,
            edge_like,
            edge_like,
        ),
        in_specs=[smem] + whole(far_count + 15),
        out_specs=tuple(whole(5)),
        scratch_shapes=[
            pltpu.VMEM((far_count * tok_rows, 2 * token_width), BF16),
            pltpu.VMEM((far_count * pieces, heads, tok_rows, keys), F32),
            pltpu.VMEM((tok_rows, token_width), F32),
        ],
        compiler_params=vmem(20 + need(far_count * pieces)),
        cost_estimate=cost(6),
    )(
        place, *gathered[near_count:], queries, carried, stats, far_bias, token_state, key_mask, token_qkv, token_proj,
        token_gain, ffn_in, ffn_out, scatter_out, encoded, member, atom_gain,
    )
    low, high = halos_of(low_edge, high_edge)

    edge = LANES
    direction_like = shape(coords.shape, F32)
    out_row = out_gain.reshape(1, -1)
    inner = pl.pallas_call(
        inner_kernel,
        out_shape=direction_like,
        in_specs=[smem, smem] + whole(10),
        out_specs=whole(1)[0],
        scratch_shapes=window_scratch(atoms - edge + HALO, atoms - 2 * edge, width),
        compiler_params=vmem(16),
        cost_estimate=cost(2.7),
    )(
        place, window_offsets, level, coords, kicks, joined, atom_normed, mask, atom_qkv, atom_proj, out_row, coord_out
    )
    direction = pl.pallas_call(
        edge_kernel,
        out_shape=direction_like,
        in_specs=[smem, smem] + whole(13),
        out_specs=whole(1)[0],
        scratch_shapes=window_scratch(2 * (edge + 2 * HALO), 2 * edge, width),
        compiler_params=vmem(12),
        cost_estimate=cost(2),
    )(
        place, window_offsets, level, coords, kicks, joined, low, atom_normed, high, mask, atom_qkv, atom_proj, out_row,
        coord_out, inner,
    )
    return (token_result, direction.transpose(1, 0, 2))


def solution(mesh):
    in_specs = (
        P(("grp", "smp"), None, "row"),
        P(("grp", "smp"), None, "row"),
        P(("grp", "smp")),
        P(("grp", "row"), None),
        P(("grp", "row"), None),
        P(("grp", "row"), "smp", None),
        P(("grp", "row")),
        P(("grp", "row")),
        P("grp"),
        P("grp"),
        P(),
        P(),
        P(),
        P(),
        P(),
        P(),
        P(),
        P(),
        P(),
        P(),
        P(),
        P(),
        P(),
        P(),
        P(),
        P(),
    )
    out_specs = (P(("grp", "smp"), "row", None), P(("grp", "smp"), None, "row"))
    return jax.shard_map(
        per_device, mesh=mesh, in_specs=in_specs, out_specs=out_specs, check_vma=False
    )
```

```python
import functools
import math

import jax
import jax.numpy as jnp
from jax import lax
from jax.experimental import pallas as pl
from jax.experimental.pallas import tpu as pltpu
from jax.sharding import PartitionSpec as P

HEADS = 16
AHEADS = 4
WQ = 32
WK = 128
HALO = 96
LANES = 128
PRIVATE = 62

sigma_data = 16.0
gamma_boost = 0.8
norm_eps = 1e-05
masked_score = -1e30
LOG2E = math.log2(math.e)
F32 = jnp.float32
BF16 = jnp.bfloat16
NT = (((1,), (1,)), ((), ()))
TN = (((0,), (0,)), ((), ()))


def vmem(mib):
    return pltpu.CompilerParams(vmem_limit_bytes=mib * 1024 * 1024)


def cost(micros):
    return pl.CostEstimate(flops=int(micros * 1e9), transcendentals=0, bytes_accessed=int(micros * 3e6))


def hbm(count):
    return [pl.BlockSpec(memory_space=pltpu.HBM)] * count


def fetch(sources, targets, sems):
    copies = [pltpu.make_async_copy(a, b, sems.at[i]) for i, (a, b) in enumerate(zip(sources, targets))]
    for copy in copies:
        copy.start()
    return copies


def whole(count):
    return [pl.BlockSpec(memory_space=pltpu.VMEM)] * count


def dot(a, b, dims=(((1,), (0,)), ((), ()))):
    return lax.dot_general(a, b, dims, preferred_element_type=F32)


def norm_rows(values, gain):
    average = jnp.mean(values, axis=-1, keepdims=True)
    centred = values - average
    variance = jnp.mean(centred * centred, axis=-1, keepdims=True)
    return centred * lax.rsqrt(variance + norm_eps) * gain


def noisy_of(level, coords, kicks):
    level_hat = (1.0 + gamma_boost) * level
    noisy = coords + jnp.sqrt(level_hat * level_hat - level * level) * kicks
    return level_hat, noisy


def column_of(row):
    size = row.shape[1]
    down = lax.broadcasted_iota(jnp.int32, (size, size), 0)
    across = lax.broadcasted_iota(jnp.int32, (size, size), 1)
    spread = jnp.where(down == across, jnp.broadcast_to(row, (size, size)), 0.0)
    return dot(spread.astype(BF16), jnp.ones((size, LANES), BF16))


def rows_of(ref):
    return jnp.concatenate([ref[k] for k in range(ref.shape[0])], axis=0)


def write_edges(normed, low_edge_ref, high_edge_ref):
    low_edge_ref[...] = normed[:HALO]
    high_edge_ref[...] = normed[normed.shape[0] - HALO :]


def prepare_kernel(
    level_ref, coords_hbm, kicks_hbm, single_hbm, coord_in_hbm, gain_hbm, state_ref, normed_ref, low_edge_ref, high_edge_ref,
    coords_ref, kicks_ref, single_ref, coord_in_ref, gain_ref, sems
):
    copies = fetch(
        [coords_hbm, kicks_hbm, single_hbm, coord_in_hbm, gain_hbm],
        [coords_ref, kicks_ref, single_ref, coord_in_ref, gain_ref], sems,
    )
    for copy in copies:
        copy.wait()
    level_hat, noisy = noisy_of(level_ref[...], rows_of(coords_ref), rows_of(kicks_ref))
    scaled = noisy / jnp.sqrt(level_hat * level_hat + sigma_data * sigma_data)
    embedded = lax.dot_general(
        scaled, coord_in_ref[...], TN, precision=lax.Precision.HIGHEST, preferred_element_type=F32
    )
    state = single_ref[...].astype(F32) + embedded
    state_ref[...] = state
    normed = norm_rows(state, gain_ref[0:1]).astype(BF16)
    normed_ref[...] = normed
    write_edges(normed, low_edge_ref, high_edge_ref)


def pair_kernel(step_rows, tile_hbm, gain_hbm, heads_hbm, bias_ref, tile_ref, gain_ref, heads_ref, tile_sems, sems):
    keys, channels = tile_ref.shape[1:]
    head_count = heads_ref.shape[0]
    steps = tile_ref.shape[0] // step_rows
    small = fetch([gain_hbm, heads_hbm], [gain_ref, heads_ref], sems)
    spans = [pl.ds(step * step_rows, step_rows) for step in range(steps)]
    tiles = fetch([tile_hbm.at[span] for span in spans], [tile_ref.at[span] for span in spans], tile_sems)
    for copy in small:
        copy.wait()
    weights = heads_ref[...].astype(F32) * gain_ref[...]
    high = weights.astype(BF16)
    low = (weights - high.astype(F32)).astype(BF16)
    total = jnp.sum(high.astype(F32) + low.astype(F32), axis=1, keepdims=True)
    left = jnp.concatenate([high, low], axis=0)
    for step in range(steps):
        tiles[step].wait()
        begin = step * step_rows
        tile = tile_ref[begin : begin + step_rows].reshape(step_rows * keys, channels).T
        wide = tile.astype(F32)
        average = jnp.mean(wide, axis=0, keepdims=True)
        centred = wide - average
        variance = jnp.mean(centred * centred, axis=0, keepdims=True)
        sums = dot(left, tile)
        raw = sums[:head_count] + sums[head_count:]
        result = (raw - average * total) * lax.rsqrt(variance + norm_eps)
        pieces = [result[:, i * keys : (i + 1) * keys] for i in range(step_rows)]
        bias_ref[:, begin : begin + step_rows, :] = jnp.swapaxes(jnp.stack(pieces, axis=0), 0, 1).astype(BF16)


def live_bias(mask_ref, chunk, outside):
    final = mask_ref.shape[0] - 1
    row = mask_ref[pl.ds(jnp.clip(chunk, 0, final), 1), :].astype(F32)
    column = column_of(row)
    column = jnp.where(outside, 0.0, column)
    return (column - 1.0) * -masked_score


def attend(queries, blocks, parts, lives, w_kv, offsets_ref, scratch):
    key_scr, value_scr, live_scr, score_scr, prob_scr, out_scr = scratch
    row_count, width = queries.shape
    block_count = len(blocks)
    head_size = width // AHEADS
    at = 0
    for part in parts:
        projected = dot(part, w_kv).astype(BF16).astype(F32)
        key_scr[at : at + part.shape[0], :] = projected[:, :width]
        value_scr[at : at + part.shape[0], :] = projected[:, width:]
        at += part.shape[0]
    at = 0
    for live in lives:
        live_scr[at : at + live.shape[0], :] = live
        at += live.shape[0]

    stacked_rows = AHEADS * WQ
    lane = lax.broadcasted_iota(jnp.int32, (stacked_rows, width), 1)
    line = lax.broadcasted_iota(jnp.int32, (stacked_rows, width), 0)
    own_head = lane // head_size == line // WQ
    pick = jnp.where(lane == 0, 1.0, 0.0).astype(BF16)
    ones = jnp.ones((WK, width), BF16)
    begins = []
    for b, (block, shift) in enumerate(blocks):
        begin = block * WQ + shift + offsets_ref[block]
        begins.append(begin)
        keys = key_scr[pl.ds(begin, WK), :].astype(BF16)
        live = live_scr[pl.ds(begin, WK), :].astype(BF16)
        query = queries[b * WQ : (b + 1) * WQ]
        query = jnp.concatenate([query] * AHEADS, axis=0)
        query = jnp.where(own_head, query, jnp.zeros_like(query))
        score_scr[b * stacked_rows : (b + 1) * stacked_rows, :] = dot(
            jnp.concatenate([query, pick], axis=1), jnp.concatenate([keys, live], axis=1), NT
        )
    factor = LOG2E / math.sqrt(head_size)
    step = 4 * stacked_rows
    for begin in range(0, block_count * stacked_rows, step):
        scores = score_scr[begin : begin + step, :]
        largest = jnp.max(scores, axis=-1, keepdims=True)
        prob_scr[begin : begin + step, :] = jnp.exp2((scores - largest) * factor).astype(BF16)
    for b in range(block_count):
        values = value_scr[pl.ds(begins[b], WK), :].astype(BF16)
        probs = prob_scr[b * stacked_rows : (b + 1) * stacked_rows, :]
        both = dot(probs, jnp.concatenate([values, ones], axis=1))
        mixed = jnp.where(own_head, both[:, :width], 0.0)
        weight = jnp.where(own_head, both[:, width:], 0.0)
        mixed = sum(mixed[h * WQ : (h + 1) * WQ] for h in range(AHEADS))
        weight = sum(weight[h * WQ : (h + 1) * WQ] for h in range(AHEADS))
        out_scr[b * WQ : (b + 1) * WQ, :] = (mixed / weight).astype(BF16)
    return out_scr[0:row_count, :]


def window_scratch(extended, row_count, width):
    scores = row_count * AHEADS
    return [
        pltpu.VMEM((extended, width), F32),
        pltpu.VMEM((extended, width), F32),
        pltpu.VMEM((extended, LANES), F32),
        pltpu.VMEM((scores, WK), F32),
        pltpu.VMEM((scores, WK), BF16),
        pltpu.VMEM((row_count, width), BF16),
    ]


def member_of(token_ref, mask_ref, first_chunk, base, tok_rows):
    chunk_count = token_ref.shape[0]
    tokens = lax.broadcasted_iota(jnp.int32, (tok_rows, LANES), 0)
    pieces = []
    for chunk in range(chunk_count):
        local = token_ref[chunk : chunk + 1, :] - base
        valid = mask_ref[pl.ds(first_chunk + chunk, 1), :]
        local = jnp.where(valid > 0, local, -1)
        pieces.append(jnp.where(local == tokens, 1.0, 0.0).astype(BF16))
    return jnp.concatenate(pieces, axis=1)


def encoder_kernel(
    place_ref, offsets_ref, level_ref, state_ref, low_ref, mid_ref, high_ref, mask_ref, token_ref, w_qkv_ref, w_out_ref,
    lift_hbm, single_hbm, embed_ref, gain_ref, encoded_ref, token_state_ref, normed_ref, member_ref, lift_ref, single_ref, sems,
    *scratch
):
    late = fetch([lift_hbm, single_hbm], [lift_ref, single_ref], sems)
    row, count = place_ref[0], place_ref[1]
    first, last = row == 0, row == count - 1
    tok_rows = single_ref.shape[0]
    chunks = token_ref.shape[0]
    width = state_ref.shape[1]
    begin = row * chunks
    low = jnp.where(first, jnp.zeros_like(low_ref[...]), low_ref[...])
    high = jnp.where(last, jnp.zeros_like(high_ref[...]), high_ref[...])
    mid = mid_ref[...]
    lives = [live_bias(mask_ref, begin - 1, first)[LANES - HALO :]]
    lives += [live_bias(mask_ref, begin + chunk, False) for chunk in range(chunks)]
    lives += [live_bias(mask_ref, begin + chunks, last)[:HALO]]
    w_qkv = w_qkv_ref[0]
    queries = dot(mid, w_qkv[:, :width]).astype(BF16)
    mixed = attend(
        queries, [(b, HALO) for b in range(mid.shape[0] // WQ)], [low, mid, high], lives, w_qkv[:, width:], offsets_ref, scratch
    )
    state = state_ref[...] + dot(mixed, w_out_ref[0])
    encoded_ref[...] = state
    for copy in late:
        copy.wait()
    lifted = jnp.maximum(dot(state.astype(BF16), lift_ref[...]), 0.0).astype(BF16)
    member = member_of(token_ref, mask_ref, begin, row * tok_rows, tok_rows)
    member_ref[...] = member
    counts = jnp.maximum(dot(member, jnp.ones((member.shape[1], LANES), BF16)), 1.0)
    pooled = dot(member, lifted) / counts[:, 0:1]
    level_hat = (1.0 + gamma_boost) * level_ref[...]
    token_state = (
        pooled + single_ref[...].astype(F32) + jnp.log(level_hat / sigma_data) / 4.0 * embed_ref[...]
    )
    token_state_ref[...] = token_state
    normed_ref[...] = norm_rows(token_state, gain_ref[0:1]).astype(BF16)


def head_spans(head_size):
    spans = []
    for h in range(HEADS):
        begin = h * head_size // LANES * LANES
        end = -(-(h + 1) * head_size // LANES) * LANES
        spans.append((begin, end))
    return spans


def inside_head(h, head_size, shape, begin):
    lane = lax.broadcasted_iota(jnp.int32, shape, 1) + begin
    return (lane >= h * head_size) & (lane < (h + 1) * head_size)


class Tiles:
    def __init__(self, rows, width):
        self.rows = rows
        self.tiles = [None] * (width // LANES)

    def add(self, h, head_size, begin, values):
        for at in range(0, values.shape[1], LANES):
            tile = (begin + at) // LANES
            inside = inside_head(h, head_size, (self.rows, LANES), begin + at)
            kept = self.tiles[tile]
            part = values[:, at : at + LANES]
            self.tiles[tile] = jnp.where(inside, part, 0.0 if kept is None else kept)

    def join(self):
        return jnp.concatenate(self.tiles, axis=1)


def weighted_values(prob_scr, kv_scr, h, count, piece, begin, end):
    ones = jnp.ones((piece, LANES), BF16)
    return functools.reduce(
        jnp.add,
        [
            dot(prob_scr[at, h], jnp.concatenate([kv_scr[at * piece : (at + 1) * piece, begin:end], ones], axis=1))
            for at in range(count)
        ],
    )


def token_scores(query_of, kv_scr, bias_of, key_mask_ref, row, near, count, per_block, spans, scale, score_scr):
    piece = key_mask_ref.shape[1]

    def one(at):
        other = (row ^ (near + at // per_block)) * per_block + at % per_block
        live = key_mask_ref[pl.ds(other, 1), :] > 0
        rows = pl.ds(at * piece if isinstance(at, int) else pl.multiple_of(at * piece, piece), piece)
        for h in range(HEADS):
            begin, end = spans[h]
            scores = dot(query_of(h), kv_scr[rows, begin:end], NT) * scale
            scores = scores + bias_of(at, other, h).astype(F32)
            score_scr[at, h] = jnp.where(live, scores, masked_score)

    if count <= 4:
        for at in range(count):
            one(at)
    else:
        lax.fori_loop(0, count, lambda at, carry: (one(at), carry)[1], 0)


def attend_first_kernel(near_count, row_count, smp_count, *refs):
    place_ref = refs[0]
    normed_refs = refs[1 : 1 + near_count]
    bias_refs = refs[1 + near_count : 1 + near_count + smp_count]
    (
        key_mask_ref, w_qkv_ref, query_ref, mixed_ref, largest_ref, total_ref, far_bias_ref, kv_scr, score_scr, prob_scr,
        bias_scr,
    ) = refs[1 + near_count + smp_count :]
    row, smp = place_ref[0], place_ref[2]
    tok_rows, width = query_ref.shape
    head_size = width // HEADS
    piece = key_mask_ref.shape[1]
    per_block = tok_rows // piece
    for d in range(smp_count):
        bias_scr[smp ^ d] = bias_refs[d][...]
    for d in range(near_count, row_count):
        for e in range(per_block):
            far_bias_ref[(d - near_count) * per_block + e] = bias_scr[(row ^ d) * per_block + e]
    queries = dot(normed_refs[0][...], w_qkv_ref[:, :width]).astype(BF16)
    query_ref[...] = queries
    for d in range(near_count):
        kv_scr[d * tok_rows : (d + 1) * tok_rows, :] = dot(normed_refs[d][...], w_qkv_ref[:, width:]).astype(BF16)
    spans = head_spans(head_size)

    def query_of(h):
        begin, end = spans[h]
        query = queries[:, begin:end]
        return jnp.where(inside_head(h, head_size, query.shape, begin), query, jnp.zeros_like(query))

    count = near_count * per_block
    token_scores(
        query_of, kv_scr, lambda at, other, h: bias_scr[other, h], key_mask_ref, row, 0, count, per_block, spans,
        1.0 / math.sqrt(head_size), score_scr,
    )
    step = 4
    for begin in range(0, HEADS, step):
        heads = slice(begin, begin + step)
        scores = [score_scr[at, heads] for at in range(count)]
        largest = jnp.max(functools.reduce(jnp.maximum, scores), axis=-1, keepdims=True)
        largest_ref[heads] = jnp.broadcast_to(largest, largest_ref[heads].shape)
        for at in range(count):
            prob_scr[at, heads] = jnp.exp2((scores[at] - largest) * LOG2E).astype(BF16)
    mixed = Tiles(tok_rows, width)
    for h in range(HEADS):
        begin, end = spans[h]
        both = weighted_values(prob_scr, kv_scr, h, count, piece, width + begin, width + end)
        mixed.add(h, head_size, begin, both[:, : end - begin])
        total_ref[h] = both[:, end - begin :]
    mixed_ref[...] = mixed.join()


def token_kernel(near_count, row_count, *refs):
    far_count = row_count - near_count
    place_ref = refs[0]
    normed_refs = refs[1 : 1 + far_count]
    (
        query_ref, carried_ref, largest_ref, total_ref, bias_ref, state_ref, key_mask_ref, w_qkv_ref, w_proj_ref, gain_ref, ffn_in_ref,
        ffn_out_ref, spread_ref, encoded_ref, member_ref, atom_gain_ref, out_ref, joined_ref, atom_normed_ref,
        low_edge_ref, high_edge_ref, kv_scr, score_scr, prob_scr, shrink_scr,
    ) = refs[1 + far_count :]
    row = place_ref[0]
    tok_rows, width = state_ref.shape
    head_size = width // HEADS
    piece = key_mask_ref.shape[1]
    per_block = tok_rows // piece
    for d in range(far_count):
        kv_scr[d * tok_rows : (d + 1) * tok_rows, :] = dot(normed_refs[d][...], w_qkv_ref[:, width:]).astype(BF16)
    spans = head_spans(head_size)
    queries = query_ref[...]

    def query_of(h):
        begin, end = spans[h]
        query = queries[:, begin:end]
        return jnp.where(inside_head(h, head_size, query.shape, begin), query, jnp.zeros_like(query))

    count = far_count * per_block
    token_scores(
        query_of, kv_scr, lambda at, other, h: bias_ref[at, h], key_mask_ref, row, near_count, count, per_block, spans,
        1.0 / math.sqrt(head_size), score_scr,
    )
    step = 4
    for begin in range(0, HEADS, step):
        heads = slice(begin, begin + step)
        scores = [score_scr[at, heads] for at in range(count)]
        before = largest_ref[heads]
        largest = jnp.max(functools.reduce(jnp.maximum, scores), axis=-1, keepdims=True)
        largest = jnp.maximum(jnp.broadcast_to(largest, before.shape), before)
        shrink_scr[heads] = jnp.exp2((before - largest) * LOG2E)
        for at in range(count):
            prob_scr[at, heads] = jnp.exp2((scores[at] - largest[:, :, :piece]) * LOG2E).astype(BF16)
    mixed, total = Tiles(tok_rows, width), Tiles(tok_rows, width)
    for h in range(HEADS):
        begin, end = spans[h]
        both = weighted_values(prob_scr, kv_scr, h, count, piece, width + begin, width + end)
        shrink = shrink_scr[h]
        weight = both[:, end - begin :] + shrink * total_ref[h]
        for at in range(begin, end, LANES):
            part = both[:, at - begin : at - begin + LANES] + shrink * carried_ref[:, at : at + LANES]
            mixed.add(h, head_size, at, part)
            total.add(h, head_size, at, weight)
    attended = (mixed.join() / total.join()).astype(BF16)
    state = state_ref[...] + dot(attended, w_proj_ref[...])
    normed = norm_rows(state, gain_ref[1:2]).astype(BF16)
    hidden = dot(normed, ffn_in_ref[...])
    half = hidden.shape[1] // 2
    gate, up = hidden[:, :half], hidden[:, half:]
    active = (gate / (1.0 + jnp.exp(-gate)) * up).astype(BF16)
    state = state + dot(active, ffn_out_ref[...])
    result = state.astype(BF16)
    out_ref[0] = result
    spread = dot(result, spread_ref[...]).astype(BF16)
    joined = encoded_ref[...] + dot(member_ref[...], spread, TN)
    joined_ref[...] = joined
    normed = norm_rows(joined, atom_gain_ref[1:2]).astype(BF16)
    atom_normed_ref[...] = normed
    write_edges(normed, low_edge_ref, high_edge_ref)


def directions(state, level_ref, coords_ref, kicks_ref, gain_ref, coord_out_ref, direction_ref, begin):
    rows = state.shape[0]
    normed = norm_rows(state, gain_ref[...]).astype(BF16)
    update = dot(coord_out_ref[...], normed, NT)
    for k in range(coords_ref.shape[0]):
        level_hat, noisy = noisy_of(
            level_ref[...], coords_ref[k, :, begin : begin + rows], kicks_ref[k, :, begin : begin + rows]
        )
        base_square = sigma_data * sigma_data + level_hat * level_hat
        skip_scale = sigma_data * sigma_data / base_square
        out_scale = level_hat * sigma_data / jnp.sqrt(base_square)
        denoised = skip_scale * noisy + out_scale * update[k : k + 1]
        direction_ref[k, :, begin : begin + rows] = (noisy - denoised) / level_hat


def inner_kernel(
    place_ref, offsets_ref, level_ref, coords_ref, kicks_ref, state_ref, mid_ref, mask_ref, w_qkv_ref, w_out_ref, gain_ref,
    coord_out_ref, direction_ref, *scratch
):
    atoms, width = state_ref.shape
    chunks = atoms // LANES
    begin = place_ref[0] * chunks
    edge = LANES
    skip = edge - HALO
    lives = [live_bias(mask_ref, begin, False)[skip:]]
    lives += [live_bias(mask_ref, begin + chunk, False) for chunk in range(1, chunks)]
    w_qkv = w_qkv_ref[1]
    queries = dot(mid_ref[edge : atoms - edge, :], w_qkv[:, :width]).astype(BF16)
    blocks = [(b, -skip) for b in range(edge // WQ, (atoms - edge) // WQ)]
    mixed = attend(queries, blocks, [mid_ref[skip:, :]], lives, w_qkv[:, width:], offsets_ref, scratch)
    state = state_ref[edge : atoms - edge, :] + dot(mixed, w_out_ref[1])
    for k in range(direction_ref.shape[0]):
        direction_ref[k, :, 0:edge] = jnp.zeros((1, edge), F32)
        direction_ref[k, :, atoms - edge :] = jnp.zeros((1, edge), F32)
    directions(state, level_ref, coords_ref, kicks_ref, gain_ref, coord_out_ref, direction_ref, edge)


def edge_kernel(
    place_ref, offsets_ref, level_ref, coords_ref, kicks_ref, state_ref, low_ref, mid_ref, high_ref, mask_ref, w_qkv_ref,
    w_out_ref, gain_ref, coord_out_ref, inner_ref, direction_ref, *scratch
):
    row, count = place_ref[0], place_ref[1]
    first, last = row == 0, row == count - 1
    atoms, width = state_ref.shape
    chunks = atoms // LANES
    begin = row * chunks
    edge = LANES
    reach = edge + HALO
    w_qkv = w_qkv_ref[1]
    w_out = w_out_ref[1]
    for k in range(direction_ref.shape[0]):
        direction_ref[k, :, edge : atoms - edge] = inner_ref[k, :, edge : atoms - edge]
    low = jnp.where(first, jnp.zeros_like(low_ref[...]), low_ref[...])
    high = jnp.where(last, jnp.zeros_like(high_ref[...]), high_ref[...])
    lives = [
        live_bias(mask_ref, begin - 1, first)[LANES - HALO :],
        live_bias(mask_ref, begin, False),
        live_bias(mask_ref, begin + 1, False)[:HALO],
        live_bias(mask_ref, begin + chunks - 2, False)[LANES - HALO :],
        live_bias(mask_ref, begin + chunks - 1, False),
        live_bias(mask_ref, begin + chunks, last)[:HALO],
    ]
    own = jnp.concatenate([mid_ref[0:edge, :], mid_ref[atoms - edge :, :]], axis=0)
    queries = dot(own, w_qkv[:, :width]).astype(BF16)
    span = edge + 2 * HALO
    blocks = [(b, HALO) for b in range(edge // WQ)]
    blocks += [(b, span + reach - atoms) for b in range((atoms - edge) // WQ, atoms // WQ)]
    mixed = attend(
        queries, blocks, [low, mid_ref[0:reach, :], mid_ref[atoms - reach :, :], high], lives, w_qkv[:, width:], offsets_ref,
        scratch,
    )
    shift = dot(mixed, w_out)
    lower = state_ref[0:edge, :] + shift[:edge]
    upper = state_ref[atoms - edge :, :] + shift[edge:]
    directions(lower, level_ref, coords_ref, kicks_ref, gain_ref, coord_out_ref, direction_ref, 0)
    directions(upper, level_ref, coords_ref, kicks_ref, gain_ref, coord_out_ref, direction_ref, atoms - edge)


def halos_of(low_edge, high_edge):
    count = lax.axis_size("row")
    up = [(i, (i + 1) % count) for i in range(count)]
    down = [((i + 1) % count, i) for i in range(count)]
    low = lax.ppermute(high_edge, "row", up)
    high = lax.ppermute(low_edge, "row", down)
    return low, high


def spread_over(block, axis, after=None):
    count = lax.axis_size(axis)
    have = {0: block}
    bit = count // 2
    while bit:
        pairs = [(i, i ^ bit) for i in range(count)]
        for d in list(have):
            sent = have[d]
            if d and after is not None:
                sent, _ = lax.optimization_barrier((sent, after))
            have[d | bit] = lax.ppermute(sent, axis, pairs)
        bit //= 2
    return [have[d] for d in range(count)]


def per_device(
    positions,
    noise_draw,
    noise_level,
    atom_single,
    token_single,
    pair_cond,
    atom_to_token,
    window_offsets,
    atom_mask,
    token_mask,
    coord_in,
    atom_gain,
    atom_qkv,
    atom_proj,
    gather_in,
    noise_embed,
    pair_gain,
    pair_heads,
    token_gain,
    token_qkv,
    token_proj,
    ffn_in,
    ffn_out,
    scatter_out,
    out_gain,
    coord_out,
):
    row_count, smp_count = lax.axis_size("row"), lax.axis_size("smp")
    atoms, width = atom_single.shape
    tok_rows, token_width = token_single.shape
    heads = pair_heads.shape[1]
    keys = pair_cond.shape[1]
    place = jnp.stack(
        [lax.axis_index("row"), jnp.int32(row_count), lax.axis_index("smp")]
    ).astype(jnp.int32)
    level = noise_level.reshape(1, 1)
    coords = positions.transpose(1, 0, 2)
    kicks = noise_draw.transpose(1, 0, 2)
    mask = atom_mask.reshape(-1, LANES)
    tokens = atom_to_token.reshape(-1, LANES)
    smem = pl.BlockSpec(memory_space=pltpu.SMEM)
    shape = jax.ShapeDtypeStruct
    state_like = shape((atoms, width), F32)
    normed_like = shape((atoms, width), BF16)
    edge_like = shape((HALO, width), BF16)

    state, normed, low_edge, high_edge = pl.pallas_call(
        prepare_kernel,
        out_shape=(state_like, normed_like, edge_like, edge_like),
        in_specs=whole(1) + hbm(5),
        out_specs=tuple(whole(4)),
        scratch_shapes=[pltpu.VMEM(a.shape, a.dtype) for a in (coords, kicks, atom_single, coord_in, atom_gain)]
        + [pltpu.SemaphoreType.DMA((5,))],
        compiler_params=vmem(PRIVATE),
        cost_estimate=cost(1.5),
    )(level, coords, kicks, atom_single, coord_in, atom_gain)
    low, high = halos_of(low_edge, high_edge)

    pair_rows, _, channels = pair_cond.shape
    step_rows = 32
    gain_row, _ = lax.optimization_barrier((pair_gain, low_edge))
    bias = pl.pallas_call(
        functools.partial(pair_kernel, step_rows),
        out_shape=shape((heads, pair_rows, keys), BF16),
        in_specs=hbm(3),
        out_specs=whole(1)[0],
        scratch_shapes=[
            pltpu.VMEM(pair_cond.shape, BF16),
            pltpu.VMEM((1, channels), F32),
            pltpu.VMEM((heads, channels), BF16),
            pltpu.SemaphoreType.DMA((pair_rows // step_rows,)),
            pltpu.SemaphoreType.DMA((2,)),
        ],
        compiler_params=vmem(PRIVATE),
        cost_estimate=cost(5),
    )(pair_cond, gain_row.reshape(1, -1), pair_heads.T)

    encoded, token_state, token_normed, member = pl.pallas_call(
        encoder_kernel,
        out_shape=(
            state_like,
            shape((tok_rows, token_width), F32),
            shape((tok_rows, token_width), BF16),
            shape((tok_rows, atoms), BF16),
        ),
        in_specs=[smem, smem] + whole(9) + hbm(2) + whole(2),
        out_specs=tuple(whole(4)),
        scratch_shapes=[
            pltpu.VMEM(gather_in.shape, BF16),
            pltpu.VMEM(token_single.shape, BF16),
            pltpu.SemaphoreType.DMA((2,)),
        ]
        + window_scratch(atoms + 2 * HALO, atoms, width),
        compiler_params=vmem(16),
        cost_estimate=cost(3.4),
    )(
        place, window_offsets, level, state, low, normed, high, mask, tokens, atom_qkv, atom_proj, gather_in,
        token_single, noise_embed.reshape(1, -1), token_gain,
    )
    gathered = spread_over(token_normed, "row")
    biases = spread_over(bias, "smp", gathered[1 : row_count // 2 + 1])

    key_mask = token_mask.reshape(-1, keys)
    near_count = row_count - row_count // 4
    far_count = row_count - near_count
    pieces = tok_rows // keys

    def need(count):
        tile = tok_rows * max(keys, LANES)
        return (count * (keys * token_width * 4 + heads * tile * 6) + smp_count * heads * tile * 2) // 2**20 + 1

    queries, carried, largest, total, far_bias = pl.pallas_call(
        functools.partial(attend_first_kernel, near_count, row_count, smp_count),
        out_shape=(
            shape((tok_rows, token_width), BF16),
            shape((tok_rows, token_width), F32),
            shape((heads, tok_rows, LANES), F32),
            shape((heads, tok_rows, LANES), F32),
            shape((far_count * pieces, heads, tok_rows, keys), BF16),
        ),
        in_specs=[smem] + whole(near_count + smp_count + 2),
        out_specs=tuple(whole(5)),
        scratch_shapes=[
            pltpu.VMEM((near_count * tok_rows, 2 * token_width), BF16),
            pltpu.VMEM((near_count * pieces, heads, tok_rows, keys), F32),
            pltpu.VMEM((near_count * pieces, heads, tok_rows, keys), BF16),
            pltpu.VMEM((smp_count, heads, tok_rows, keys), BF16),
        ],
        compiler_params=vmem(14 + need(near_count * pieces) * 3 // 2),
        cost_estimate=cost(4),
    )(place, *gathered[:near_count], *biases, key_mask, token_qkv)
    token_result, joined, atom_normed, low_edge, high_edge = pl.pallas_call(
        functools.partial(token_kernel, near_count, row_count),
        out_shape=(
            shape((1, tok_rows, token_width), BF16),
            state_like,
            normed_like,
            edge_like,
            edge_like,
        ),
        in_specs=[smem] + whole(far_count + 16),
        out_specs=tuple(whole(5)),
        scratch_shapes=[
            pltpu.VMEM((far_count * tok_rows, 2 * token_width), BF16),
            pltpu.VMEM((far_count * pieces, heads, tok_rows, keys), F32),
            pltpu.VMEM((far_count * pieces, heads, tok_rows, keys), BF16),
            pltpu.VMEM((heads, tok_rows, LANES), F32),
        ],
        compiler_params=vmem(20 + need(far_count * pieces)),
        cost_estimate=cost(6),
    )(
        place, *gathered[near_count:], queries, carried, largest, total, far_bias, token_state, key_mask, token_qkv, token_proj,
        token_gain, ffn_in, ffn_out, scatter_out, encoded, member, atom_gain,
    )
    low, high = halos_of(low_edge, high_edge)

    edge = LANES
    direction_like = shape(coords.shape, F32)
    out_row = out_gain.reshape(1, -1)
    inner = pl.pallas_call(
        inner_kernel,
        out_shape=direction_like,
        in_specs=[smem, smem] + whole(10),
        out_specs=whole(1)[0],
        scratch_shapes=window_scratch(atoms - edge + HALO, atoms - 2 * edge, width),
        compiler_params=vmem(16),
        cost_estimate=cost(2.7),
    )(
        place, window_offsets, level, coords, kicks, joined, atom_normed, mask, atom_qkv, atom_proj, out_row, coord_out
    )
    direction = pl.pallas_call(
        edge_kernel,
        out_shape=direction_like,
        in_specs=[smem, smem] + whole(13),
        out_specs=whole(1)[0],
        scratch_shapes=window_scratch(2 * (edge + 2 * HALO), 2 * edge, width),
        compiler_params=vmem(12),
        cost_estimate=cost(2),
    )(
        place, window_offsets, level, coords, kicks, joined, low, atom_normed, high, mask, atom_qkv, atom_proj, out_row,
        coord_out, inner,
    )
    return (token_result, direction.transpose(1, 0, 2))


def solution(mesh):
    in_specs = (
        P(("grp", "smp"), None, "row"),
        P(("grp", "smp"), None, "row"),
        P(("grp", "smp")),
        P(("grp", "row"), None),
        P(("grp", "row"), None),
        P(("grp", "row"), "smp", None),
        P(("grp", "row")),
        P(("grp", "row")),
        P("grp"),
        P("grp"),
        P(),
        P(),
        P(),
        P(),
        P(),
        P(),
        P(),
        P(),
        P(),
        P(),
        P(),
        P(),
        P(),
        P(),
        P(),
        P(),
    )
    out_specs = (P(("grp", "smp"), "row", None), P(("grp", "smp"), None, "row"))
    return jax.shard_map(
        per_device, mesh=mesh, in_specs=in_specs, out_specs=out_specs, check_vma=False
    )
```

```python
import functools
import math

import jax
import jax.numpy as jnp
from jax import lax
from jax.experimental import pallas as pl
from jax.experimental.pallas import tpu as pltpu
from jax.sharding import PartitionSpec as P

HEADS = 16
AHEADS = 4
WQ = 32
WK = 128
HALO = 96
LANES = 128
PRIVATE = 62

sigma_data = 16.0
gamma_boost = 0.8
norm_eps = 1e-05
masked_score = -1e30
LOG2E = math.log2(math.e)
F32 = jnp.float32
BF16 = jnp.bfloat16
NT = (((1,), (1,)), ((), ()))
TN = (((0,), (0,)), ((), ()))


def vmem(mib):
    return pltpu.CompilerParams(vmem_limit_bytes=mib * 1024 * 1024)


def cost(micros):
    return pl.CostEstimate(flops=int(micros * 1e9), transcendentals=0, bytes_accessed=int(micros * 3e6))


def hbm(count):
    return [pl.BlockSpec(memory_space=pltpu.HBM)] * count


def fetch(sources, targets, sems):
    copies = [pltpu.make_async_copy(a, b, sems.at[i]) for i, (a, b) in enumerate(zip(sources, targets))]
    for copy in copies:
        copy.start()
    return copies


def whole(count):
    return [pl.BlockSpec(memory_space=pltpu.VMEM)] * count


def dot(a, b, dims=(((1,), (0,)), ((), ()))):
    return lax.dot_general(a, b, dims, preferred_element_type=F32)


def norm_rows(values, gain):
    average = jnp.mean(values, axis=-1, keepdims=True)
    centred = values - average
    variance = jnp.mean(centred * centred, axis=-1, keepdims=True)
    return centred * lax.rsqrt(variance + norm_eps) * gain


def noisy_of(level, coords, kicks):
    level_hat = (1.0 + gamma_boost) * level
    noisy = coords + jnp.sqrt(level_hat * level_hat - level * level) * kicks
    return level_hat, noisy


def column_of(row):
    size = row.shape[1]
    down = lax.broadcasted_iota(jnp.int32, (size, size), 0)
    across = lax.broadcasted_iota(jnp.int32, (size, size), 1)
    spread = jnp.where(down == across, jnp.broadcast_to(row, (size, size)), 0.0)
    return dot(spread.astype(BF16), jnp.ones((size, LANES), BF16))


def rows_of(ref):
    return jnp.concatenate([ref[k] for k in range(ref.shape[0])], axis=0)


def write_edges(normed, row, first_edge_ref, second_edge_ref):
    even = row % 2 == 0
    low, high = normed[:HALO], normed[normed.shape[0] - HALO :]
    first_edge_ref[...] = jnp.where(even, high, low)
    second_edge_ref[...] = jnp.where(even, low, high)


def halo_rows(row, count, first_ref, second_ref):
    even = row % 2 == 0
    low = jnp.where(even, second_ref[...], first_ref[...])
    high = jnp.where(even, first_ref[...], second_ref[...])
    low = jnp.where(row == 0, jnp.zeros_like(low), low)
    high = jnp.where(row == count - 1, jnp.zeros_like(high), high)
    return low, high


def prepare_kernel(
    level_hbm, coords_hbm, kicks_hbm, single_hbm, coord_in_hbm, gain_hbm, state_ref, normed_ref, second_edge_ref, first_edge_ref,
    level_ref, coords_ref, kicks_ref, single_ref, coord_in_ref, gain_ref, sems
):
    copies = fetch(
        [level_hbm, coords_hbm, kicks_hbm, single_hbm, coord_in_hbm, gain_hbm],
        [level_ref, coords_ref, kicks_ref, single_ref, coord_in_ref, gain_ref], sems,
    )
    for copy in copies:
        copy.wait()
    level_hat, noisy = noisy_of(level_ref[...], rows_of(coords_ref), rows_of(kicks_ref))
    scaled = noisy / jnp.sqrt(level_hat * level_hat + sigma_data * sigma_data)
    embedded = lax.dot_general(
        scaled, coord_in_ref[...], TN, precision=lax.Precision.HIGHEST, preferred_element_type=F32
    )
    state = single_ref[...].astype(F32) + embedded
    state_ref[...] = state
    normed = norm_rows(state, gain_ref[0:1]).astype(BF16)
    normed_ref[...] = normed
    write_edges(normed, lax.axis_index("row"), first_edge_ref, second_edge_ref)


def pair_kernel(step_rows, tile_hbm, gain_hbm, heads_hbm, bias_ref, tile_ref, gain_ref, heads_ref, tile_sems, sems):
    keys, channels = tile_ref.shape[1:]
    head_count = heads_ref.shape[0]
    steps = tile_ref.shape[0] // step_rows
    small = fetch([gain_hbm, heads_hbm], [gain_ref, heads_ref], sems)
    spans = [pl.ds(step * step_rows, step_rows) for step in range(steps)]
    tiles = fetch([tile_hbm.at[span] for span in spans], [tile_ref.at[span] for span in spans], tile_sems)
    for copy in small:
        copy.wait()
    weights = heads_ref[...].astype(F32) * gain_ref[...]
    high = weights.astype(BF16)
    low = (weights - high.astype(F32)).astype(BF16)
    total = jnp.sum(high.astype(F32) + low.astype(F32), axis=1, keepdims=True)
    left = jnp.concatenate([high, low], axis=0)
    for step in range(steps):
        tiles[step].wait()
        begin = step * step_rows
        tile = tile_ref[begin : begin + step_rows].reshape(step_rows * keys, channels).T
        wide = tile.astype(F32)
        average = jnp.mean(wide, axis=0, keepdims=True)
        centred = wide - average
        variance = jnp.mean(centred * centred, axis=0, keepdims=True)
        sums = dot(left, tile)
        raw = sums[:head_count] + sums[head_count:]
        result = (raw - average * total) * lax.rsqrt(variance + norm_eps)
        pieces = [result[:, i * keys : (i + 1) * keys] for i in range(step_rows)]
        bias_ref[:, begin : begin + step_rows, :] = jnp.swapaxes(jnp.stack(pieces, axis=0), 0, 1).astype(BF16)


def live_bias(mask_ref, chunk, outside):
    final = mask_ref.shape[0] - 1
    row = mask_ref[pl.ds(jnp.clip(chunk, 0, final), 1), :].astype(F32)
    column = column_of(row)
    column = jnp.where(outside, 0.0, column)
    return (column - 1.0) * -masked_score


def attend(queries, blocks, parts, lives, w_kv, offsets_ref, scratch):
    key_scr, value_scr, live_scr, score_scr, prob_scr, out_scr = scratch
    offsets = offsets_ref[...]
    row_count, width = queries.shape
    block_count = len(blocks)
    head_size = width // AHEADS
    at = 0
    for part in parts:
        projected = dot(part, w_kv).astype(BF16).astype(F32)
        key_scr[at : at + part.shape[0], :] = projected[:, :width]
        value_scr[at : at + part.shape[0], :] = projected[:, width:]
        at += part.shape[0]
    at = 0
    for live in lives:
        live_scr[at : at + live.shape[0], :] = live
        at += live.shape[0]

    stacked_rows = AHEADS * WQ
    lane = lax.broadcasted_iota(jnp.int32, (stacked_rows, width), 1)
    line = lax.broadcasted_iota(jnp.int32, (stacked_rows, width), 0)
    own_head = lane // head_size == line // WQ
    pick = jnp.where(lane == 0, 1.0, 0.0).astype(BF16)
    ones = jnp.ones((WK, width), BF16)
    begins = []
    for b, (block, shift) in enumerate(blocks):
        begin = block * WQ + shift + offsets[0, block]
        begins.append(begin)
        keys = key_scr[pl.ds(begin, WK), :].astype(BF16)
        live = live_scr[pl.ds(begin, WK), :].astype(BF16)
        query = queries[b * WQ : (b + 1) * WQ]
        query = jnp.concatenate([query] * AHEADS, axis=0)
        query = jnp.where(own_head, query, jnp.zeros_like(query))
        score_scr[b * stacked_rows : (b + 1) * stacked_rows, :] = dot(
            jnp.concatenate([query, pick], axis=1), jnp.concatenate([keys, live], axis=1), NT
        )
    factor = LOG2E / math.sqrt(head_size)
    step = 4 * stacked_rows
    for begin in range(0, block_count * stacked_rows, step):
        scores = score_scr[begin : begin + step, :]
        largest = jnp.max(scores, axis=-1, keepdims=True)
        prob_scr[begin : begin + step, :] = jnp.exp2((scores - largest) * factor).astype(BF16)
    for b in range(block_count):
        values = value_scr[pl.ds(begins[b], WK), :].astype(BF16)
        probs = prob_scr[b * stacked_rows : (b + 1) * stacked_rows, :]
        both = dot(probs, jnp.concatenate([values, ones], axis=1))
        mixed = jnp.where(own_head, both[:, :width], 0.0)
        weight = jnp.where(own_head, both[:, width:], 0.0)
        mixed = sum(mixed[h * WQ : (h + 1) * WQ] for h in range(AHEADS))
        weight = sum(weight[h * WQ : (h + 1) * WQ] for h in range(AHEADS))
        out_scr[b * WQ : (b + 1) * WQ, :] = (mixed / weight).astype(BF16)
    return out_scr[0:row_count, :]


def window_scratch(extended, row_count, width):
    scores = row_count * AHEADS
    return [
        pltpu.VMEM((extended, width), F32),
        pltpu.VMEM((extended, width), F32),
        pltpu.VMEM((extended, LANES), F32),
        pltpu.VMEM((scores, WK), F32),
        pltpu.VMEM((scores, WK), BF16),
        pltpu.VMEM((row_count, width), BF16),
    ]


def member_of(token_ref, mask_ref, first_chunk, base, tok_rows):
    chunk_count = token_ref.shape[0]
    tokens = lax.broadcasted_iota(jnp.int32, (tok_rows, LANES), 0)
    pieces = []
    for chunk in range(chunk_count):
        local = token_ref[chunk : chunk + 1, :] - base
        valid = mask_ref[pl.ds(first_chunk + chunk, 1), :]
        local = jnp.where(valid > 0, local, -1)
        pieces.append(jnp.where(local == tokens, 1.0, 0.0).astype(BF16))
    return jnp.concatenate(pieces, axis=1)


def encoder_kernel(
    offsets_ref, level_ref, state_ref, low_ref, mid_ref, high_ref, mask_ref, token_ref, w_qkv_ref, w_out_ref,
    lift_ref, single_ref, embed_ref, gain_ref, encoded_ref, token_state_ref, normed_ref, member_ref, *scratch
):
    row, count = lax.axis_index("row"), lax.axis_size("row")
    first, last = row == 0, row == count - 1
    tok_rows = single_ref.shape[0]
    chunks = token_ref.shape[0]
    width = state_ref.shape[1]
    begin = row * chunks
    low, high = halo_rows(row, count, low_ref, high_ref)
    mid = mid_ref[...]
    lives = [live_bias(mask_ref, begin - 1, first)[LANES - HALO :]]
    lives += [live_bias(mask_ref, begin + chunk, False) for chunk in range(chunks)]
    lives += [live_bias(mask_ref, begin + chunks, last)[:HALO]]
    w_qkv = w_qkv_ref[0]
    queries = dot(mid, w_qkv[:, :width]).astype(BF16)
    mixed = attend(
        queries, [(b, HALO) for b in range(mid.shape[0] // WQ)], [low, mid, high], lives, w_qkv[:, width:], offsets_ref, scratch
    )
    state = state_ref[...] + dot(mixed, w_out_ref[0])
    encoded_ref[...] = state
    lifted = jnp.maximum(dot(state.astype(BF16), lift_ref[...]), 0.0).astype(BF16)
    member = member_of(token_ref, mask_ref, begin, row * tok_rows, tok_rows)
    member_ref[...] = member
    counts = jnp.maximum(dot(member, jnp.ones((member.shape[1], LANES), BF16)), 1.0)
    pooled = dot(member, lifted) / counts[:, 0:1]
    level_hat = (1.0 + gamma_boost) * level_ref[...]
    token_state = (
        pooled + single_ref[...].astype(F32) + jnp.log(level_hat / sigma_data) / 4.0 * embed_ref[...]
    )
    token_state_ref[...] = token_state
    normed_ref[...] = norm_rows(token_state, gain_ref[0:1]).astype(BF16)


def head_spans(head_size):
    spans = []
    for h in range(HEADS):
        begin = h * head_size // LANES * LANES
        end = -(-(h + 1) * head_size // LANES) * LANES
        spans.append((begin, end))
    return spans


def inside_head(h, head_size, shape, begin):
    lane = lax.broadcasted_iota(jnp.int32, shape, 1) + begin
    return (lane >= h * head_size) & (lane < (h + 1) * head_size)


class Tiles:
    def __init__(self, rows, width):
        self.rows = rows
        self.tiles = [None] * (width // LANES)

    def add(self, h, head_size, begin, values):
        for at in range(0, values.shape[1], LANES):
            tile = (begin + at) // LANES
            inside = inside_head(h, head_size, (self.rows, LANES), begin + at)
            kept = self.tiles[tile]
            part = values[:, at : at + LANES]
            self.tiles[tile] = jnp.where(inside, part, 0.0 if kept is None else kept)

    def join(self):
        return jnp.concatenate(self.tiles, axis=1)


def weighted_values(prob_scr, kv_scr, h, count, piece, begin, end):
    ones = jnp.ones((piece, LANES), BF16)
    return functools.reduce(
        jnp.add,
        [
            dot(prob_scr[at, h], jnp.concatenate([kv_scr[at * piece : (at + 1) * piece, begin:end], ones], axis=1))
            for at in range(count)
        ],
    )


def token_scores(query_of, kv_scr, bias_of, key_mask_ref, row, near, count, per_block, spans, scale, score_scr):
    piece = key_mask_ref.shape[1]

    def one(at):
        other = (row ^ (near + at // per_block)) * per_block + at % per_block
        live = key_mask_ref[pl.ds(other, 1), :] > 0
        rows = pl.ds(at * piece if isinstance(at, int) else pl.multiple_of(at * piece, piece), piece)
        for h in range(HEADS):
            begin, end = spans[h]
            scores = dot(query_of(h), kv_scr[rows, begin:end], NT) * scale
            scores = scores + bias_of(at, other, h).astype(F32)
            score_scr[at, h] = jnp.where(live, scores, masked_score)

    if count <= 4:
        for at in range(count):
            one(at)
    else:
        lax.fori_loop(0, count, lambda at, carry: (one(at), carry)[1], 0)


def attend_first_kernel(near_count, row_count, smp_count, *refs):
    normed_refs = refs[:near_count]
    bias_refs = refs[near_count : near_count + smp_count]
    (
        key_mask_ref, w_qkv_ref, query_ref, mixed_ref, largest_ref, total_ref, far_bias_ref, kv_scr, score_scr, prob_scr,
        bias_scr,
    ) = refs[near_count + smp_count :]
    row, smp = lax.axis_index("row"), lax.axis_index("smp")
    tok_rows, width = query_ref.shape
    head_size = width // HEADS
    piece = key_mask_ref.shape[1]
    per_block = tok_rows // piece
    for d in range(smp_count):
        bias_scr[smp ^ d] = bias_refs[d][...]
    for d in range(near_count, row_count):
        for e in range(per_block):
            far_bias_ref[(d - near_count) * per_block + e] = bias_scr[(row ^ d) * per_block + e]
    queries = dot(normed_refs[0][...], w_qkv_ref[:, :width]).astype(BF16)
    query_ref[...] = queries
    for d in range(near_count):
        kv_scr[d * tok_rows : (d + 1) * tok_rows, :] = dot(normed_refs[d][...], w_qkv_ref[:, width:]).astype(BF16)
    spans = head_spans(head_size)

    def query_of(h):
        begin, end = spans[h]
        query = queries[:, begin:end]
        return jnp.where(inside_head(h, head_size, query.shape, begin), query, jnp.zeros_like(query))

    count = near_count * per_block
    token_scores(
        query_of, kv_scr, lambda at, other, h: bias_scr[other, h], key_mask_ref, row, 0, count, per_block, spans,
        1.0 / math.sqrt(head_size), score_scr,
    )
    step = 4
    for begin in range(0, HEADS, step):
        heads = slice(begin, begin + step)
        scores = [score_scr[at, heads] for at in range(count)]
        largest = jnp.max(functools.reduce(jnp.maximum, scores), axis=-1, keepdims=True)
        largest_ref[heads] = jnp.broadcast_to(largest, largest_ref[heads].shape)
        for at in range(count):
            prob_scr[at, heads] = jnp.exp2((scores[at] - largest) * LOG2E).astype(BF16)
    mixed = Tiles(tok_rows, width)
    for h in range(HEADS):
        begin, end = spans[h]
        both = weighted_values(prob_scr, kv_scr, h, count, piece, width + begin, width + end)
        mixed.add(h, head_size, begin, both[:, : end - begin])
        total_ref[h] = both[:, end - begin :]
    mixed_ref[...] = mixed.join()


def token_kernel(near_count, row_count, *refs):
    far_count = row_count - near_count
    normed_refs = refs[:far_count]
    (
        query_ref, carried_ref, largest_ref, total_ref, bias_ref, state_ref, key_mask_ref, w_qkv_ref, w_proj_ref, gain_ref, ffn_in_ref,
        ffn_out_ref, spread_ref, encoded_ref, member_ref, atom_gain_ref, out_ref, joined_ref, atom_normed_ref,
        second_edge_ref, first_edge_ref, kv_scr, score_scr, prob_scr, shrink_scr,
    ) = refs[far_count:]
    row = lax.axis_index("row")
    tok_rows, width = state_ref.shape
    head_size = width // HEADS
    piece = key_mask_ref.shape[1]
    per_block = tok_rows // piece
    for d in range(far_count):
        kv_scr[d * tok_rows : (d + 1) * tok_rows, :] = dot(normed_refs[d][...], w_qkv_ref[:, width:]).astype(BF16)
    spans = head_spans(head_size)
    queries = query_ref[...]

    def query_of(h):
        begin, end = spans[h]
        query = queries[:, begin:end]
        return jnp.where(inside_head(h, head_size, query.shape, begin), query, jnp.zeros_like(query))

    count = far_count * per_block
    token_scores(
        query_of, kv_scr, lambda at, other, h: bias_ref[at, h], key_mask_ref, row, near_count, count, per_block, spans,
        1.0 / math.sqrt(head_size), score_scr,
    )
    step = 4
    for begin in range(0, HEADS, step):
        heads = slice(begin, begin + step)
        scores = [score_scr[at, heads] for at in range(count)]
        before = largest_ref[heads]
        largest = jnp.max(functools.reduce(jnp.maximum, scores), axis=-1, keepdims=True)
        largest = jnp.maximum(jnp.broadcast_to(largest, before.shape), before)
        shrink_scr[heads] = jnp.exp2((before - largest) * LOG2E)
        for at in range(count):
            prob_scr[at, heads] = jnp.exp2((scores[at] - largest[:, :, :piece]) * LOG2E).astype(BF16)
    mixed, total = Tiles(tok_rows, width), Tiles(tok_rows, width)
    for h in range(HEADS):
        begin, end = spans[h]
        both = weighted_values(prob_scr, kv_scr, h, count, piece, width + begin, width + end)
        shrink = shrink_scr[h]
        weight = both[:, end - begin :] + shrink * total_ref[h]
        for at in range(begin, end, LANES):
            part = both[:, at - begin : at - begin + LANES] + shrink * carried_ref[:, at : at + LANES]
            mixed.add(h, head_size, at, part)
            total.add(h, head_size, at, weight)
    attended = (mixed.join() / total.join()).astype(BF16)
    state = state_ref[...] + dot(attended, w_proj_ref[...])
    normed = norm_rows(state, gain_ref[1:2]).astype(BF16)
    hidden = dot(normed, ffn_in_ref[...])
    half = hidden.shape[1] // 2
    gate, up = hidden[:, :half], hidden[:, half:]
    active = (gate / (1.0 + jnp.exp(-gate)) * up).astype(BF16)
    state = state + dot(active, ffn_out_ref[...])
    result = state.astype(BF16)
    out_ref[0] = result
    spread = dot(result, spread_ref[...]).astype(BF16)
    joined = encoded_ref[...] + dot(member_ref[...], spread, TN)
    joined_ref[...] = joined
    normed = norm_rows(joined, atom_gain_ref[1:2]).astype(BF16)
    atom_normed_ref[...] = normed
    write_edges(normed, row, first_edge_ref, second_edge_ref)


def directions(state, level_ref, coords_ref, kicks_ref, gain_ref, coord_out_ref, direction_ref, begin):
    rows = state.shape[0]
    normed = norm_rows(state, gain_ref[...]).astype(BF16)
    update = dot(coord_out_ref[...], normed, NT)
    for k in range(coords_ref.shape[0]):
        level_hat, noisy = noisy_of(
            level_ref[...], coords_ref[k, :, begin : begin + rows], kicks_ref[k, :, begin : begin + rows]
        )
        base_square = sigma_data * sigma_data + level_hat * level_hat
        skip_scale = sigma_data * sigma_data / base_square
        out_scale = level_hat * sigma_data / jnp.sqrt(base_square)
        denoised = skip_scale * noisy + out_scale * update[k : k + 1]
        direction_ref[k, :, begin : begin + rows] = (noisy - denoised) / level_hat


def inner_kernel(
    offsets_ref, level_ref, coords_ref, kicks_ref, state_ref, mid_ref, mask_ref, w_qkv_ref, w_out_ref, gain_ref,
    coord_out_ref, direction_ref, *scratch
):
    atoms, width = state_ref.shape
    chunks = atoms // LANES
    begin = lax.axis_index("row") * chunks
    edge = LANES
    skip = edge - HALO
    lives = [live_bias(mask_ref, begin, False)[skip:]]
    lives += [live_bias(mask_ref, begin + chunk, False) for chunk in range(1, chunks)]
    w_qkv = w_qkv_ref[1]
    queries = dot(mid_ref[edge : atoms - edge, :], w_qkv[:, :width]).astype(BF16)
    blocks = [(b, -skip) for b in range(edge // WQ, (atoms - edge) // WQ)]
    mixed = attend(queries, blocks, [mid_ref[skip:, :]], lives, w_qkv[:, width:], offsets_ref, scratch)
    state = state_ref[edge : atoms - edge, :] + dot(mixed, w_out_ref[1])
    for k in range(direction_ref.shape[0]):
        direction_ref[k, :, 0:edge] = jnp.zeros((1, edge), F32)
        direction_ref[k, :, atoms - edge :] = jnp.zeros((1, edge), F32)
    directions(state, level_ref, coords_ref, kicks_ref, gain_ref, coord_out_ref, direction_ref, edge)


def edge_kernel(
    offsets_ref, level_ref, coords_ref, kicks_ref, state_ref, low_ref, mid_ref, high_ref, mask_ref, w_qkv_ref,
    w_out_ref, gain_ref, coord_out_ref, inner_ref, direction_ref, *scratch
):
    row, count = lax.axis_index("row"), lax.axis_size("row")
    first, last = row == 0, row == count - 1
    atoms, width = state_ref.shape
    chunks = atoms // LANES
    begin = row * chunks
    edge = LANES
    reach = edge + HALO
    w_qkv = w_qkv_ref[1]
    w_out = w_out_ref[1]
    for k in range(direction_ref.shape[0]):
        direction_ref[k, :, edge : atoms - edge] = inner_ref[k, :, edge : atoms - edge]
    low, high = halo_rows(row, count, low_ref, high_ref)
    lives = [
        live_bias(mask_ref, begin - 1, first)[LANES - HALO :],
        live_bias(mask_ref, begin, False),
        live_bias(mask_ref, begin + 1, False)[:HALO],
        live_bias(mask_ref, begin + chunks - 2, False)[LANES - HALO :],
        live_bias(mask_ref, begin + chunks - 1, False),
        live_bias(mask_ref, begin + chunks, last)[:HALO],
    ]
    own = jnp.concatenate([mid_ref[0:edge, :], mid_ref[atoms - edge :, :]], axis=0)
    queries = dot(own, w_qkv[:, :width]).astype(BF16)
    span = edge + 2 * HALO
    blocks = [(b, HALO) for b in range(edge // WQ)]
    blocks += [(b, span + reach - atoms) for b in range((atoms - edge) // WQ, atoms // WQ)]
    mixed = attend(
        queries, blocks, [low, mid_ref[0:reach, :], mid_ref[atoms - reach :, :], high], lives, w_qkv[:, width:], offsets_ref,
        scratch,
    )
    shift = dot(mixed, w_out)
    lower = state_ref[0:edge, :] + shift[:edge]
    upper = state_ref[atoms - edge :, :] + shift[edge:]
    directions(lower, level_ref, coords_ref, kicks_ref, gain_ref, coord_out_ref, direction_ref, 0)
    directions(upper, level_ref, coords_ref, kicks_ref, gain_ref, coord_out_ref, direction_ref, atoms - edge)


def halos_of(first_edge, second_edge):
    count = lax.axis_size("row")
    second = [(0, 0), (count - 1, count - 1)]
    second += [(i, i + 1 if i % 2 else i - 1) for i in range(1, count - 1)]
    from_second = lax.ppermute(second_edge, "row", second)
    return lax.ppermute(first_edge, "row", [(i, i ^ 1) for i in range(count)]), from_second


def spread_over(block, axis, after=None):
    count = lax.axis_size(axis)
    have = {0: block}
    bit = count // 2
    while bit:
        pairs = [(i, i ^ bit) for i in range(count)]
        for d in list(have):
            sent = have[d]
            if d and after is not None:
                sent, _ = lax.optimization_barrier((sent, after))
            have[d | bit] = lax.ppermute(sent, axis, pairs)
        bit //= 2
    return [have[d] for d in range(count)]


def per_device(
    positions,
    noise_draw,
    noise_level,
    atom_single,
    token_single,
    pair_cond,
    atom_to_token,
    window_offsets,
    atom_mask,
    token_mask,
    coord_in,
    atom_gain,
    atom_qkv,
    atom_proj,
    gather_in,
    noise_embed,
    pair_gain,
    pair_heads,
    token_gain,
    token_qkv,
    token_proj,
    ffn_in,
    ffn_out,
    scatter_out,
    out_gain,
    coord_out,
):
    row_count, smp_count = lax.axis_size("row"), lax.axis_size("smp")
    atoms, width = atom_single.shape
    tok_rows, token_width = token_single.shape
    heads = pair_heads.shape[1]
    keys = pair_cond.shape[1]
    level = noise_level.reshape(1, 1)
    coords = positions.transpose(1, 0, 2)
    kicks = noise_draw.transpose(1, 0, 2)
    mask = atom_mask.reshape(-1, LANES)
    tokens = atom_to_token.reshape(-1, LANES)
    shape = jax.ShapeDtypeStruct
    state_like = shape((atoms, width), F32)
    normed_like = shape((atoms, width), BF16)
    edge_like = shape((HALO, width), BF16)

    state, normed, second_edge, first_edge = pl.pallas_call(
        prepare_kernel,
        out_shape=(state_like, normed_like, edge_like, edge_like),
        in_specs=hbm(6),
        out_specs=tuple(whole(4)),
        scratch_shapes=[pltpu.VMEM(a.shape, a.dtype) for a in (level, coords, kicks, atom_single, coord_in, atom_gain)]
        + [pltpu.SemaphoreType.DMA((6,))],
        compiler_params=vmem(PRIVATE),
        cost_estimate=cost(1.5),
    )(level, coords, kicks, atom_single, coord_in, atom_gain)
    low, high = halos_of(first_edge, second_edge)

    pair_rows, _, channels = pair_cond.shape
    step_rows = 32
    gain_row, _ = lax.optimization_barrier((pair_gain, second_edge))
    bias = pl.pallas_call(
        functools.partial(pair_kernel, step_rows),
        out_shape=shape((heads, pair_rows, keys), BF16),
        in_specs=hbm(3),
        out_specs=whole(1)[0],
        scratch_shapes=[
            pltpu.VMEM(pair_cond.shape, BF16),
            pltpu.VMEM((1, channels), F32),
            pltpu.VMEM((heads, channels), BF16),
            pltpu.SemaphoreType.DMA((pair_rows // step_rows,)),
            pltpu.SemaphoreType.DMA((2,)),
        ],
        compiler_params=vmem(PRIVATE),
        cost_estimate=cost(5),
    )(pair_cond, gain_row.reshape(1, -1), pair_heads.T)

    encoded, token_state, token_normed, member = pl.pallas_call(
        encoder_kernel,
        out_shape=(
            state_like,
            shape((tok_rows, token_width), F32),
            shape((tok_rows, token_width), BF16),
            shape((tok_rows, atoms), BF16),
        ),
        in_specs=whole(1) + whole(13),
        out_specs=tuple(whole(4)),
        scratch_shapes=window_scratch(atoms + 2 * HALO, atoms, width),
        compiler_params=vmem(16),
        cost_estimate=cost(3.4),
    )(
        window_offsets.reshape(1, -1), level, state, low, normed, high, mask, tokens, atom_qkv, atom_proj, gather_in,
        token_single, noise_embed.reshape(1, -1), token_gain,
    )
    gathered = spread_over(token_normed, "row")
    biases = spread_over(bias, "smp", gathered[1 : row_count // 2 + 1])

    key_mask = token_mask.reshape(-1, keys)
    near_count = row_count - row_count // 4
    far_count = row_count - near_count
    pieces = tok_rows // keys

    def need(count):
        tile = tok_rows * max(keys, LANES)
        return (count * (keys * token_width * 4 + heads * tile * 6) + smp_count * heads * tile * 2) // 2**20 + 1

    queries, carried, largest, total, far_bias = pl.pallas_call(
        functools.partial(attend_first_kernel, near_count, row_count, smp_count),
        out_shape=(
            shape((tok_rows, token_width), BF16),
            shape((tok_rows, token_width), F32),
            shape((heads, tok_rows, LANES), F32),
            shape((heads, tok_rows, LANES), F32),
            shape((far_count * pieces, heads, tok_rows, keys), BF16),
        ),
        in_specs=whole(near_count + smp_count + 2),
        out_specs=tuple(whole(5)),
        scratch_shapes=[
            pltpu.VMEM((near_count * tok_rows, 2 * token_width), BF16),
            pltpu.VMEM((near_count * pieces, heads, tok_rows, keys), F32),
            pltpu.VMEM((near_count * pieces, heads, tok_rows, keys), BF16),
            pltpu.VMEM((smp_count, heads, tok_rows, keys), BF16),
        ],
        compiler_params=vmem(14 + need(near_count * pieces) * 3 // 2),
        cost_estimate=cost(4),
    )(*gathered[:near_count], *biases, key_mask, token_qkv)
    token_result, joined, atom_normed, second_edge, first_edge = pl.pallas_call(
        functools.partial(token_kernel, near_count, row_count),
        out_shape=(
            shape((1, tok_rows, token_width), BF16),
            state_like,
            normed_like,
            edge_like,
            edge_like,
        ),
        in_specs=whole(far_count + 16),
        out_specs=tuple(whole(5)),
        scratch_shapes=[
            pltpu.VMEM((far_count * tok_rows, 2 * token_width), BF16),
            pltpu.VMEM((far_count * pieces, heads, tok_rows, keys), F32),
            pltpu.VMEM((far_count * pieces, heads, tok_rows, keys), BF16),
            pltpu.VMEM((heads, tok_rows, LANES), F32),
        ],
        compiler_params=vmem(20 + need(far_count * pieces)),
        cost_estimate=cost(6),
    )(
        *gathered[near_count:], queries, carried, largest, total, far_bias, token_state, key_mask, token_qkv, token_proj,
        token_gain, ffn_in, ffn_out, scatter_out, encoded, member, atom_gain,
    )
    low, high = halos_of(first_edge, second_edge)

    edge = LANES
    direction_like = shape(coords.shape, F32)
    out_row = out_gain.reshape(1, -1)
    inner = pl.pallas_call(
        inner_kernel,
        out_shape=direction_like,
        in_specs=whole(1) + whole(10),
        out_specs=whole(1)[0],
        scratch_shapes=window_scratch(atoms - edge + HALO, atoms - 2 * edge, width),
        compiler_params=vmem(16),
        cost_estimate=cost(2.7),
    )(
        window_offsets.reshape(1, -1), level, coords, kicks, joined, atom_normed, mask, atom_qkv, atom_proj, out_row, coord_out
    )
    direction = pl.pallas_call(
        edge_kernel,
        out_shape=direction_like,
        in_specs=whole(1) + whole(13),
        out_specs=whole(1)[0],
        scratch_shapes=window_scratch(2 * (edge + 2 * HALO), 2 * edge, width),
        compiler_params=vmem(12),
        cost_estimate=cost(2),
    )(
        window_offsets.reshape(1, -1), level, coords, kicks, joined, low, atom_normed, high, mask, atom_qkv, atom_proj, out_row,
        coord_out, inner,
    )
    return (token_result, direction.transpose(1, 0, 2))


def solution(mesh):
    in_specs = (
        P(("grp", "smp"), None, "row"),
        P(("grp", "smp"), None, "row"),
        P(("grp", "smp")),
        P(("grp", "row"), None),
        P(("grp", "row"), None),
        P(("grp", "row"), "smp", None),
        P(("grp", "row")),
        P(("grp", "row")),
        P("grp"),
        P("grp"),
        P(),
        P(),
        P(),
        P(),
        P(),
        P(),
        P(),
        P(),
        P(),
        P(),
        P(),
        P(),
        P(),
        P(),
        P(),
        P(),
    )
    out_specs = (P(("grp", "smp"), "row", None), P(("grp", "smp"), None, "row"))
    return jax.shard_map(
        per_device, mesh=mesh, in_specs=in_specs, out_specs=out_specs, check_vma=False
    )
```

```python
import functools
import math

import jax
import jax.numpy as jnp
from jax import lax
from jax.experimental import pallas as pl
from jax.experimental.pallas import tpu as pltpu
from jax.sharding import PartitionSpec as P

HEADS = 16
AHEADS = 4
WQ = 32
WK = 128
HALO = 96
LANES = 128
PRIVATE = 62

sigma_data = 16.0
gamma_boost = 0.8
norm_eps = 1e-05
masked_score = -1e30
LOG2E = math.log2(math.e)
F32 = jnp.float32
BF16 = jnp.bfloat16
NT = (((1,), (1,)), ((), ()))
TN = (((0,), (0,)), ((), ()))


def vmem(mib):
    return pltpu.CompilerParams(vmem_limit_bytes=mib * 1024 * 1024)


def cost(micros):
    return pl.CostEstimate(flops=int(micros * 1e9), transcendentals=0, bytes_accessed=int(micros * 3e6))


def hbm(count):
    return [pl.BlockSpec(memory_space=pltpu.HBM)] * count


def fetch(sources, targets, sems):
    copies = [pltpu.make_async_copy(a, b, sems.at[i]) for i, (a, b) in enumerate(zip(sources, targets))]
    for copy in copies:
        copy.start()
    return copies


def whole(count):
    return [pl.BlockSpec(memory_space=pltpu.VMEM)] * count


def dot(a, b, dims=(((1,), (0,)), ((), ()))):
    return lax.dot_general(a, b, dims, preferred_element_type=F32)


def norm_rows(values, gain):
    average = jnp.mean(values, axis=-1, keepdims=True)
    centred = values - average
    variance = jnp.mean(centred * centred, axis=-1, keepdims=True)
    return centred * lax.rsqrt(variance + norm_eps) * gain


def noisy_of(level, coords, kicks):
    level_hat = (1.0 + gamma_boost) * level
    noisy = coords + jnp.sqrt(level_hat * level_hat - level * level) * kicks
    return level_hat, noisy


def column_of(row):
    size = row.shape[1]
    down = lax.broadcasted_iota(jnp.int32, (size, size), 0)
    across = lax.broadcasted_iota(jnp.int32, (size, size), 1)
    spread = jnp.where(down == across, jnp.broadcast_to(row, (size, size)), 0.0)
    return dot(spread.astype(BF16), jnp.ones((size, LANES), BF16))


def rows_of(ref):
    return jnp.concatenate([ref[k] for k in range(ref.shape[0])], axis=0)


def write_edges(normed, row, first_edge_ref, second_edge_ref):
    even = row % 2 == 0
    low, high = normed[:HALO], normed[normed.shape[0] - HALO :]
    first_edge_ref[...] = jnp.where(even, high, low)
    second_edge_ref[...] = jnp.where(even, low, high)


def halo_rows(row, count, first_ref, second_ref):
    even = row % 2 == 0
    low = jnp.where(even, second_ref[...], first_ref[...])
    high = jnp.where(even, first_ref[...], second_ref[...])
    low = jnp.where(row == 0, jnp.zeros_like(low), low)
    high = jnp.where(row == count - 1, jnp.zeros_like(high), high)
    return low, high


def prepare_kernel(
    level_hbm, coords_hbm, kicks_hbm, single_hbm, coord_in_hbm, gain_hbm, state_ref, normed_ref, second_edge_ref, first_edge_ref,
    level_ref, coords_ref, kicks_ref, single_ref, coord_in_ref, gain_ref, sems
):
    copies = fetch(
        [level_hbm, coords_hbm, kicks_hbm, single_hbm, coord_in_hbm, gain_hbm],
        [level_ref, coords_ref, kicks_ref, single_ref, coord_in_ref, gain_ref], sems,
    )
    for copy in copies:
        copy.wait()
    level_hat, noisy = noisy_of(level_ref[...], rows_of(coords_ref), rows_of(kicks_ref))
    scaled = noisy / jnp.sqrt(level_hat * level_hat + sigma_data * sigma_data)
    embedded = lax.dot_general(
        scaled, coord_in_ref[...], TN, precision=lax.Precision.HIGHEST, preferred_element_type=F32
    )
    state = single_ref[...].astype(F32) + embedded
    state_ref[...] = state
    normed = norm_rows(state, gain_ref[0:1]).astype(BF16)
    normed_ref[...] = normed
    write_edges(normed, lax.axis_index("row"), first_edge_ref, second_edge_ref)


def pair_kernel(
    steps, tile_hbm, gain_hbm, heads_hbm, bias_hbm, tile_ref, gain_ref, heads_ref, bias_ref, tile_sems, bias_sems, sems
):
    keys, channels = tile_ref.shape[1:]
    head_count = heads_ref.shape[0]
    small = fetch([gain_hbm, heads_hbm], [gain_ref, heads_ref], sems)
    spans = [pl.ds(begin, step_rows) for begin, step_rows in steps]
    tiles = fetch([tile_hbm.at[span] for span in spans], [tile_ref.at[span] for span in spans], tile_sems)
    for copy in small:
        copy.wait()
    weights = heads_ref[...].astype(F32) * gain_ref[...]
    high = weights.astype(BF16)
    low = (weights - high.astype(F32)).astype(BF16)
    total = jnp.sum(high.astype(F32) + low.astype(F32), axis=1, keepdims=True)
    left = jnp.concatenate([high, low], axis=0)
    sent = []
    for step, (begin, step_rows) in enumerate(steps):
        tiles[step].wait()
        tile = tile_ref[begin : begin + step_rows].reshape(step_rows * keys, channels).T
        wide = tile.astype(F32)
        average = jnp.mean(wide, axis=0, keepdims=True)
        centred = wide - average
        variance = jnp.mean(centred * centred, axis=0, keepdims=True)
        sums = dot(left, tile)
        raw = sums[:head_count] + sums[head_count:]
        result = (raw - average * total) * lax.rsqrt(variance + norm_eps)
        pieces = [result[:, i * keys : (i + 1) * keys] for i in range(step_rows)]
        bias_ref[:, begin : begin + step_rows, :] = jnp.swapaxes(jnp.stack(pieces, axis=0), 0, 1).astype(BF16)
        copy = pltpu.make_async_copy(
            bias_ref.at[:, spans[step], :], bias_hbm.at[:, spans[step], :], bias_sems.at[step]
        )
        copy.start()
        sent.append(copy)
    for copy in sent:
        copy.wait()


def live_bias(mask_ref, chunk, outside):
    final = mask_ref.shape[0] - 1
    row = mask_ref[pl.ds(jnp.clip(chunk, 0, final), 1), :].astype(F32)
    column = column_of(row)
    column = jnp.where(outside, 0.0, column)
    return (column - 1.0) * -masked_score


def attend(queries, blocks, parts, lives, w_kv, offsets_ref, scratch):
    key_scr, value_scr, live_scr, score_scr, prob_scr, out_scr = scratch
    offsets = offsets_ref[...]
    row_count, width = queries.shape
    block_count = len(blocks)
    head_size = width // AHEADS
    at = 0
    for part in parts:
        projected = dot(part, w_kv).astype(BF16).astype(F32)
        key_scr[at : at + part.shape[0], :] = projected[:, :width]
        value_scr[at : at + part.shape[0], :] = projected[:, width:]
        at += part.shape[0]
    at = 0
    for live in lives:
        live_scr[at : at + live.shape[0], :] = live
        at += live.shape[0]

    stacked_rows = AHEADS * WQ
    lane = lax.broadcasted_iota(jnp.int32, (stacked_rows, width), 1)
    line = lax.broadcasted_iota(jnp.int32, (stacked_rows, width), 0)
    own_head = lane // head_size == line // WQ
    pick = jnp.where(lane == 0, 1.0, 0.0).astype(BF16)
    ones = jnp.ones((WK, width), BF16)
    begins = []
    for b, (block, shift) in enumerate(blocks):
        begin = block * WQ + shift + offsets[0, block]
        begins.append(begin)
        keys = key_scr[pl.ds(begin, WK), :].astype(BF16)
        live = live_scr[pl.ds(begin, WK), :].astype(BF16)
        query = queries[b * WQ : (b + 1) * WQ]
        query = jnp.concatenate([query] * AHEADS, axis=0)
        query = jnp.where(own_head, query, jnp.zeros_like(query))
        score_scr[b * stacked_rows : (b + 1) * stacked_rows, :] = dot(
            jnp.concatenate([query, pick], axis=1), jnp.concatenate([keys, live], axis=1), NT
        )
    factor = LOG2E / math.sqrt(head_size)
    step = 4 * stacked_rows
    for begin in range(0, block_count * stacked_rows, step):
        scores = score_scr[begin : begin + step, :]
        largest = jnp.max(scores, axis=-1, keepdims=True)
        prob_scr[begin : begin + step, :] = jnp.exp2((scores - largest) * factor).astype(BF16)
    for b in range(block_count):
        values = value_scr[pl.ds(begins[b], WK), :].astype(BF16)
        probs = prob_scr[b * stacked_rows : (b + 1) * stacked_rows, :]
        both = dot(probs, jnp.concatenate([values, ones], axis=1))
        mixed = jnp.where(own_head, both[:, :width], 0.0)
        weight = jnp.where(own_head, both[:, width:], 0.0)
        mixed = sum(mixed[h * WQ : (h + 1) * WQ] for h in range(AHEADS))
        weight = sum(weight[h * WQ : (h + 1) * WQ] for h in range(AHEADS))
        out_scr[b * WQ : (b + 1) * WQ, :] = (mixed / weight).astype(BF16)
    return out_scr[0:row_count, :]


def window_scratch(extended, row_count, width):
    scores = row_count * AHEADS
    return [
        pltpu.VMEM((extended, width), F32),
        pltpu.VMEM((extended, width), F32),
        pltpu.VMEM((extended, LANES), F32),
        pltpu.VMEM((scores, WK), F32),
        pltpu.VMEM((scores, WK), BF16),
        pltpu.VMEM((row_count, width), BF16),
    ]


def member_of(token_ref, mask_ref, first_chunk, base, tok_rows):
    chunk_count = token_ref.shape[0]
    tokens = lax.broadcasted_iota(jnp.int32, (tok_rows, LANES), 0)
    pieces = []
    for chunk in range(chunk_count):
        local = token_ref[chunk : chunk + 1, :] - base
        valid = mask_ref[pl.ds(first_chunk + chunk, 1), :]
        local = jnp.where(valid > 0, local, -1)
        pieces.append(jnp.where(local == tokens, 1.0, 0.0).astype(BF16))
    return jnp.concatenate(pieces, axis=1)


def encoder_kernel(
    offsets_ref, level_ref, state_ref, low_ref, mid_ref, high_ref, mask_ref, token_ref, w_qkv_ref, w_out_ref,
    lift_ref, single_ref, embed_ref, gain_ref, encoded_ref, token_state_ref, normed_ref, member_ref, *scratch
):
    row, count = lax.axis_index("row"), lax.axis_size("row")
    first, last = row == 0, row == count - 1
    tok_rows = single_ref.shape[0]
    chunks = token_ref.shape[0]
    width = state_ref.shape[1]
    begin = row * chunks
    low, high = halo_rows(row, count, low_ref, high_ref)
    mid = mid_ref[...]
    lives = [live_bias(mask_ref, begin - 1, first)[LANES - HALO :]]
    lives += [live_bias(mask_ref, begin + chunk, False) for chunk in range(chunks)]
    lives += [live_bias(mask_ref, begin + chunks, last)[:HALO]]
    w_qkv = w_qkv_ref[0]
    queries = dot(mid, w_qkv[:, :width]).astype(BF16)
    mixed = attend(
        queries, [(b, HALO) for b in range(mid.shape[0] // WQ)], [low, mid, high], lives, w_qkv[:, width:], offsets_ref, scratch
    )
    state = state_ref[...] + dot(mixed, w_out_ref[0])
    encoded_ref[...] = state
    lifted = jnp.maximum(dot(state.astype(BF16), lift_ref[...]), 0.0).astype(BF16)
    member = member_of(token_ref, mask_ref, begin, row * tok_rows, tok_rows)
    member_ref[...] = member
    counts = jnp.maximum(dot(member, jnp.ones((member.shape[1], LANES), BF16)), 1.0)
    pooled = dot(member, lifted) / counts[:, 0:1]
    level_hat = (1.0 + gamma_boost) * level_ref[...]
    token_state = (
        pooled + single_ref[...].astype(F32) + jnp.log(level_hat / sigma_data) / 4.0 * embed_ref[...]
    )
    token_state_ref[...] = token_state
    normed_ref[...] = norm_rows(token_state, gain_ref[0:1]).astype(BF16)


def head_spans(head_size):
    spans = []
    for h in range(HEADS):
        begin = h * head_size // LANES * LANES
        end = -(-(h + 1) * head_size // LANES) * LANES
        spans.append((begin, end))
    return spans


def inside_head(h, head_size, shape, begin):
    lane = lax.broadcasted_iota(jnp.int32, shape, 1) + begin
    return (lane >= h * head_size) & (lane < (h + 1) * head_size)


class Tiles:
    def __init__(self, rows, width):
        self.rows = rows
        self.tiles = [None] * (width // LANES)

    def add(self, h, head_size, begin, values):
        for at in range(0, values.shape[1], LANES):
            tile = (begin + at) // LANES
            inside = inside_head(h, head_size, (self.rows, LANES), begin + at)
            kept = self.tiles[tile]
            part = values[:, at : at + LANES]
            self.tiles[tile] = jnp.where(inside, part, 0.0 if kept is None else kept)

    def join(self):
        return jnp.concatenate(self.tiles, axis=1)


def weighted_values(prob_scr, kv_scr, h, count, piece, begin, end):
    ones = jnp.ones((piece, LANES), BF16)
    return functools.reduce(
        jnp.add,
        [
            dot(prob_scr[at, h], jnp.concatenate([kv_scr[at * piece : (at + 1) * piece, begin:end], ones], axis=1))
            for at in range(count)
        ],
    )


def token_scores(query_of, kv_scr, bias_of, key_mask_ref, row, near, count, per_block, spans, scale, score_scr):
    piece = key_mask_ref.shape[1]

    def one(at):
        other = (row ^ (near + at // per_block)) * per_block + at % per_block
        live = key_mask_ref[pl.ds(other, 1), :] > 0
        rows = pl.ds(at * piece if isinstance(at, int) else pl.multiple_of(at * piece, piece), piece)
        for h in range(HEADS):
            begin, end = spans[h]
            scores = dot(query_of(h), kv_scr[rows, begin:end], NT) * scale
            scores = scores + bias_of(at, other, h).astype(F32)
            score_scr[at, h] = jnp.where(live, scores, masked_score)

    if count <= 4:
        for at in range(count):
            one(at)
    else:
        lax.fori_loop(0, count, lambda at, carry: (one(at), carry)[1], 0)


def attend_first_kernel(near_count, row_count, smp_count, *refs):
    normed_refs = refs[:near_count]
    bias_refs = refs[near_count : near_count + smp_count]
    (
        key_mask_ref, w_qkv_ref, query_ref, mixed_ref, largest_ref, total_ref, far_bias_ref, kv_scr, score_scr, prob_scr,
        bias_scr,
    ) = refs[near_count + smp_count :]
    row, smp = lax.axis_index("row"), lax.axis_index("smp")
    tok_rows, width = query_ref.shape
    head_size = width // HEADS
    piece = key_mask_ref.shape[1]
    per_block = tok_rows // piece
    for d in range(smp_count):
        bias_scr[smp ^ d] = bias_refs[d][...]
    for d in range(near_count, row_count):
        for e in range(per_block):
            far_bias_ref[(d - near_count) * per_block + e] = bias_scr[(row ^ d) * per_block + e]
    queries = dot(normed_refs[0][...], w_qkv_ref[:, :width]).astype(BF16)
    query_ref[...] = queries
    for d in range(near_count):
        kv_scr[d * tok_rows : (d + 1) * tok_rows, :] = dot(normed_refs[d][...], w_qkv_ref[:, width:]).astype(BF16)
    spans = head_spans(head_size)

    def query_of(h):
        begin, end = spans[h]
        query = queries[:, begin:end]
        return jnp.where(inside_head(h, head_size, query.shape, begin), query, jnp.zeros_like(query))

    count = near_count * per_block
    token_scores(
        query_of, kv_scr, lambda at, other, h: bias_scr[other, h], key_mask_ref, row, 0, count, per_block, spans,
        1.0 / math.sqrt(head_size), score_scr,
    )
    step = 4
    for begin in range(0, HEADS, step):
        heads = slice(begin, begin + step)
        scores = [score_scr[at, heads] for at in range(count)]
        largest = jnp.max(functools.reduce(jnp.maximum, scores), axis=-1, keepdims=True)
        largest_ref[heads] = jnp.broadcast_to(largest, largest_ref[heads].shape)
        for at in range(count):
            prob_scr[at, heads] = jnp.exp2((scores[at] - largest) * LOG2E).astype(BF16)
    mixed = Tiles(tok_rows, width)
    for h in range(HEADS):
        begin, end = spans[h]
        both = weighted_values(prob_scr, kv_scr, h, count, piece, width + begin, width + end)
        mixed.add(h, head_size, begin, both[:, : end - begin])
        total_ref[h] = both[:, end - begin :]
    mixed_ref[...] = mixed.join()


def token_kernel(near_count, row_count, *refs):
    far_count = row_count - near_count
    normed_refs = refs[:far_count]
    (
        query_ref, carried_ref, largest_ref, total_ref, bias_ref, state_ref, key_mask_ref, w_qkv_ref, w_proj_ref, gain_ref, ffn_in_ref,
        ffn_out_ref, spread_ref, encoded_ref, member_ref, atom_gain_ref, out_ref, joined_ref, atom_normed_ref,
        second_edge_ref, first_edge_ref, kv_scr, score_scr, prob_scr, shrink_scr,
    ) = refs[far_count:]
    row = lax.axis_index("row")
    tok_rows, width = state_ref.shape
    head_size = width // HEADS
    piece = key_mask_ref.shape[1]
    per_block = tok_rows // piece
    for d in range(far_count):
        kv_scr[d * tok_rows : (d + 1) * tok_rows, :] = dot(normed_refs[d][...], w_qkv_ref[:, width:]).astype(BF16)
    spans = head_spans(head_size)
    queries = query_ref[...]

    def query_of(h):
        begin, end = spans[h]
        query = queries[:, begin:end]
        return jnp.where(inside_head(h, head_size, query.shape, begin), query, jnp.zeros_like(query))

    count = far_count * per_block
    token_scores(
        query_of, kv_scr, lambda at, other, h: bias_ref[at, h], key_mask_ref, row, near_count, count, per_block, spans,
        1.0 / math.sqrt(head_size), score_scr,
    )
    step = 4
    for begin in range(0, HEADS, step):
        heads = slice(begin, begin + step)
        scores = [score_scr[at, heads] for at in range(count)]
        before = largest_ref[heads]
        largest = jnp.max(functools.reduce(jnp.maximum, scores), axis=-1, keepdims=True)
        largest = jnp.maximum(jnp.broadcast_to(largest, before.shape), before)
        shrink_scr[heads] = jnp.exp2((before - largest) * LOG2E)
        for at in range(count):
            prob_scr[at, heads] = jnp.exp2((scores[at] - largest[:, :, :piece]) * LOG2E).astype(BF16)
    mixed, total = Tiles(tok_rows, width), Tiles(tok_rows, width)
    for h in range(HEADS):
        begin, end = spans[h]
        both = weighted_values(prob_scr, kv_scr, h, count, piece, width + begin, width + end)
        shrink = shrink_scr[h]
        weight = both[:, end - begin :] + shrink * total_ref[h]
        for at in range(begin, end, LANES):
            part = both[:, at - begin : at - begin + LANES] + shrink * carried_ref[:, at : at + LANES]
            mixed.add(h, head_size, at, part)
            total.add(h, head_size, at, weight)
    attended = (mixed.join() / total.join()).astype(BF16)
    state = state_ref[...] + dot(attended, w_proj_ref[...])
    normed = norm_rows(state, gain_ref[1:2]).astype(BF16)
    hidden = dot(normed, ffn_in_ref[...])
    half = hidden.shape[1] // 2
    gate, up = hidden[:, :half], hidden[:, half:]
    active = (gate / (1.0 + jnp.exp(-gate)) * up).astype(BF16)
    state = state + dot(active, ffn_out_ref[...])
    result = state.astype(BF16)
    out_ref[0] = result
    spread = dot(result, spread_ref[...]).astype(BF16)
    joined = encoded_ref[...] + dot(member_ref[...], spread, TN)
    joined_ref[...] = joined
    normed = norm_rows(joined, atom_gain_ref[1:2]).astype(BF16)
    atom_normed_ref[...] = normed
    write_edges(normed, row, first_edge_ref, second_edge_ref)


def directions(state, level_ref, coords_ref, kicks_ref, gain_ref, coord_out_ref, direction_ref, begin):
    rows = state.shape[0]
    normed = norm_rows(state, gain_ref[...]).astype(BF16)
    update = dot(coord_out_ref[...], normed, NT)
    for k in range(coords_ref.shape[0]):
        level_hat, noisy = noisy_of(
            level_ref[...], coords_ref[k, :, begin : begin + rows], kicks_ref[k, :, begin : begin + rows]
        )
        base_square = sigma_data * sigma_data + level_hat * level_hat
        skip_scale = sigma_data * sigma_data / base_square
        out_scale = level_hat * sigma_data / jnp.sqrt(base_square)
        denoised = skip_scale * noisy + out_scale * update[k : k + 1]
        direction_ref[k, :, begin : begin + rows] = (noisy - denoised) / level_hat


def inner_kernel(
    offsets_ref, level_ref, coords_ref, kicks_ref, state_ref, mid_ref, mask_ref, w_qkv_ref, w_out_ref, gain_ref,
    coord_out_ref, direction_ref, *scratch
):
    atoms, width = state_ref.shape
    chunks = atoms // LANES
    begin = lax.axis_index("row") * chunks
    edge = LANES
    skip = edge - HALO
    lives = [live_bias(mask_ref, begin, False)[skip:]]
    lives += [live_bias(mask_ref, begin + chunk, False) for chunk in range(1, chunks)]
    w_qkv = w_qkv_ref[1]
    queries = dot(mid_ref[edge : atoms - edge, :], w_qkv[:, :width]).astype(BF16)
    blocks = [(b, -skip) for b in range(edge // WQ, (atoms - edge) // WQ)]
    mixed = attend(queries, blocks, [mid_ref[skip:, :]], lives, w_qkv[:, width:], offsets_ref, scratch)
    state = state_ref[edge : atoms - edge, :] + dot(mixed, w_out_ref[1])
    for k in range(direction_ref.shape[0]):
        direction_ref[k, :, 0:edge] = jnp.zeros((1, edge), F32)
        direction_ref[k, :, atoms - edge :] = jnp.zeros((1, edge), F32)
    directions(state, level_ref, coords_ref, kicks_ref, gain_ref, coord_out_ref, direction_ref, edge)


def edge_kernel(
    offsets_ref, level_ref, coords_ref, kicks_ref, state_ref, low_ref, mid_ref, high_ref, mask_ref, w_qkv_ref,
    w_out_ref, gain_ref, coord_out_ref, inner_ref, direction_ref, *scratch
):
    row, count = lax.axis_index("row"), lax.axis_size("row")
    first, last = row == 0, row == count - 1
    atoms, width = state_ref.shape
    chunks = atoms // LANES
    begin = row * chunks
    edge = LANES
    reach = edge + HALO
    w_qkv = w_qkv_ref[1]
    w_out = w_out_ref[1]
    for k in range(direction_ref.shape[0]):
        direction_ref[k, :, edge : atoms - edge] = inner_ref[k, :, edge : atoms - edge]
    low, high = halo_rows(row, count, low_ref, high_ref)
    lives = [
        live_bias(mask_ref, begin - 1, first)[LANES - HALO :],
        live_bias(mask_ref, begin, False),
        live_bias(mask_ref, begin + 1, False)[:HALO],
        live_bias(mask_ref, begin + chunks - 2, False)[LANES - HALO :],
        live_bias(mask_ref, begin + chunks - 1, False),
        live_bias(mask_ref, begin + chunks, last)[:HALO],
    ]
    own = jnp.concatenate([mid_ref[0:edge, :], mid_ref[atoms - edge :, :]], axis=0)
    queries = dot(own, w_qkv[:, :width]).astype(BF16)
    span = edge + 2 * HALO
    blocks = [(b, HALO) for b in range(edge // WQ)]
    blocks += [(b, span + reach - atoms) for b in range((atoms - edge) // WQ, atoms // WQ)]
    mixed = attend(
        queries, blocks, [low, mid_ref[0:reach, :], mid_ref[atoms - reach :, :], high], lives, w_qkv[:, width:], offsets_ref,
        scratch,
    )
    shift = dot(mixed, w_out)
    lower = state_ref[0:edge, :] + shift[:edge]
    upper = state_ref[atoms - edge :, :] + shift[edge:]
    directions(lower, level_ref, coords_ref, kicks_ref, gain_ref, coord_out_ref, direction_ref, 0)
    directions(upper, level_ref, coords_ref, kicks_ref, gain_ref, coord_out_ref, direction_ref, atoms - edge)


def halos_of(first_edge, second_edge):
    count = lax.axis_size("row")
    second = [(0, 0), (count - 1, count - 1)]
    second += [(i, i + 1 if i % 2 else i - 1) for i in range(1, count - 1)]
    from_second = lax.ppermute(second_edge, "row", second)
    return lax.ppermute(first_edge, "row", [(i, i ^ 1) for i in range(count)]), from_second


def spread_over(block, axis, after=None):
    count = lax.axis_size(axis)
    have = {0: block}
    bit = count // 2
    while bit:
        pairs = [(i, i ^ bit) for i in range(count)]
        for d in list(have):
            sent = have[d]
            if d and after is not None:
                sent, _ = lax.optimization_barrier((sent, after))
            have[d | bit] = lax.ppermute(sent, axis, pairs)
        bit //= 2
    return [have[d] for d in range(count)]


def per_device(
    positions,
    noise_draw,
    noise_level,
    atom_single,
    token_single,
    pair_cond,
    atom_to_token,
    window_offsets,
    atom_mask,
    token_mask,
    coord_in,
    atom_gain,
    atom_qkv,
    atom_proj,
    gather_in,
    noise_embed,
    pair_gain,
    pair_heads,
    token_gain,
    token_qkv,
    token_proj,
    ffn_in,
    ffn_out,
    scatter_out,
    out_gain,
    coord_out,
):
    row_count, smp_count = lax.axis_size("row"), lax.axis_size("smp")
    atoms, width = atom_single.shape
    tok_rows, token_width = token_single.shape
    heads = pair_heads.shape[1]
    keys = pair_cond.shape[1]
    level = noise_level.reshape(1, 1)
    coords = positions.transpose(1, 0, 2)
    kicks = noise_draw.transpose(1, 0, 2)
    mask = atom_mask.reshape(-1, LANES)
    tokens = atom_to_token.reshape(-1, LANES)
    shape = jax.ShapeDtypeStruct
    state_like = shape((atoms, width), F32)
    normed_like = shape((atoms, width), BF16)
    edge_like = shape((HALO, width), BF16)

    state, normed, second_edge, first_edge = pl.pallas_call(
        prepare_kernel,
        out_shape=(state_like, normed_like, edge_like, edge_like),
        in_specs=hbm(6),
        out_specs=tuple(whole(4)),
        scratch_shapes=[pltpu.VMEM(a.shape, a.dtype) for a in (level, coords, kicks, atom_single, coord_in, atom_gain)]
        + [pltpu.SemaphoreType.DMA((6,))],
        compiler_params=vmem(PRIVATE),
        cost_estimate=cost(1.5),
    )(level, coords, kicks, atom_single, coord_in, atom_gain)
    low, high = halos_of(first_edge, second_edge)

    pair_rows, _, channels = pair_cond.shape
    step_rows = 32
    half = pair_rows // 2
    steps = [(0, step_rows), (step_rows, half - step_rows), (half, pair_rows - half)]
    gain_row, _ = lax.optimization_barrier((pair_gain, second_edge))
    bias = pl.pallas_call(
        functools.partial(pair_kernel, steps),
        out_shape=shape((heads, pair_rows, keys), BF16),
        in_specs=hbm(3),
        out_specs=hbm(1)[0],
        scratch_shapes=[
            pltpu.VMEM(pair_cond.shape, BF16),
            pltpu.VMEM((1, channels), F32),
            pltpu.VMEM((heads, channels), BF16),
            pltpu.VMEM((heads, pair_rows, keys), BF16),
            pltpu.SemaphoreType.DMA((len(steps),)),
            pltpu.SemaphoreType.DMA((len(steps),)),
            pltpu.SemaphoreType.DMA((2,)),
        ],
        compiler_params=vmem(PRIVATE),
        cost_estimate=cost(5),
    )(pair_cond, gain_row.reshape(1, -1), pair_heads.T)

    encoded, token_state, token_normed, member = pl.pallas_call(
        encoder_kernel,
        out_shape=(
            state_like,
            shape((tok_rows, token_width), F32),
            shape((tok_rows, token_width), BF16),
            shape((tok_rows, atoms), BF16),
        ),
        in_specs=whole(1) + whole(13),
        out_specs=tuple(whole(4)),
        scratch_shapes=window_scratch(atoms + 2 * HALO, atoms, width),
        compiler_params=vmem(16),
        cost_estimate=cost(3.4),
    )(
        window_offsets.reshape(1, -1), level, state, low, normed, high, mask, tokens, atom_qkv, atom_proj, gather_in,
        token_single, noise_embed.reshape(1, -1), token_gain,
    )
    gathered = spread_over(token_normed, "row")
    biases = spread_over(bias, "smp", gathered[1 : row_count // 2 + 1])

    key_mask = token_mask.reshape(-1, keys)
    near_count = row_count - row_count // 4
    far_count = row_count - near_count
    pieces = tok_rows // keys

    def need(count):
        tile = tok_rows * max(keys, LANES)
        return (count * (keys * token_width * 4 + heads * tile * 6) + smp_count * heads * tile * 2) // 2**20 + 1

    queries, carried, largest, total, far_bias = pl.pallas_call(
        functools.partial(attend_first_kernel, near_count, row_count, smp_count),
        out_shape=(
            shape((tok_rows, token_width), BF16),
            shape((tok_rows, token_width), F32),
            shape((heads, tok_rows, LANES), F32),
            shape((heads, tok_rows, LANES), F32),
            shape((far_count * pieces, heads, tok_rows, keys), BF16),
        ),
        in_specs=whole(near_count + smp_count + 2),
        out_specs=tuple(whole(5)),
        scratch_shapes=[
            pltpu.VMEM((near_count * tok_rows, 2 * token_width), BF16),
            pltpu.VMEM((near_count * pieces, heads, tok_rows, keys), F32),
            pltpu.VMEM((near_count * pieces, heads, tok_rows, keys), BF16),
            pltpu.VMEM((smp_count, heads, tok_rows, keys), BF16),
        ],
        compiler_params=vmem(14 + need(near_count * pieces) * 3 // 2),
        cost_estimate=cost(4),
    )(*gathered[:near_count], *biases, key_mask, token_qkv)
    token_result, joined, atom_normed, second_edge, first_edge = pl.pallas_call(
        functools.partial(token_kernel, near_count, row_count),
        out_shape=(
            shape((1, tok_rows, token_width), BF16),
            state_like,
            normed_like,
            edge_like,
            edge_like,
        ),
        in_specs=whole(far_count + 16),
        out_specs=tuple(whole(5)),
        scratch_shapes=[
            pltpu.VMEM((far_count * tok_rows, 2 * token_width), BF16),
            pltpu.VMEM((far_count * pieces, heads, tok_rows, keys), F32),
            pltpu.VMEM((far_count * pieces, heads, tok_rows, keys), BF16),
            pltpu.VMEM((heads, tok_rows, LANES), F32),
        ],
        compiler_params=vmem(20 + need(far_count * pieces)),
        cost_estimate=cost(6),
    )(
        *gathered[near_count:], queries, carried, largest, total, far_bias, token_state, key_mask, token_qkv, token_proj,
        token_gain, ffn_in, ffn_out, scatter_out, encoded, member, atom_gain,
    )
    low, high = halos_of(first_edge, second_edge)

    edge = LANES
    direction_like = shape(coords.shape, F32)
    out_row = out_gain.reshape(1, -1)
    inner = pl.pallas_call(
        inner_kernel,
        out_shape=direction_like,
        in_specs=whole(1) + whole(10),
        out_specs=whole(1)[0],
        scratch_shapes=window_scratch(atoms - edge + HALO, atoms - 2 * edge, width),
        compiler_params=vmem(16),
        cost_estimate=cost(2.7),
    )(
        window_offsets.reshape(1, -1), level, coords, kicks, joined, atom_normed, mask, atom_qkv, atom_proj, out_row, coord_out
    )
    direction = pl.pallas_call(
        edge_kernel,
        out_shape=direction_like,
        in_specs=whole(1) + whole(13),
        out_specs=whole(1)[0],
        scratch_shapes=window_scratch(2 * (edge + 2 * HALO), 2 * edge, width),
        compiler_params=vmem(12),
        cost_estimate=cost(2),
    )(
        window_offsets.reshape(1, -1), level, coords, kicks, joined, low, atom_normed, high, mask, atom_qkv, atom_proj, out_row,
        coord_out, inner,
    )
    return (token_result, direction.transpose(1, 0, 2))


def solution(mesh):
    in_specs = (
        P(("grp", "smp"), None, "row"),
        P(("grp", "smp"), None, "row"),
        P(("grp", "smp")),
        P(("grp", "row"), None),
        P(("grp", "row"), None),
        P(("grp", "row"), "smp", None),
        P(("grp", "row")),
        P(("grp", "row")),
        P("grp"),
        P("grp"),
        P(),
        P(),
        P(),
        P(),
        P(),
        P(),
        P(),
        P(),
        P(),
        P(),
        P(),
        P(),
        P(),
        P(),
        P(),
        P(),
    )
    out_specs = (P(("grp", "smp"), "row", None), P(("grp", "smp"), None, "row"))
    return jax.shard_map(
        per_device, mesh=mesh, in_specs=in_specs, out_specs=out_specs, check_vma=False
    )
```

```python
import functools
import math

import jax
import jax.numpy as jnp
from jax import lax
from jax.experimental import pallas as pl
from jax.experimental.pallas import tpu as pltpu
from jax.sharding import PartitionSpec as P

HEADS = 16
AHEADS = 4
WQ = 32
WK = 128
HALO = 96
LANES = 128
PRIVATE = 62

sigma_data = 16.0
gamma_boost = 0.8
norm_eps = 1e-05
masked_score = -1e30
LOG2E = math.log2(math.e)
F32 = jnp.float32
BF16 = jnp.bfloat16
NT = (((1,), (1,)), ((), ()))
TN = (((0,), (0,)), ((), ()))


def vmem(mib):
    return pltpu.CompilerParams(vmem_limit_bytes=mib * 1024 * 1024)


def cost(micros):
    return pl.CostEstimate(flops=int(micros * 1e9), transcendentals=0, bytes_accessed=int(micros * 3e6))


def hbm(count):
    return [pl.BlockSpec(memory_space=pltpu.HBM)] * count


def fetch(sources, targets, sems):
    copies = [pltpu.make_async_copy(a, b, sems.at[i]) for i, (a, b) in enumerate(zip(sources, targets))]
    for copy in copies:
        copy.start()
    return copies


def whole(count):
    return [pl.BlockSpec(memory_space=pltpu.VMEM)] * count


def dot(a, b, dims=(((1,), (0,)), ((), ()))):
    return lax.dot_general(a, b, dims, preferred_element_type=F32)


def norm_rows(values, gain):
    average = jnp.mean(values, axis=-1, keepdims=True)
    centred = values - average
    variance = jnp.mean(centred * centred, axis=-1, keepdims=True)
    return centred * lax.rsqrt(variance + norm_eps) * gain


def noisy_of(level, coords, kicks):
    level_hat = (1.0 + gamma_boost) * level
    noisy = coords + jnp.sqrt(level_hat * level_hat - level * level) * kicks
    return level_hat, noisy


def column_of(row):
    size = row.shape[1]
    down = lax.broadcasted_iota(jnp.int32, (size, size), 0)
    across = lax.broadcasted_iota(jnp.int32, (size, size), 1)
    spread = jnp.where(down == across, jnp.broadcast_to(row, (size, size)), 0.0)
    return dot(spread.astype(BF16), jnp.ones((size, LANES), BF16))


def rows_of(ref):
    return jnp.concatenate([ref[k] for k in range(ref.shape[0])], axis=0)


def write_edges(normed, row, first_edge_ref, second_edge_ref):
    even = row % 2 == 0
    low, high = normed[:HALO], normed[normed.shape[0] - HALO :]
    first_edge_ref[...] = jnp.where(even, high, low)
    second_edge_ref[...] = jnp.where(even, low, high)


def halo_rows(row, count, first_ref, second_ref):
    even = row % 2 == 0
    low = jnp.where(even, second_ref[...], first_ref[...])
    high = jnp.where(even, first_ref[...], second_ref[...])
    low = jnp.where(row == 0, jnp.zeros_like(low), low)
    high = jnp.where(row == count - 1, jnp.zeros_like(high), high)
    return low, high


def prepare_kernel(
    level_hbm, coords_hbm, kicks_hbm, single_hbm, coord_in_hbm, gain_hbm, state_ref, normed_ref, second_edge_ref, first_edge_ref,
    level_ref, coords_ref, kicks_ref, single_ref, coord_in_ref, gain_ref, sems
):
    copies = fetch(
        [level_hbm, coords_hbm, kicks_hbm, single_hbm, coord_in_hbm, gain_hbm],
        [level_ref, coords_ref, kicks_ref, single_ref, coord_in_ref, gain_ref], sems,
    )
    for copy in copies:
        copy.wait()
    level_hat, noisy = noisy_of(level_ref[...], rows_of(coords_ref), rows_of(kicks_ref))
    scaled = noisy / jnp.sqrt(level_hat * level_hat + sigma_data * sigma_data)
    embedded = lax.dot_general(
        scaled, coord_in_ref[...], TN, precision=lax.Precision.HIGHEST, preferred_element_type=F32
    )
    state = single_ref[...].astype(F32) + embedded
    state_ref[...] = state
    normed = norm_rows(state, gain_ref[0:1]).astype(BF16)
    normed_ref[...] = normed
    write_edges(normed, lax.axis_index("row"), first_edge_ref, second_edge_ref)


def pair_kernel(
    steps, tile_hbm, gain_hbm, heads_hbm, bias_hbm, tile_ref, gain_ref, heads_ref, bias_ref, tile_sems, bias_sems, sems
):
    keys, channels = tile_ref.shape[1:]
    head_count = heads_ref.shape[0]
    small = fetch([gain_hbm, heads_hbm], [gain_ref, heads_ref], sems)
    spans = [pl.ds(begin, step_rows) for begin, step_rows in steps]
    tiles = fetch([tile_hbm.at[span] for span in spans], [tile_ref.at[span] for span in spans], tile_sems)
    for copy in small:
        copy.wait()
    weights = heads_ref[...].astype(F32) * gain_ref[...]
    high = weights.astype(BF16)
    low = (weights - high.astype(F32)).astype(BF16)
    total = jnp.sum(high.astype(F32) + low.astype(F32), axis=1, keepdims=True)
    left = jnp.concatenate([high, low], axis=0)
    sent = []
    for step, (begin, step_rows) in enumerate(steps):
        tiles[step].wait()
        tile = tile_ref[begin : begin + step_rows].reshape(step_rows * keys, channels).T
        wide = tile.astype(F32)
        average = jnp.mean(wide, axis=0, keepdims=True)
        centred = wide - average
        variance = jnp.mean(centred * centred, axis=0, keepdims=True)
        sums = dot(left, tile)
        raw = sums[:head_count] + sums[head_count:]
        result = (raw - average * total) * lax.rsqrt(variance + norm_eps)
        pieces = [result[:, i * keys : (i + 1) * keys] for i in range(step_rows)]
        bias_ref[:, begin : begin + step_rows, :] = jnp.swapaxes(jnp.stack(pieces, axis=0), 0, 1).astype(BF16)
        copy = pltpu.make_async_copy(
            bias_ref.at[:, spans[step], :], bias_hbm.at[:, spans[step], :], bias_sems.at[step]
        )
        copy.start()
        sent.append(copy)
    for copy in sent:
        copy.wait()


def live_bias(mask_ref, chunk, outside):
    final = mask_ref.shape[0] - 1
    row = mask_ref[pl.ds(jnp.clip(chunk, 0, final), 1), :].astype(F32)
    column = column_of(row)
    column = jnp.where(outside, 0.0, column)
    return (column - 1.0) * -masked_score


def attend(queries, blocks, parts, lives, w_kv, offsets_ref, scratch):
    key_scr, value_scr, live_scr, score_scr, prob_scr, out_scr = scratch
    offsets = offsets_ref[...]
    row_count, width = queries.shape
    block_count = len(blocks)
    head_size = width // AHEADS
    at = 0
    for part in parts:
        projected = dot(part, w_kv).astype(BF16).astype(F32)
        key_scr[at : at + part.shape[0], :] = projected[:, :width]
        value_scr[at : at + part.shape[0], :] = projected[:, width:]
        at += part.shape[0]
    at = 0
    for live in lives:
        live_scr[at : at + live.shape[0], :] = live
        at += live.shape[0]

    stacked_rows = AHEADS * WQ
    lane = lax.broadcasted_iota(jnp.int32, (stacked_rows, width), 1)
    line = lax.broadcasted_iota(jnp.int32, (stacked_rows, width), 0)
    own_head = lane // head_size == line // WQ
    pick = jnp.where(lane == 0, 1.0, 0.0).astype(BF16)
    ones = jnp.ones((WK, width), BF16)
    begins = []
    for b, (block, shift) in enumerate(blocks):
        begin = block * WQ + shift + offsets[0, block]
        begins.append(begin)
        keys = key_scr[pl.ds(begin, WK), :].astype(BF16)
        live = live_scr[pl.ds(begin, WK), :].astype(BF16)
        query = queries[b * WQ : (b + 1) * WQ]
        query = jnp.concatenate([query] * AHEADS, axis=0)
        query = jnp.where(own_head, query, jnp.zeros_like(query))
        score_scr[b * stacked_rows : (b + 1) * stacked_rows, :] = dot(
            jnp.concatenate([query, pick], axis=1), jnp.concatenate([keys, live], axis=1), NT
        )
    factor = LOG2E / math.sqrt(head_size)
    step = 4 * stacked_rows
    for begin in range(0, block_count * stacked_rows, step):
        scores = score_scr[begin : begin + step, :]
        largest = jnp.max(scores, axis=-1, keepdims=True)
        prob_scr[begin : begin + step, :] = jnp.exp2((scores - largest) * factor).astype(BF16)
    for b in range(block_count):
        values = value_scr[pl.ds(begins[b], WK), :].astype(BF16)
        probs = prob_scr[b * stacked_rows : (b + 1) * stacked_rows, :]
        both = dot(probs, jnp.concatenate([values, ones], axis=1))
        mixed = jnp.where(own_head, both[:, :width], 0.0)
        weight = jnp.where(own_head, both[:, width:], 0.0)
        mixed = sum(mixed[h * WQ : (h + 1) * WQ] for h in range(AHEADS))
        weight = sum(weight[h * WQ : (h + 1) * WQ] for h in range(AHEADS))
        out_scr[b * WQ : (b + 1) * WQ, :] = (mixed / weight).astype(BF16)
    return out_scr[0:row_count, :]


def window_scratch(extended, row_count, width):
    scores = row_count * AHEADS
    return [
        pltpu.VMEM((extended, width), F32),
        pltpu.VMEM((extended, width), F32),
        pltpu.VMEM((extended, LANES), F32),
        pltpu.VMEM((scores, WK), F32),
        pltpu.VMEM((scores, WK), BF16),
        pltpu.VMEM((row_count, width), BF16),
    ]


def member_of(token_ref, mask_ref, first_chunk, base, tok_rows):
    chunk_count = token_ref.shape[0]
    tokens = lax.broadcasted_iota(jnp.int32, (tok_rows, LANES), 0)
    pieces = []
    for chunk in range(chunk_count):
        local = token_ref[chunk : chunk + 1, :] - base
        valid = mask_ref[pl.ds(first_chunk + chunk, 1), :]
        local = jnp.where(valid > 0, local, -1)
        pieces.append(jnp.where(local == tokens, 1.0, 0.0).astype(BF16))
    return jnp.concatenate(pieces, axis=1)


def encoder_kernel(
    offsets_ref, level_ref, state_ref, low_ref, mid_ref, high_ref, mask_ref, token_ref, w_qkv_ref, w_out_ref,
    lift_ref, single_ref, embed_ref, gain_ref, encoded_ref, token_state_ref, normed_ref, member_ref, *scratch
):
    row, count = lax.axis_index("row"), lax.axis_size("row")
    first, last = row == 0, row == count - 1
    tok_rows = single_ref.shape[0]
    chunks = token_ref.shape[0]
    width = state_ref.shape[1]
    begin = row * chunks
    low, high = halo_rows(row, count, low_ref, high_ref)
    mid = mid_ref[...]
    lives = [live_bias(mask_ref, begin - 1, first)[LANES - HALO :]]
    lives += [live_bias(mask_ref, begin + chunk, False) for chunk in range(chunks)]
    lives += [live_bias(mask_ref, begin + chunks, last)[:HALO]]
    w_qkv = w_qkv_ref[0]
    queries = dot(mid, w_qkv[:, :width]).astype(BF16)
    mixed = attend(
        queries, [(b, HALO) for b in range(mid.shape[0] // WQ)], [low, mid, high], lives, w_qkv[:, width:], offsets_ref, scratch
    )
    state = state_ref[...] + dot(mixed, w_out_ref[0])
    encoded_ref[...] = state
    lifted = jnp.maximum(dot(state.astype(BF16), lift_ref[...]), 0.0).astype(BF16)
    member = member_of(token_ref, mask_ref, begin, row * tok_rows, tok_rows)
    member_ref[...] = member
    counts = jnp.maximum(dot(member, jnp.ones((member.shape[1], LANES), BF16)), 1.0)
    pooled = dot(member, lifted) / counts[:, 0:1]
    level_hat = (1.0 + gamma_boost) * level_ref[...]
    token_state = (
        pooled + single_ref[...].astype(F32) + jnp.log(level_hat / sigma_data) / 4.0 * embed_ref[...]
    )
    token_state_ref[...] = token_state
    normed_ref[...] = norm_rows(token_state, gain_ref[0:1]).astype(BF16)


def head_spans(head_size):
    spans = []
    for h in range(HEADS):
        begin = h * head_size // LANES * LANES
        end = -(-(h + 1) * head_size // LANES) * LANES
        spans.append((begin, end))
    return spans


def inside_head(h, head_size, shape, begin):
    lane = lax.broadcasted_iota(jnp.int32, shape, 1) + begin
    return (lane >= h * head_size) & (lane < (h + 1) * head_size)


class Tiles:
    def __init__(self, rows, width):
        self.rows = rows
        self.tiles = [None] * (width // LANES)

    def add(self, h, head_size, begin, values):
        for at in range(0, values.shape[1], LANES):
            tile = (begin + at) // LANES
            inside = inside_head(h, head_size, (self.rows, LANES), begin + at)
            kept = self.tiles[tile]
            part = values[:, at : at + LANES]
            self.tiles[tile] = jnp.where(inside, part, 0.0 if kept is None else kept)

    def join(self):
        return jnp.concatenate(self.tiles, axis=1)


def weighted_values(prob_scr, kv_scr, h, count, piece, begin, end):
    ones = jnp.ones((piece, LANES), BF16)
    return functools.reduce(
        jnp.add,
        [
            dot(prob_scr[at, h], jnp.concatenate([kv_scr[at * piece : (at + 1) * piece, begin:end], ones], axis=1))
            for at in range(count)
        ],
    )


def token_scores(query_of, kv_scr, bias_of, key_mask_ref, row, near, count, per_block, spans, scale, score_scr):
    piece = key_mask_ref.shape[1]

    def one(at):
        other = (row ^ (near + at // per_block)) * per_block + at % per_block
        live = key_mask_ref[pl.ds(other, 1), :] > 0
        rows = pl.ds(at * piece if isinstance(at, int) else pl.multiple_of(at * piece, piece), piece)
        for h in range(HEADS):
            begin, end = spans[h]
            scores = dot(query_of(h), kv_scr[rows, begin:end], NT) * scale
            scores = scores + bias_of(at, other, h).astype(F32)
            score_scr[at, h] = jnp.where(live, scores, masked_score)

    if count <= 4:
        for at in range(count):
            one(at)
    else:
        lax.fori_loop(0, count, lambda at, carry: (one(at), carry)[1], 0)


def attend_first_kernel(near_count, row_count, smp_count, *refs):
    normed_refs = refs[:near_count]
    bias_refs = refs[near_count : near_count + smp_count]
    (
        key_mask_ref, w_qkv_ref, query_ref, mixed_ref, largest_ref, total_ref, far_bias_ref, kv_scr, score_scr, prob_scr,
        bias_scr,
    ) = refs[near_count + smp_count :]
    row, smp = lax.axis_index("row"), lax.axis_index("smp")
    tok_rows, width = query_ref.shape
    head_size = width // HEADS
    piece = key_mask_ref.shape[1]
    per_block = tok_rows // piece
    for d in range(smp_count):
        bias_scr[smp ^ d] = bias_refs[d][...]
    for d in range(near_count, row_count):
        for e in range(per_block):
            far_bias_ref[(d - near_count) * per_block + e] = bias_scr[(row ^ d) * per_block + e]
    queries = dot(normed_refs[0][...], w_qkv_ref[:, :width]).astype(BF16)
    query_ref[...] = queries
    for d in range(near_count):
        kv_scr[d * tok_rows : (d + 1) * tok_rows, :] = dot(normed_refs[d][...], w_qkv_ref[:, width:]).astype(BF16)
    spans = head_spans(head_size)

    def query_of(h):
        begin, end = spans[h]
        query = queries[:, begin:end]
        return jnp.where(inside_head(h, head_size, query.shape, begin), query, jnp.zeros_like(query))

    count = near_count * per_block
    token_scores(
        query_of, kv_scr, lambda at, other, h: bias_scr[other, h], key_mask_ref, row, 0, count, per_block, spans,
        1.0 / math.sqrt(head_size), score_scr,
    )
    step = 4
    for begin in range(0, HEADS, step):
        heads = slice(begin, begin + step)
        scores = [score_scr[at, heads] for at in range(count)]
        largest = jnp.max(functools.reduce(jnp.maximum, scores), axis=-1, keepdims=True)
        largest_ref[heads] = jnp.broadcast_to(largest, largest_ref[heads].shape)
        for at in range(count):
            prob_scr[at, heads] = jnp.exp2((scores[at] - largest) * LOG2E).astype(BF16)
    mixed = Tiles(tok_rows, width)
    for h in range(HEADS):
        begin, end = spans[h]
        both = weighted_values(prob_scr, kv_scr, h, count, piece, width + begin, width + end)
        mixed.add(h, head_size, begin, both[:, : end - begin])
        total_ref[h] = both[:, end - begin :]
    mixed_ref[...] = mixed.join()


def token_kernel(near_count, row_count, *refs):
    far_count = row_count - near_count
    normed_refs = refs[:far_count]
    (
        query_ref, carried_ref, largest_ref, total_ref, bias_ref, state_ref, key_mask_ref, w_qkv_ref, w_proj_ref, gain_ref, ffn_in_ref,
        ffn_out_ref, spread_ref, encoded_ref, member_ref, atom_gain_ref, out_ref, joined_ref, atom_normed_ref,
        second_edge_ref, first_edge_ref, kv_scr, score_scr, prob_scr, shrink_scr,
    ) = refs[far_count:]
    row = lax.axis_index("row")
    tok_rows, width = state_ref.shape
    head_size = width // HEADS
    piece = key_mask_ref.shape[1]
    per_block = tok_rows // piece
    for d in range(far_count):
        kv_scr[d * tok_rows : (d + 1) * tok_rows, :] = dot(normed_refs[d][...], w_qkv_ref[:, width:]).astype(BF16)
    spans = head_spans(head_size)
    queries = query_ref[...]

    def query_of(h):
        begin, end = spans[h]
        query = queries[:, begin:end]
        return jnp.where(inside_head(h, head_size, query.shape, begin), query, jnp.zeros_like(query))

    count = far_count * per_block
    token_scores(
        query_of, kv_scr, lambda at, other, h: bias_ref[at, h], key_mask_ref, row, near_count, count, per_block, spans,
        1.0 / math.sqrt(head_size), score_scr,
    )
    step = 4
    for begin in range(0, HEADS, step):
        heads = slice(begin, begin + step)
        scores = [score_scr[at, heads] for at in range(count)]
        before = largest_ref[heads]
        largest = jnp.max(functools.reduce(jnp.maximum, scores), axis=-1, keepdims=True)
        largest = jnp.maximum(jnp.broadcast_to(largest, before.shape), before)
        shrink_scr[heads] = jnp.exp2((before - largest) * LOG2E)
        for at in range(count):
            prob_scr[at, heads] = jnp.exp2((scores[at] - largest[:, :, :piece]) * LOG2E).astype(BF16)
    mixed, total = Tiles(tok_rows, width), Tiles(tok_rows, width)
    for h in range(HEADS):
        begin, end = spans[h]
        both = weighted_values(prob_scr, kv_scr, h, count, piece, width + begin, width + end)
        shrink = shrink_scr[h]
        weight = both[:, end - begin :] + shrink * total_ref[h]
        for at in range(begin, end, LANES):
            part = both[:, at - begin : at - begin + LANES] + shrink * carried_ref[:, at : at + LANES]
            mixed.add(h, head_size, at, part)
            total.add(h, head_size, at, weight)
    attended = (mixed.join() / total.join()).astype(BF16)
    state = state_ref[...] + dot(attended, w_proj_ref[...])
    normed = norm_rows(state, gain_ref[1:2]).astype(BF16)
    hidden = dot(normed, ffn_in_ref[...])
    half = hidden.shape[1] // 2
    gate, up = hidden[:, :half], hidden[:, half:]
    active = (gate / (1.0 + jnp.exp(-gate)) * up).astype(BF16)
    state = state + dot(active, ffn_out_ref[...])
    result = state.astype(BF16)
    out_ref[0] = result
    spread = dot(result, spread_ref[...]).astype(BF16)
    joined = encoded_ref[...] + dot(member_ref[...], spread, TN)
    joined_ref[...] = joined
    normed = norm_rows(joined, atom_gain_ref[1:2]).astype(BF16)
    atom_normed_ref[...] = normed
    write_edges(normed, row, first_edge_ref, second_edge_ref)


def directions(state, level_ref, coords_ref, kicks_ref, gain_ref, coord_out_ref, direction_ref, begin):
    rows = state.shape[0]
    normed = norm_rows(state, gain_ref[...]).astype(BF16)
    update = dot(coord_out_ref[...], normed, NT)
    for k in range(coords_ref.shape[0]):
        level_hat, noisy = noisy_of(
            level_ref[...], coords_ref[k, :, begin : begin + rows], kicks_ref[k, :, begin : begin + rows]
        )
        base_square = sigma_data * sigma_data + level_hat * level_hat
        skip_scale = sigma_data * sigma_data / base_square
        out_scale = level_hat * sigma_data / jnp.sqrt(base_square)
        denoised = skip_scale * noisy + out_scale * update[k : k + 1]
        direction_ref[k, :, begin : begin + rows] = (noisy - denoised) / level_hat


def inner_kernel(
    offsets_ref, level_ref, coords_ref, kicks_ref, state_ref, mid_ref, mask_ref, w_qkv_ref, w_out_ref, gain_ref,
    coord_out_ref, direction_ref, *scratch
):
    atoms, width = state_ref.shape
    chunks = atoms // LANES
    begin = lax.axis_index("row") * chunks
    edge = LANES
    skip = edge - HALO
    lives = [live_bias(mask_ref, begin, False)[skip:]]
    lives += [live_bias(mask_ref, begin + chunk, False) for chunk in range(1, chunks)]
    w_qkv = w_qkv_ref[1]
    queries = dot(mid_ref[edge : atoms - edge, :], w_qkv[:, :width]).astype(BF16)
    blocks = [(b, -skip) for b in range(edge // WQ, (atoms - edge) // WQ)]
    mixed = attend(queries, blocks, [mid_ref[skip:, :]], lives, w_qkv[:, width:], offsets_ref, scratch)
    state = state_ref[edge : atoms - edge, :] + dot(mixed, w_out_ref[1])
    for k in range(direction_ref.shape[0]):
        direction_ref[k, :, 0:edge] = jnp.zeros((1, edge), F32)
        direction_ref[k, :, atoms - edge :] = jnp.zeros((1, edge), F32)
    directions(state, level_ref, coords_ref, kicks_ref, gain_ref, coord_out_ref, direction_ref, edge)


def edge_kernel(
    offsets_ref, level_ref, coords_ref, kicks_ref, state_ref, low_ref, mid_ref, high_ref, mask_ref, w_qkv_ref,
    w_out_ref, gain_ref, coord_out_ref, inner_ref, direction_ref, *scratch
):
    row, count = lax.axis_index("row"), lax.axis_size("row")
    first, last = row == 0, row == count - 1
    atoms, width = state_ref.shape
    chunks = atoms // LANES
    begin = row * chunks
    edge = LANES
    reach = edge + HALO
    w_qkv = w_qkv_ref[1]
    w_out = w_out_ref[1]
    for k in range(direction_ref.shape[0]):
        direction_ref[k, :, edge : atoms - edge] = inner_ref[k, :, edge : atoms - edge]
    low, high = halo_rows(row, count, low_ref, high_ref)
    lives = [
        live_bias(mask_ref, begin - 1, first)[LANES - HALO :],
        live_bias(mask_ref, begin, False),
        live_bias(mask_ref, begin + 1, False)[:HALO],
        live_bias(mask_ref, begin + chunks - 2, False)[LANES - HALO :],
        live_bias(mask_ref, begin + chunks - 1, False),
        live_bias(mask_ref, begin + chunks, last)[:HALO],
    ]
    own = jnp.concatenate([mid_ref[0:edge, :], mid_ref[atoms - edge :, :]], axis=0)
    queries = dot(own, w_qkv[:, :width]).astype(BF16)
    span = edge + 2 * HALO
    blocks = [(b, HALO) for b in range(edge // WQ)]
    blocks += [(b, span + reach - atoms) for b in range((atoms - edge) // WQ, atoms // WQ)]
    mixed = attend(
        queries, blocks, [low, mid_ref[0:reach, :], mid_ref[atoms - reach :, :], high], lives, w_qkv[:, width:], offsets_ref,
        scratch,
    )
    shift = dot(mixed, w_out)
    lower = state_ref[0:edge, :] + shift[:edge]
    upper = state_ref[atoms - edge :, :] + shift[edge:]
    directions(lower, level_ref, coords_ref, kicks_ref, gain_ref, coord_out_ref, direction_ref, 0)
    directions(upper, level_ref, coords_ref, kicks_ref, gain_ref, coord_out_ref, direction_ref, atoms - edge)


def halos_of(first_edge, second_edge):
    count = lax.axis_size("row")
    second = [(0, 0), (count - 1, count - 1)]
    second += [(i, i + 1 if i % 2 else i - 1) for i in range(1, count - 1)]
    from_second = lax.ppermute(second_edge, "row", second)
    return lax.ppermute(first_edge, "row", [(i, i ^ 1) for i in range(count)]), from_second


def spread_over(block, axis, after=None):
    count = lax.axis_size(axis)
    have = {0: block}
    bit = count // 2
    while bit:
        pairs = [(i, i ^ bit) for i in range(count)]
        for d in list(have):
            sent = have[d]
            if d and after is not None:
                sent, _ = lax.optimization_barrier((sent, after))
            have[d | bit] = lax.ppermute(sent, axis, pairs)
        bit //= 2
    return [have[d] for d in range(count)]


def per_device(
    positions,
    noise_draw,
    noise_level,
    atom_single,
    token_single,
    pair_cond,
    atom_to_token,
    window_offsets,
    atom_mask,
    token_mask,
    coord_in,
    atom_gain,
    atom_qkv,
    atom_proj,
    gather_in,
    noise_embed,
    pair_gain,
    pair_heads,
    token_gain,
    token_qkv,
    token_proj,
    ffn_in,
    ffn_out,
    scatter_out,
    out_gain,
    coord_out,
):
    row_count, smp_count = lax.axis_size("row"), lax.axis_size("smp")
    atoms, width = atom_single.shape
    tok_rows, token_width = token_single.shape
    heads = pair_heads.shape[1]
    keys = pair_cond.shape[1]
    level = noise_level.reshape(1, 1)
    coords = positions.transpose(1, 0, 2)
    kicks = noise_draw.transpose(1, 0, 2)
    mask = atom_mask.reshape(-1, LANES)
    tokens = atom_to_token.reshape(-1, LANES)
    shape = jax.ShapeDtypeStruct
    state_like = shape((atoms, width), F32)
    normed_like = shape((atoms, width), BF16)
    edge_like = shape((HALO, width), BF16)

    state, normed, second_edge, first_edge = pl.pallas_call(
        prepare_kernel,
        out_shape=(state_like, normed_like, edge_like, edge_like),
        in_specs=hbm(6),
        out_specs=tuple(whole(4)),
        scratch_shapes=[pltpu.VMEM(a.shape, a.dtype) for a in (level, coords, kicks, atom_single, coord_in, atom_gain)]
        + [pltpu.SemaphoreType.DMA((6,))],
        compiler_params=vmem(PRIVATE),
        cost_estimate=cost(1.5),
    )(level, coords, kicks, atom_single, coord_in, atom_gain)
    low, high = halos_of(first_edge, second_edge)

    pair_rows, _, channels = pair_cond.shape
    step_rows = 32
    steps = [(0, step_rows), (step_rows, pair_rows - step_rows)]
    gain_row, _ = lax.optimization_barrier((pair_gain, second_edge))
    bias = pl.pallas_call(
        functools.partial(pair_kernel, steps),
        out_shape=shape((heads, pair_rows, keys), BF16),
        in_specs=hbm(3),
        out_specs=hbm(1)[0],
        scratch_shapes=[
            pltpu.VMEM(pair_cond.shape, BF16),
            pltpu.VMEM((1, channels), F32),
            pltpu.VMEM((heads, channels), BF16),
            pltpu.VMEM((heads, pair_rows, keys), BF16),
            pltpu.SemaphoreType.DMA((len(steps),)),
            pltpu.SemaphoreType.DMA((len(steps),)),
            pltpu.SemaphoreType.DMA((2,)),
        ],
        compiler_params=vmem(PRIVATE),
        cost_estimate=cost(5),
    )(pair_cond, gain_row.reshape(1, -1), pair_heads.T)

    encoded, token_state, token_normed, member = pl.pallas_call(
        encoder_kernel,
        out_shape=(
            state_like,
            shape((tok_rows, token_width), F32),
            shape((tok_rows, token_width), BF16),
            shape((tok_rows, atoms), BF16),
        ),
        in_specs=whole(1) + whole(13),
        out_specs=tuple(whole(4)),
        scratch_shapes=window_scratch(atoms + 2 * HALO, atoms, width),
        compiler_params=vmem(16),
        cost_estimate=cost(3.4),
    )(
        window_offsets.reshape(1, -1), level, state, low, normed, high, mask, tokens, atom_qkv, atom_proj, gather_in,
        token_single, noise_embed.reshape(1, -1), token_gain,
    )
    gathered = spread_over(token_normed, "row")
    biases = spread_over(bias, "smp", gathered[1 : row_count // 2 + 1])

    key_mask = token_mask.reshape(-1, keys)
    near_count = row_count - row_count // 4
    far_count = row_count - near_count
    pieces = tok_rows // keys

    def need(count):
        tile = tok_rows * max(keys, LANES)
        return (count * (keys * token_width * 4 + heads * tile * 6) + smp_count * heads * tile * 2) // 2**20 + 1

    queries, carried, largest, total, far_bias = pl.pallas_call(
        functools.partial(attend_first_kernel, near_count, row_count, smp_count),
        out_shape=(
            shape((tok_rows, token_width), BF16),
            shape((tok_rows, token_width), F32),
            shape((heads, tok_rows, LANES), F32),
            shape((heads, tok_rows, LANES), F32),
            shape((far_count * pieces, heads, tok_rows, keys), BF16),
        ),
        in_specs=whole(near_count + smp_count + 2),
        out_specs=tuple(whole(5)),
        scratch_shapes=[
            pltpu.VMEM((near_count * tok_rows, 2 * token_width), BF16),
            pltpu.VMEM((near_count * pieces, heads, tok_rows, keys), F32),
            pltpu.VMEM((near_count * pieces, heads, tok_rows, keys), BF16),
            pltpu.VMEM((smp_count, heads, tok_rows, keys), BF16),
        ],
        compiler_params=vmem(14 + need(near_count * pieces) * 3 // 2),
        cost_estimate=cost(4),
    )(*gathered[:near_count], *biases, key_mask, token_qkv)
    token_result, joined, atom_normed, second_edge, first_edge = pl.pallas_call(
        functools.partial(token_kernel, near_count, row_count),
        out_shape=(
            shape((1, tok_rows, token_width), BF16),
            state_like,
            normed_like,
            edge_like,
            edge_like,
        ),
        in_specs=whole(far_count + 16),
        out_specs=tuple(whole(5)),
        scratch_shapes=[
            pltpu.VMEM((far_count * tok_rows, 2 * token_width), BF16),
            pltpu.VMEM((far_count * pieces, heads, tok_rows, keys), F32),
            pltpu.VMEM((far_count * pieces, heads, tok_rows, keys), BF16),
            pltpu.VMEM((heads, tok_rows, LANES), F32),
        ],
        compiler_params=vmem(20 + need(far_count * pieces)),
        cost_estimate=cost(6),
    )(
        *gathered[near_count:], queries, carried, largest, total, far_bias, token_state, key_mask, token_qkv, token_proj,
        token_gain, ffn_in, ffn_out, scatter_out, encoded, member, atom_gain,
    )
    low, high = halos_of(first_edge, second_edge)

    edge = LANES
    direction_like = shape(coords.shape, F32)
    out_row = out_gain.reshape(1, -1)
    inner = pl.pallas_call(
        inner_kernel,
        out_shape=direction_like,
        in_specs=whole(1) + whole(10),
        out_specs=whole(1)[0],
        scratch_shapes=window_scratch(atoms - edge + HALO, atoms - 2 * edge, width),
        compiler_params=vmem(16),
        cost_estimate=cost(2.7),
    )(
        window_offsets.reshape(1, -1), level, coords, kicks, joined, atom_normed, mask, atom_qkv, atom_proj, out_row, coord_out
    )
    direction = pl.pallas_call(
        edge_kernel,
        out_shape=direction_like,
        in_specs=whole(1) + whole(13),
        out_specs=whole(1)[0],
        scratch_shapes=window_scratch(2 * (edge + 2 * HALO), 2 * edge, width),
        compiler_params=vmem(12),
        cost_estimate=cost(2),
    )(
        window_offsets.reshape(1, -1), level, coords, kicks, joined, low, atom_normed, high, mask, atom_qkv, atom_proj, out_row,
        coord_out, inner,
    )
    return (token_result, direction.transpose(1, 0, 2))


def solution(mesh):
    in_specs = (
        P(("grp", "smp"), None, "row"),
        P(("grp", "smp"), None, "row"),
        P(("grp", "smp")),
        P(("grp", "row"), None),
        P(("grp", "row"), None),
        P(("grp", "row"), "smp", None),
        P(("grp", "row")),
        P(("grp", "row")),
        P("grp"),
        P("grp"),
        P(),
        P(),
        P(),
        P(),
        P(),
        P(),
        P(),
        P(),
        P(),
        P(),
        P(),
        P(),
        P(),
        P(),
        P(),
        P(),
    )
    out_specs = (P(("grp", "smp"), "row", None), P(("grp", "smp"), None, "row"))
    return jax.shard_map(
        per_device, mesh=mesh, in_specs=in_specs, out_specs=out_specs, check_vma=False
    )
```
